32 devices in a mesh: dom: 32 (over z, y, x, core).
Axes of the slice: x: 2, y: 2, z: 4, core: 2. Of those that a mesh axis runs over, the one named last changes fastest.
Arguments:
- dof_values: float32 [9, 20, 8192], P(None, None, 'dom'), may hold values from -6 to 6
- star_mats: bfloat16 [3, 9, 9, 8192], P(None, None, None, 'dom'), may hold values from -0.1796875 to 0.1796875
- flux_local: bfloat16 [4, 9, 9, 8192], P(None, None, None, 'dom'), may hold values from -0.19921875 to 0.19921875
- flux_neigh: bfloat16 [4, 9, 9, 8192], P(None, None, None, 'dom'), may hold values from -0.19921875 to 0.19921875
- kstiff: float32 [3, 20, 20], replicated, may hold values from -1.25 to 1.25
- flux_minus: float32 [4, 20, 20], replicated, may hold values from -1.25 to 1.25
- flux_plus: float32 [4, 4, 20, 20], replicated, may hold values from -1.25 to 1.25
- neighbour: int32 [4, 8192], P(None, 'dom'), may hold values from 0 to 511, as said below
- neigh_face: int32 [4, 8192], P(None, 'dom'), may hold values from 0 to 3
- cluster: int32 [8192], P('dom'), may hold values from 0 to 1
- send_list: int32 [32, 4, 64], P('dom'), may hold values from 0 to 255
- damage_list: int32 [32, 256], P('dom'), may hold values from 0 to 255, as said below
- damage_count: int32 [32], P('dom'), may hold values from 0 to 256, as said below
- yield_mask: int32 [20, 8192], P(None, 'dom'), may hold values 0 or 1
- cohesion: float32 [8192], P('dom'), may hold values from 0.3 to 3
- to_points: float32 [20, 20], replicated, may hold values from -1.25 to 1.25
- from_points: float32 [20, 20], replicated, may hold values from -1.25 to 1.25
Outputs:
- new_dofs: float32 [9, 20, 8192], P(None, None, 'dom')
The draws below stay inside these ranges and needn't reach their ends.
Inputs may be any that keep to these rules, and one draw needn't show every extreme that they name: `neighbour`: entries below 256 are elements of the same partition; the entry 256 + j * 64 + i names ghost slot i of offset slot j. `damage_list`: the entries of one partition's row are distinct. `damage_count`: some partition has exactly 256.
All inputs are finite; a program needn't handle non-finite values. No bound on the sum of `yield_mask` on one device may be relied on, other than what follows from the above.
Results may differ from the reference program's by a relative error of at most 0.0003.
Values sent between devices are 32-bit elements; how exact they have to be, the bound alone decides.
No kernel may reach another device: no remote copies, remote signals or barrier semaphores. Data moves between devices by JAX's collectives and lax.ppermute only.
A program may use at most 128 MiB of HBM per device.

```python
import math
import jax
import jax.numpy as jnp
from jax import lax

NQTY = 9
NBASIS = 20
NQP = 20
NDER = 3
NOFF = 4
E_DEV = 256
NB = 64
NDMG = 256
ELEMS = 8192
N_DOM = 32


def draw_neighbour(key, part):
    choose_key, local_key, ghost_key = jax.random.split(key, 3)
    choose_kind = jax.random.randint(choose_key, (4, ELEMS), 0, 5)
    local_ids = jax.random.randint(local_key, (4, ELEMS), 0, E_DEV)
    ghost_ids = jax.random.randint(ghost_key, (4, ELEMS), E_DEV, E_DEV + NOFF * NB)
    return jnp.where(choose_kind == 0, ghost_ids, local_ids).astype(jnp.int32)


def draw_damage_list(key, part):
    row_keys = jax.random.split(key, N_DOM)

    def one_row(row_key):
        return jax.random.permutation(row_key, E_DEV)[:NDMG]
    return jax.vmap(one_row)(row_keys).astype(jnp.int32)


def draw_damage_count(key, part):
    count_key, top_key = jax.random.split(key)
    counts = jax.random.randint(count_key, (N_DOM,), NDMG // 16, NDMG + 1)
    busiest = jax.random.randint(top_key, (), 0, N_DOM)
    return counts.at[busiest].set(NDMG).astype(jnp.int32)


def plant(drawn, key, smallest, top_value):
    place = [jax.random.randint(jax.random.fold_in(key, axis), (), 0, length) for axis, length in enumerate(drawn.shape)]
    widest = drawn.shape.index(max(drawn.shape))
    beside = place[:widest] + [(place[widest] + 1) % drawn.shape[widest]] + place[widest + 1:]
    return drawn.at[tuple(place)].set(smallest).at[tuple(beside)].set(top_value)


def block_scale(rng, extent, cuts, low, largest):
    loudness, own = 1.0, jax.random.fold_in(rng, 6)
    for position, parts in cuts:
        draws = jnp.exp(jax.random.uniform(jax.random.fold_in(own, position), (parts,), jnp.float32, low / len(cuts), largest / len(cuts)))
        loudness = loudness * jnp.repeat(draws, extent[position] // parts).reshape([-1 if axis == position else 1 for axis in range(len(extent))])
    return loudness


def noise(key, extent, spread, bound, cuts=(), held_as=jnp.bfloat16):
    drawn = jax.random.normal(key, extent, jnp.float32) * spread
    if len(cuts) > 0:
        drawn = block_scale(key, extent, cuts, -0.22, 0.18) * drawn
    return jnp.clip(drawn, min=-bound, max=bound).astype(held_as)


def setup_inputs(seed: int = 0) -> dict:
    key_list = jax.random.split(jax.random.key(seed), 18)
    dof_values = noise(key_list[0], (NQTY, NBASIS, ELEMS), 1.0, 6.0, ((2, 32),), jnp.float32)
    star_mats = noise(key_list[1], (3, NQTY, NQTY, ELEMS), 0.03, 0.1796875, ((3, 32),))
    flux_local = noise(key_list[2], (4, NQTY, NQTY, ELEMS), 0.035, 0.19921875, ((3, 32),))
    flux_neigh = noise(key_list[3], (4, NQTY, NQTY, ELEMS), 0.035, 0.19921875, ((3, 32),))
    kstiff = noise(key_list[4], (3, NBASIS, NBASIS), NBASIS ** -0.5, 1.25, (), jnp.float32)
    flux_minus = noise(key_list[5], (4, NBASIS, NBASIS), NBASIS ** -0.5, 1.25, (), jnp.float32)
    flux_plus = noise(key_list[6], (4, 4, NBASIS, NBASIS), NBASIS ** -0.5, 1.25, (), jnp.float32)
    neighbour = draw_neighbour(jax.random.fold_in(key_list[17], 71), 0)
    neigh_face = plant(jax.random.randint(key_list[8], (4, ELEMS), 0, 4), jax.random.fold_in(key_list[8], 1), 0, 3).astype(jnp.int32)
    cluster = plant(jax.random.randint(key_list[9], (ELEMS,), 0, 2), jax.random.fold_in(key_list[9], 1), 0, 1).astype(jnp.int32)
    send_list = plant(jax.random.randint(key_list[10], (N_DOM, NOFF, NB), 0, E_DEV), jax.random.fold_in(key_list[10], 1), 0, E_DEV - 1).astype(jnp.int32)
    damage_list = draw_damage_list(jax.random.fold_in(key_list[17], 71), 0)
    damage_count = draw_damage_count(jax.random.fold_in(key_list[17], 71), 0)
    yield_mask = plant((jax.random.randint(key_list[13], (NQP, ELEMS), 0, 2) < 1).astype(jnp.int32), jax.random.fold_in(key_list[13], 1), 0, 1)
    cohesion = jnp.clip(jnp.exp(math.log(3.0) - 2.3025851 * jax.random.uniform(key_list[14], (ELEMS,), jnp.float32) ** block_scale(key_list[14], (ELEMS,), ((0, 32),), -0.2, 0.2)), 0.3, 3.0)
    to_points = noise(key_list[15], (NQP, NBASIS), NBASIS ** -0.5, 1.25, (), jnp.float32)
    from_points = noise(key_list[16], (NBASIS, NQP), NQP ** -0.5, 1.25, (), jnp.float32)
    return {"dof_values": dof_values, "star_mats": star_mats, "flux_local": flux_local, "flux_neigh": flux_neigh, "kstiff": kstiff, "flux_minus": flux_minus, "flux_plus": flux_plus, "neighbour": neighbour, "neigh_face": neigh_face, "cluster": cluster, "send_list": send_list, "damage_list": damage_list, "damage_count": damage_count, "yield_mask": yield_mask, "cohesion": cohesion, "to_points": to_points, "from_points": from_points}


PRECISE = lax.Precision.HIGHEST
OFFSETS = (1, -1, 2, -2)
FRICTION = 0.6
RELAXATION = 0.5

def star_apply(source, matrix):
    wide = matrix.astype(jnp.float32)
    total = source[0][None, :, :] * wide[0][:, None, :]
    for quantity in range(1, source.shape[0]):
        total = total + source[quantity][None, :, :] * wide[quantity][:, None, :]
    return total

def derivatives(source, star_part, kstiff):
    series = [source]
    for degree in range(NDER - 1):
        latest = series[-1]
        following = jnp.zeros_like(latest)
        for direction in range(3):
            rotated = star_apply(latest, star_part[direction])
            following = following + jnp.einsum('bc,pce->pbe', kstiff[direction], rotated, precision=PRECISE)
        series.append(following)
    return series

def taylor(series, time_begin, time_end):
    summed = jnp.zeros_like(series[0])
    divisor = 1.0
    for degree in range(len(series)):
        divisor = divisor * (degree + 1)
        weight_now = (time_end ** (degree + 1) - time_begin ** (degree + 1)) / divisor
        summed = summed + weight_now * series[degree]
    return summed

def volume(integral, star_part, kstiff):
    summed = jnp.zeros_like(integral)
    for direction in range(3):
        rotated = star_apply(integral, star_part[direction])
        summed = summed + jnp.einsum('cb,pce->pbe', kstiff[direction], rotated, precision=PRECISE)
    return summed

def face_values(extended, neighbours):
    return jnp.stack([jnp.take(extended, neighbours[face_id], axis=2) for face_id in range(4)])

def surface(integral, others, neigh_faces, local_flux, neigh_flux, flux_minus, flux_plus):
    summed = jnp.zeros_like(integral)
    for face_id in range(4):
        own_side = star_apply(integral, local_flux[face_id])
        summed = summed + jnp.einsum('bc,pce->pbe', flux_minus[face_id], own_side, precision=PRECISE)
        far_side = star_apply(others[face_id], neigh_flux[face_id])
        selector = (neigh_faces[face_id][None, :] == jnp.arange(4, dtype=jnp.int32)[:, None]).astype(jnp.float32)
        masked = far_side[None] * selector[:, None, None, :]
        summed = summed + jnp.einsum('hbc,hpce->pbe', flux_plus[face_id], masked, precision=PRECISE)
    return summed

def plastic(stress, strength, plastic_mask, to_points, from_points):
    points = jnp.einsum('nb,qbp->qnp', to_points, stress, precision=PRECISE)
    pressure = (points[0] + points[1] + points[2]) / 3.0
    normal = points[:3] - pressure[None]
    shear_part = points[3:]
    tau_eff = jnp.sqrt(0.5 * lax.optimization_barrier(jnp.sum(normal * normal, axis=0)) + lax.optimization_barrier(jnp.sum(shear_part * shear_part, axis=0)))
    yield_limit = jnp.maximum(strength[None, :] - FRICTION * pressure, 0.5 * strength[None, :])
    rate_now = jnp.where(plastic_mask > 0.5, RELAXATION * (yield_limit / jnp.maximum(tau_eff, yield_limit) - 1.0), 0.0)
    change = jnp.concatenate([normal, shear_part], axis=0) * rate_now[None]
    return jnp.einsum('bn,qnp->qbp', from_points, change, precision=PRECISE)

def to_parts(array):
    shaped = array.reshape(array.shape[:-1] + (N_DOM, E_DEV))
    return jnp.moveaxis(shaped, -2, 0)

def from_parts(array):
    moved = jnp.moveaxis(array, 0, -2)
    return moved.reshape(moved.shape[:-2] + (N_DOM * E_DEV,))

def ghosts(buffers, send_list):

    def pick_rows(buffer, listing):
        return jnp.take(buffer, listing.reshape(-1), axis=2)
    blocks = jax.vmap(pick_rows)(buffers, send_list)
    blocks = blocks.reshape(blocks.shape[:3] + (len(OFFSETS), NB))
    pieces = []
    for slot_id in range(len(OFFSETS)):
        offset = OFFSETS[slot_id]
        one_block = blocks[:, :, :, slot_id, :]
        padding = jnp.zeros((abs(offset),) + one_block.shape[1:], jnp.float32)
        if offset > 0:
            shifted = jnp.concatenate([padding, one_block[:-offset]], axis=0)
        else:
            shifted = jnp.concatenate([one_block[-offset:], padding], axis=0)
        pieces.append(shifted)
    return jnp.concatenate(pieces, axis=3)

def reference(dof_values, star_mats, flux_local, flux_neigh, kstiff, flux_minus, flux_plus, neighbour, neigh_face, cluster, send_list, damage_list, damage_count, yield_mask, cohesion, to_points, from_points):
    parts_dofs = to_parts(dof_values)
    parts_star = to_parts(star_mats)
    parts_local = to_parts(flux_local)
    parts_neigh = to_parts(flux_neigh)
    parts_ids = to_parts(neighbour)
    parts_face = to_parts(neigh_face)
    parts_cluster = to_parts(cluster)
    parts_mask = to_parts(yield_mask)
    parts_strength = to_parts(cohesion)

    def section_one(inputs):
        source, star_part = inputs
        return taylor(derivatives(source, star_part, kstiff), 0.0, 1.0)
    buffer_one = lax.map(section_one, (parts_dofs, parts_star))
    ghost_one = ghosts(buffer_one, send_list)

    def section_two(inputs):
        source, star_part, local_flux, neigh_flux, neighbours, neigh_faces, clusters, own_buffer, own_ghost = inputs
        is_fine = (clusters == 0)[None, None, :]
        others = face_values(jnp.concatenate([own_buffer, own_ghost], axis=2), neighbours)
        updated = source + volume(own_buffer, star_part, kstiff) - surface(own_buffer, others, neigh_faces, local_flux, neigh_flux, flux_minus, flux_plus)
        state_one = jnp.where(is_fine, updated, source)
        series = derivatives(state_one, star_part, kstiff)
        buffer_two = jnp.where(is_fine, taylor(series, 0.0, 1.0), taylor(series, 1.0, 2.0))
        return (state_one, buffer_two)
    state_one, buffer_two = lax.map(section_two, (parts_dofs, parts_star, parts_local, parts_neigh, parts_ids, parts_face, parts_cluster, buffer_one, ghost_one))
    ghost_two = ghosts(buffer_two, send_list)

    def section_three(inputs):
        state_now, star_part, local_flux, neigh_flux, neighbours, neigh_faces, clusters, own_one, own_two, ghost_first, ghost_second, listing, live_count, masks, strength = inputs
        is_fine = (clusters == 0)[None, None, :]
        summed_buffer = own_one + own_two
        fine_side = face_values(jnp.concatenate([own_two, ghost_second], axis=2), neighbours)
        coarse_side = face_values(jnp.concatenate([summed_buffer, ghost_first + ghost_second], axis=2), neighbours)
        others = jnp.where(is_fine[None], fine_side, coarse_side)
        integral = jnp.where(is_fine, own_two, summed_buffer)
        state_two = state_now + volume(integral, star_part, kstiff) - surface(integral, others, neigh_faces, local_flux, neigh_flux, flux_minus, flux_plus)
        stress = jnp.take(state_two[:6], listing, axis=2)
        correction = plastic(stress, jnp.take(strength, listing), jnp.take(masks, listing, axis=1).astype(jnp.float32), to_points, from_points)
        live_slots = (jnp.arange(NDMG, dtype=jnp.int32) < live_count).astype(jnp.float32)
        return state_two.at[:6, :, listing].add(correction * live_slots[None, None, :])
    result = lax.map(section_three, (state_one, parts_star, parts_local, parts_neigh, parts_ids, parts_face, parts_cluster, buffer_one, buffer_two, ghost_one, ghost_two, damage_list, damage_count, parts_mask, parts_strength))
    return from_parts(result)
```

```python
import jax
import jax.numpy as jnp
from jax import lax
from jax.experimental import pallas as pl
from jax.experimental.pallas import tpu as pltpu
from jax.sharding import PartitionSpec as P

NQ = 9
NB = 20
R = 24
K3 = 3 * R
LANES = 128
FRICTION = 0.6
RELAXATION = 0.5
F32 = jnp.float32
BF16 = jnp.bfloat16


def stack_weights(w):
    w = jnp.pad(w, [(0, 0)] * (w.ndim - 2) + [(0, R - NB), (0, R - NB)])
    high = lax.reduce_precision(w, 8, 7)
    low = w - high
    return jnp.concatenate([high, high, low], axis=-1).astype(BF16)


def stack_values(x):
    high = x.astype(BF16).astype(F32)
    return jnp.concatenate([high, x - high, high], axis=0).astype(BF16)


def dot(a, b):
    return jnp.dot(a, b, preferred_element_type=F32)


def widen(src_ref, dst_ref, base):
    blocks = src_ref.shape[0]

    def one(k, _):
        for q in range(NQ):
            dst_ref[(base + k) * NQ + q] = src_ref[k, q].astype(F32)
        return 0

    lax.fori_loop(0, blocks, one, 0)


def basis_products(weights, x_ref, y_ref, blocks, base=0):
    for q in range(NQ):
        out = dot(weights, stack_values(x_ref[q]))
        for k in range(blocks):
            y_ref[base + k, q] = out[k * R : (k + 1) * R]


def star_sum(y_ref, m_ref, blocks, lanes, start):
    def one(k, acc):
        acc = list(acc)
        for q in range(NQ):
            y = y_ref[k, q, :, lanes]
            for p in range(NQ):
                acc[p] = acc[p] + y * m_ref[k * NQ + q, p : p + 1, lanes]
        return tuple(acc)

    return lax.fori_loop(0, blocks, one, tuple(start))


def each_half(elements, body):
    def one(half, _):
        body(pl.ds(pl.multiple_of(half * LANES, LANES), LANES))
        return 0

    lax.fori_loop(0, elements // LANES, one, 0)


def taylor_buffer(x_ref, first_ref, y_ref, m_ref, wk, weights_at, out_ref):
    elements = x_ref.shape[-1]
    basis_products(wk, x_ref, y_ref, 3)

    def first(lanes):
        acc = star_sum(y_ref, m_ref, 3, lanes, [jnp.zeros((R, LANES), F32)] * NQ)
        for p in range(NQ):
            first_ref[p, :, lanes] = acc[p]

    each_half(elements, first)
    basis_products(wk, first_ref, y_ref, 3)

    def second(lanes):
        acc = star_sum(y_ref, m_ref, 3, lanes, [jnp.zeros((R, LANES), F32)] * NQ)
        w1, w2 = weights_at(lanes)
        for p in range(NQ):
            out_ref[p, :, lanes] = x_ref[p, :, lanes] + (w1 * first_ref[p, :, lanes] + w2 * acc[p])

    each_half(elements, second)


def send_blocks(b_ref, send_ref, near_ref, far_ref):
    elements = b_ref.shape[-1]
    columns = send_ref.shape[-1]
    b = b_ref[...].reshape(NQ * R, elements)
    high = b.astype(BF16)
    low = (b - high.astype(F32)).astype(BF16)
    rows = lax.broadcasted_iota(jnp.int32, (elements, columns), 0)
    hot = jnp.where(rows == send_ref[...], 1.0, 0.0).astype(BF16)
    out = dot(high, hot) + dot(low, hot)
    near_ref[...] = out[:, : columns // 2]
    far_ref[...] = out[:, columns // 2 :]


def far_sides(source, index_ref, face_ref, wf_ref, g_ref, y_ref, base):
    depth = source.shape[-1]
    high = source.astype(BF16)
    low = (source - high.astype(F32)).astype(BF16)
    both = jnp.concatenate([high, low], axis=0)
    rows = lax.broadcasted_iota(jnp.int32, (depth, index_ref.shape[-1]), 0)
    size = NQ * R

    def one(f, _):
        hot = jnp.where(rows == index_ref[pl.ds(f, 1), :], 1.0, 0.0).astype(BF16)
        g_ref[...] = dot(both, hot)
        kind = jnp.broadcast_to(face_ref[pl.ds(f, 1), :], (R, index_ref.shape[-1]))
        w = wf_ref[f]
        for q in range(NQ):
            high_rows = g_ref[q * R : (q + 1) * R]
            low_rows = g_ref[size + q * R : size + (q + 1) * R]
            out = dot(w, jnp.concatenate([high_rows, low_rows, high_rows], axis=0).astype(BF16))
            y_ref[base + f, q] = jnp.where(
                kind < 2,
                jnp.where(kind == 0, out[:R], out[R : 2 * R]),
                jnp.where(kind == 2, out[2 * R : 3 * R], out[3 * R :]),
            )
        return 0

    lax.fori_loop(0, 4, one, 0)


def predict_kernel(dof_ref, star_ref, wk_ref, send_ref, b_ref, near_ref, far_ref, x_ref, first_ref, y_ref, m_ref):
    widen(star_ref, m_ref, 0)
    x_ref[:, NB:, :] = jnp.zeros((NQ, R - NB, x_ref.shape[-1]), F32)
    x_ref[:, :NB, :] = dof_ref[...]
    taylor_buffer(x_ref, first_ref, y_ref, m_ref, wk_ref[...], lambda lanes: (0.5, 1.0 / 6.0), b_ref)
    send_blocks(b_ref, send_ref, near_ref, far_ref)


def local_kernel(
    base_ref, b_ref, star_ref, local_ref, neigh_ref, wv_ref, wf_ref, index_ref, face_ref, out_ref, y_ref, m_ref, g_ref
):
    elements = b_ref.shape[-1]
    rows = base_ref.shape[1]
    widen(star_ref, m_ref, 0)
    widen(local_ref, m_ref, 3)
    widen(neigh_ref, m_ref, 7)
    basis_products(wv_ref[...], b_ref, y_ref, 7)
    far_sides(b_ref[...].reshape(NQ * R, elements), index_ref, face_ref, wf_ref, g_ref, y_ref, 7)

    def body(lanes):
        acc = star_sum(y_ref, m_ref, 11, lanes, [jnp.zeros((R, LANES), F32)] * NQ)
        for p in range(NQ):
            out_ref[p, :, lanes] = acc[p]

    each_half(elements, body)
    out_ref[:, :rows, :] = out_ref[:, :rows, :] + base_ref[...]


def ghost_index(pos_ref, index_ref, ghost_ref, elements, ghosts):
    me, total = pos_ref[0], pos_ref[1]
    core = me % 2
    chip = (me // 2) % 2
    width = 2 * ghosts
    up = jnp.where(chip == 0, width, 2 * width)
    down = jnp.where(chip == 0, 2 * width, width)
    nowhere = -8 * width
    starts = (
        jnp.where(me >= 1, jnp.where(core == 1, 0, down), nowhere),
        jnp.where(me <= total - 2, jnp.where(core == 0, ghosts, up + ghosts), nowhere),
        jnp.where(me >= 2, down + ghosts, nowhere),
        jnp.where(me <= total - 3, up, nowhere),
    )
    index = index_ref[...] - elements
    out = jnp.full(index.shape, -1, jnp.int32)
    for j in range(4):
        inside = (index >= j * ghosts) & (index < (j + 1) * ghosts)
        out = jnp.where(inside, index - j * ghosts + starts[j], out)
    ghost_ref[...] = out


def ghost_part(
    pos_ref, v_ref, near_ref, even_ref, odd_ref, neigh_ref, wf_ref, index_ref, face_ref, ghost_ref, y_ref, m_ref, g_ref, base
):
    elements = v_ref.shape[-1]
    ghost_index(pos_ref, index_ref, ghost_ref, elements, near_ref.shape[-1] // 2)
    widen(neigh_ref, m_ref, base)
    source = jnp.concatenate([near_ref[...], even_ref[...], odd_ref[...]], axis=1)
    far_sides(source, ghost_ref, face_ref, wf_ref, g_ref, y_ref, 0)


def second_kernel(
    pos_ref, v_ref, dof_ref, near_ref, even_ref, odd_ref, star_ref, neigh_ref, wk_ref, wf_ref, index_ref, face_ref,
    cluster_ref, send_ref,
    state_ref, b_ref, near_out, far_out,
    x_ref, first_ref, y_ref, m_ref, mf_ref, g_ref, ghost_ref,
):
    elements = v_ref.shape[-1]
    ghost_part(
        pos_ref, v_ref, near_ref, even_ref, odd_ref, neigh_ref, wf_ref, index_ref, face_ref, ghost_ref, y_ref, mf_ref, g_ref, 0
    )
    widen(star_ref, m_ref, 0)

    def body(lanes):
        acc = star_sum(y_ref, mf_ref, 4, lanes, [v_ref[p, :, lanes] for p in range(NQ)])
        fine = cluster_ref[:, lanes] == 0
        pad = jnp.zeros((R - NB, LANES), F32)
        for p in range(NQ):
            state_ref[p, :, lanes] = acc[p]
            old = jnp.concatenate([dof_ref[p, :, lanes], pad], axis=0)
            x_ref[p, :, lanes] = jnp.where(fine, acc[p], old)

    each_half(elements, body)

    def weights_at(lanes):
        fine = cluster_ref[:, lanes] == 0
        return jnp.where(fine, 0.5, 1.5), jnp.where(fine, 1.0 / 6.0, 7.0 / 6.0)

    taylor_buffer(x_ref, first_ref, y_ref, m_ref, wk_ref[...], weights_at, b_ref)
    send_blocks(b_ref, send_ref, near_out, far_out)


def last_kernel(
    pos_ref, count_ref, v_ref, near_ref, even_ref, odd_ref, neigh_ref, wf_ref, index_ref, face_ref,
    damage_ref, yield_ref, cohesion_ref, wp_ref,
    out_ref,
    x_ref, y_ref, mf_ref, g_ref, ghost_ref, mask_ref,
):
    elements = v_ref.shape[-1]
    ghost_part(
        pos_ref, v_ref, near_ref, even_ref, odd_ref, neigh_ref, wf_ref, index_ref, face_ref, ghost_ref, y_ref, mf_ref, g_ref, 0
    )

    def body(lanes):
        acc = star_sum(y_ref, mf_ref, 4, lanes, [v_ref[p, :, lanes] for p in range(NQ)])
        for p in range(NQ):
            x_ref[p, :, lanes] = acc[p]

    each_half(elements, body)

    slots = damage_ref.shape[-1]
    rows = lax.broadcasted_iota(jnp.int32, (elements, slots), 0)
    slot = lax.broadcasted_iota(jnp.int32, (elements, slots), 1)
    hit = (rows == damage_ref[...]) & (slot < count_ref[0])
    listed = lax.dot_general(
        jnp.ones((8, slots), BF16),
        jnp.where(hit, 1.0, 0.0).astype(BF16),
        (((1,), (1,)), ((), ())),
        preferred_element_type=F32,
    )[0:1]
    mask_ref[NB:, :] = jnp.zeros((R - NB, elements), F32)
    mask_ref[:NB, :] = jnp.where((yield_ref[...] == 1) & (listed > 0.5), 1.0, 0.0)

    points = [dot(wp_ref[0], stack_values(x_ref[q])) for q in range(6)]
    pressure = (points[0] + points[1] + points[2]) / 3.0
    normal = [points[q] - pressure for q in range(3)]
    normal_sum = normal[0] * normal[0] + normal[1] * normal[1] + normal[2] * normal[2]
    shear_sum = points[3] * points[3] + points[4] * points[4] + points[5] * points[5]
    tau = jnp.sqrt(0.5 * normal_sum + shear_sum)
    strength = cohesion_ref[...]
    limit = jnp.maximum(strength - FRICTION * pressure, 0.5 * strength)
    rate = jnp.where(mask_ref[...] > 0.5, RELAXATION * (limit / jnp.maximum(tau, limit) - 1.0), 0.0)
    deviation = normal + points[3:]
    for q in range(6):
        change = dot(wp_ref[1], stack_values(rate * deviation[q]))
        out_ref[q] = (x_ref[q] + change)[:NB]
    for q in range(6, NQ):
        out_ref[q] = x_ref[q, :NB, :]


def spec(shape, dtype=F32):
    return jax.ShapeDtypeStruct(shape, dtype)


VMEM = pl.BlockSpec(memory_space=pltpu.VMEM)
SMEM = pl.BlockSpec(memory_space=pltpu.SMEM)


def call(kernel, inputs, outputs, scratch, smem=0, cost=0):
    return pl.pallas_call(
        kernel,
        out_shape=outputs,
        in_specs=[SMEM] * smem + [VMEM] * (len(inputs) - smem),
        out_specs=jax.tree.map(lambda _: VMEM, outputs),
        scratch_shapes=[pltpu.VMEM(shape, dtype) for shape, dtype in scratch],
        compiler_params=pltpu.CompilerParams(vmem_limit_bytes=40 * 1024 * 1024),
        cost_estimate=pl.CostEstimate(flops=cost, bytes_accessed=1 << 20, transcendentals=0),
    )(*inputs)


def core_swap(total):
    return [(i, i ^ 1) for i in range(total)]


def even_chip_swap(total):
    return [(i, i ^ 2) for i in range(total)]


def odd_chip_swap(total):
    route = [(i, i) for i in (0, 1, total - 2, total - 1)]
    for i in range(2, total - 2, 4):
        for k in (i, i + 1):
            route += [(k, k + 2), (k + 2, k)]
    return route


def exchange(near, far, me, total):
    got = lax.ppermute(near, "dom", core_swap(total))
    left = lax.broadcasted_iota(jnp.int32, got.shape, 1) < got.shape[1] // 2
    forward = left == ((me // 2) % 2 == 0)
    even = lax.ppermute(jnp.where(forward, got, far), "dom", even_chip_swap(total))
    odd = lax.ppermute(jnp.where(forward, far, got), "dom", odd_chip_swap(total))
    return got, even, odd


def per_device(
    dof_values,
    star_mats,
    flux_local,
    flux_neigh,
    kstiff,
    flux_minus,
    flux_plus,
    neighbour,
    neigh_face,
    cluster,
    send_list,
    damage_list,
    damage_count,
    yield_mask,
    cohesion,
    to_points,
    from_points,
):
    elements = dof_values.shape[-1]
    total = lax.axis_size("dom")
    me = lax.axis_index("dom")
    position = jnp.stack([me.astype(jnp.int32), jnp.int32(total)])
    wk = stack_weights(kstiff).reshape(3 * R, K3)
    wv = stack_weights(jnp.concatenate([jnp.swapaxes(kstiff, 1, 2), -flux_minus])).reshape(7 * R, K3)
    wf = stack_weights(-flux_plus).reshape(4, 4 * R, K3)
    wp = stack_weights(jnp.stack([to_points, from_points]))
    send = jnp.concatenate([send_list[0, 0], send_list[0, 1], send_list[0, 3], send_list[0, 2]])[None]
    cluster = cluster[None]
    cohesion = cohesion[None]

    field = spec((NQ, R, elements))
    block = spec((NQ * R, send.shape[-1] // 2))
    x_s = ((NQ, R, elements), F32)
    g_s = ((2 * NQ * R, elements), F32)
    ghost_s = ((4, elements), jnp.int32)

    def y_s(blocks):
        return ((blocks, NQ, R, elements), F32)

    def m_s(blocks):
        return ((blocks * NQ, NQ, elements), F32)

    def local_part(base, buffer):
        return call(
            local_kernel,
            [base, buffer, star_mats, flux_local, flux_neigh, wv, wf, neighbour, neigh_face],
            field,
            [y_s(11), m_s(11), g_s],
            cost=1_000_000_000,
        )

    buffer_one, near, far = call(
        predict_kernel,
        [dof_values, star_mats, wk, send],
        (field, block, block),
        [x_s, x_s, y_s(3), m_s(3)],
    )
    near, even, odd = exchange(near, far, me, total)
    started = local_part(dof_values, buffer_one)
    updated, buffer_two, near, far = call(
        second_kernel,
        [
            position, started, dof_values, near, even, odd, star_mats, flux_neigh, wk, wf, neighbour, neigh_face,
            cluster, send,
        ],
        (field, field, block, block),
        [x_s, x_s, y_s(4), m_s(3), m_s(4), g_s, ghost_s],
        smem=1,
    )
    near, even, odd = exchange(near, far, me, total)
    started = local_part(updated, buffer_two)
    return call(
        last_kernel,
        [
            position, damage_count, started, near, even, odd, flux_neigh, wf, neighbour, neigh_face,
            damage_list, yield_mask, cohesion, wp,
        ],
        spec(dof_values.shape),
        [x_s, y_s(4), m_s(4), g_s, ghost_s, ((R, elements), F32)],
        smem=2,
    )


def solution(mesh):
    return jax.shard_map(
        per_device,
        mesh=mesh,
        in_specs=(
            P(None, None, "dom"),
            P(None, None, None, "dom"),
            P(None, None, None, "dom"),
            P(None, None, None, "dom"),
            P(),
            P(),
            P(),
            P(None, "dom"),
            P(None, "dom"),
            P("dom"),
            P("dom", None, None),
            P("dom", None),
            P("dom"),
            P(None, "dom"),
            P("dom"),
            P(),
            P(),
        ),
        out_specs=P(None, None, "dom"),
        check_vma=False,
    )
```

```python
import functools

import jax
import jax.numpy as jnp
from jax import lax
from jax.experimental import pallas as pl
from jax.experimental.pallas import tpu as pltpu
from jax.sharding import PartitionSpec as P

NQ = 9
NB = 20
R = 24
K3 = 3 * R
LANES = 128
FRICTION = 0.6
RELAXATION = 0.5
F32 = jnp.float32
BF16 = jnp.bfloat16


def stack_weights(w):
    w = jnp.pad(w, [(0, 0)] * (w.ndim - 2) + [(0, R - NB), (0, R - NB)])
    high = lax.reduce_precision(w, 8, 7)
    low = w - high
    return jnp.concatenate([high, high, low], axis=-1).astype(BF16)


def stack_values(x):
    high = x.astype(BF16).astype(F32)
    return jnp.concatenate([high, x - high, high], axis=0).astype(BF16)


def dot(a, b):
    return jnp.dot(a, b, preferred_element_type=F32)


def widen(src_ref, dst_ref):
    for q in range(NQ):
        for p in range(NQ):
            dst_ref[q * NQ + p] = src_ref[q, p].astype(F32)


def basis_products(weights, x_ref, y_ref, blocks, base=0):
    for q in range(NQ):
        out = dot(weights, stack_values(x_ref[q]))
        for k in range(blocks):
            y_ref[base + k, q] = out[k * R : (k + 1) * R]


def star_sum(y_ref, m_refs, lanes, start):
    acc = list(start)
    for q in range(NQ):
        k = 0
        for m_ref in m_refs:
            for row in range(m_ref.shape[1]):
                y = y_ref[k, q, :, lanes]
                for p in range(NQ):
                    acc[p] = acc[p] + y * m_ref[q * NQ + p, row : row + 1, lanes]
                k += 1
    return acc


def each_half(elements, body):
    for start in range(0, elements, LANES):
        body(pl.ds(start, LANES))


def taylor_buffer(x_ref, first_ref, y_ref, m_ref, wk, weights_at, out_ref):
    elements = x_ref.shape[-1]
    basis_products(wk, x_ref, y_ref, 3)

    def first(lanes):
        acc = star_sum(y_ref, [m_ref], lanes, [jnp.zeros((R, LANES), F32)] * NQ)
        for p in range(NQ):
            first_ref[p, :, lanes] = acc[p]

    each_half(elements, first)
    basis_products(wk, first_ref, y_ref, 3)

    def second(lanes):
        acc = star_sum(y_ref, [m_ref], lanes, [jnp.zeros((R, LANES), F32)] * NQ)
        w1, w2 = weights_at(lanes)
        for p in range(NQ):
            out_ref[p, :, lanes] = x_ref[p, :, lanes] + (w1 * first_ref[p, :, lanes] + w2 * acc[p])

    each_half(elements, second)


def send_blocks(b_ref, send, near_ref, far_ref):
    elements = b_ref.shape[-1]
    columns = send.shape[-1]
    b = b_ref[...].reshape(NQ * R, elements)
    high = b.astype(BF16)
    low = (b - high.astype(F32)).astype(BF16)
    rows = lax.broadcasted_iota(jnp.int32, (elements, columns), 0).astype(F32)
    hot = jnp.where(rows == send, 1.0, 0.0).astype(BF16)
    out = dot(high, hot) + dot(low, hot)
    near_ref[...] = out[:, : columns // 2]
    far_ref[...] = out[:, columns // 2 :]


def far_sides(source, index, face, wf_ref, y_ref, base):
    high = source.astype(BF16)
    low = (source - high.astype(F32)).astype(BF16)
    both = jnp.concatenate([high, low], axis=0)
    elements = index.shape[-1]
    rows = lax.broadcasted_iota(jnp.int32, (source.shape[-1], elements), 0).astype(F32)
    size = NQ * R
    gathered = []
    for f in range(4):
        hot = jnp.where(rows == index[f : f + 1], 1.0, 0.0).astype(BF16)
        gathered.append(dot(both, hot))
    for f, picked in enumerate(gathered):
        kind = jnp.broadcast_to(face[f : f + 1], (R, elements))
        w = wf_ref[f]
        for q in range(NQ):
            high_rows = picked[q * R : (q + 1) * R]
            low_rows = picked[size + q * R : size + (q + 1) * R]
            out = dot(w, jnp.concatenate([high_rows, low_rows, high_rows], axis=0).astype(BF16))
            y_ref[base + f, q] = jnp.where(
                kind < 2,
                jnp.where(kind == 0, out[:R], out[R : 2 * R]),
                jnp.where(kind == 2, out[2 * R : 3 * R], out[3 * R :]),
            )


def place_weights(w_ref):
    w = w_ref[...]
    high = w.astype(BF16)
    low = (w - high.astype(F32)).astype(BF16)
    row = lax.broadcasted_iota(jnp.int32, (LANES, K3), 0)
    column = lax.broadcasted_iota(jnp.int32, (LANES, K3), 1)
    twice = jnp.where((column == row) | (column == row + R), 1.0, 0.0).astype(BF16)
    once = jnp.where(column == row + 2 * R, 1.0, 0.0).astype(BF16)
    return (dot(high, twice) + dot(low, once)).astype(BF16)


def send_columns(send_ref):
    slots, ghosts = send_ref.shape
    width = slots * ghosts
    row = lax.broadcasted_iota(jnp.int32, (ghosts, width), 0)
    column = lax.broadcasted_iota(jnp.int32, (ghosts, width), 1)
    repeat = jnp.where(column % ghosts == row, 1.0, 0.0).astype(BF16)
    wide = dot(send_ref[...].astype(F32).astype(BF16), repeat)
    slot = lax.broadcasted_iota(jnp.int32, (1, width), 1) // ghosts
    first = jnp.where(slot == 0, wide[0:1], wide[1:2])
    second = jnp.where(slot == 2, wide[3:4], wide[2:3])
    return jnp.where(slot < 2, first, second)


NEIGHBOUR, FACE, CLUSTER, DAMAGE, COUNT, COHESION, SEND, YIELD = 0, 4, 8, 9, 10, 11, 12, 16
ROWS = 40


def predict_kernel(
    dof_ref, star_ref, kstiff_ref, send_ref, index_ref, face_ref, cluster_ref, damage_ref, count_ref, cohesion_ref, yield_ref,
    b_out, near_out, far_out, table_out, wk_out,
    dof_v, star_v, kstiff_v, send_v, index_v, face_v, cluster_v, damage_v, count_v, cohesion_v, yield_v,
    w_ref, x_ref, first_ref, y_ref, m_ref, b_ref, near_ref, far_ref, table_ref, wk_ref, in_sems, out_sems,
):
    sources = [
        kstiff_ref, send_ref.at[0], dof_ref, star_ref, index_ref, face_ref, cluster_ref, damage_ref, count_ref, cohesion_ref, yield_ref
    ]
    targets = [kstiff_v, send_v, dof_v, star_v, index_v, face_v, cluster_v, damage_v, count_v, cohesion_v, yield_v]
    moves = [pltpu.make_async_copy(*pair, in_sems.at[i]) for i, pair in enumerate(zip(sources, targets))]
    for move in moves:
        move.start()
    results = [(b_ref, b_out), (near_ref, near_out), (far_ref, far_out), (table_ref, table_out), (wk_ref, wk_out)]
    writes = [pltpu.make_async_copy(*pair, out_sems.at[i]) for i, pair in enumerate(results)]
    elements = x_ref.shape[-1]
    w_ref[...] = jnp.zeros(w_ref.shape, F32)
    x_ref[:, NB:, :] = jnp.zeros((NQ, R - NB, elements), F32)
    table_ref[...] = jnp.zeros(table_ref.shape, F32)
    for move in moves:
        move.wait()
    for d in range(3):
        w_ref[d * R : d * R + NB, :NB] = kstiff_v[d]
    wk = place_weights(w_ref)
    wk_ref[...] = wk
    x_ref[:, :NB, :] = dof_v[...]
    widen(star_v, m_ref)
    taylor_buffer(x_ref, first_ref, y_ref, m_ref, wk, lambda lanes: (0.5, 1.0 / 6.0), b_ref)
    writes[0].start()
    writes[4].start()
    send = send_columns(send_v)
    send_blocks(b_ref, send, near_ref, far_ref)
    writes[1].start()
    writes[2].start()
    table_ref[NEIGHBOUR : NEIGHBOUR + 4, :] = index_v[...].astype(F32)
    table_ref[FACE : FACE + 4, :] = face_v[...].astype(F32)
    table_ref[CLUSTER : CLUSTER + 1, :] = cluster_v[...].astype(F32)
    table_ref[DAMAGE : DAMAGE + 1, :] = damage_v[...].astype(F32)
    table_ref[COUNT : COUNT + 1, :] = jnp.full((1, elements), count_v[0], jnp.int32).astype(F32)
    table_ref[COHESION : COHESION + 1, :] = cohesion_v[...]
    table_ref[SEND : SEND + 1, :] = send
    table_ref[YIELD : YIELD + NB, :] = yield_v[...].astype(F32)
    writes[3].start()
    for write in writes:
        write.wait()


def local_part(b_ref, wv_ref, wf_ref, table_ref, ms_ref, ml_ref, mn_ref, out_ref, y_ref, start):
    elements = b_ref.shape[-1]
    basis_products(wv_ref[...], b_ref, y_ref, 7)
    source = b_ref[...].reshape(NQ * R, elements)
    far_sides(source, table_ref[NEIGHBOUR : NEIGHBOUR + 4], table_ref[FACE : FACE + 4], wf_ref, y_ref, 7)

    def body(lanes):
        acc = star_sum(y_ref, [ms_ref, ml_ref, mn_ref], lanes, [start(p, lanes) for p in range(NQ)])
        for p in range(NQ):
            out_ref[p, :, lanes] = acc[p]

    each_half(elements, body)


def padded(ref, p, lanes):
    return jnp.concatenate([ref[p, :, lanes], jnp.zeros((R - NB, LANES), F32)], axis=0)


def local_kernel(
    dof_ref, b_ref, star_ref, local_ref, neigh_ref, wv_ref, wf_ref, table_ref, out_ref, ms_ref, ml_ref, mn_ref, mask_ref, y_ref
):
    widen(star_ref, ms_ref)
    widen(local_ref, ml_ref)
    widen(neigh_ref, mn_ref)
    local_part(
        b_ref, wv_ref, wf_ref, table_ref, ms_ref, ml_ref, mn_ref, out_ref, y_ref, lambda p, lanes: padded(dof_ref, p, lanes)
    )
    elements = out_ref.shape[-1]
    rows = lax.broadcasted_iota(jnp.int32, (elements, elements), 0).astype(F32)
    slot = lax.broadcasted_iota(jnp.int32, (1, elements), 1).astype(F32)
    live = jnp.where(slot < table_ref[COUNT : COUNT + 1], table_ref[DAMAGE : DAMAGE + 1], -1.0)
    listed = lax.dot_general(
        jnp.ones((8, elements), BF16),
        jnp.where(rows == live, 1.0, 0.0).astype(BF16),
        (((1,), (1,)), ((), ())),
        preferred_element_type=F32,
    )[0:1]
    mask_ref[...] = jnp.where(listed > 0.5, table_ref[YIELD : YIELD + R], 0.0)


def again_kernel(base_ref, b_ref, wv_ref, wf_ref, table_ref, ms_ref, ml_ref, mn_ref, out_ref, y_ref):
    local_part(b_ref, wv_ref, wf_ref, table_ref, ms_ref, ml_ref, mn_ref, out_ref, y_ref, lambda p, lanes: base_ref[p, :, lanes])


def ghost_source(pos_ref, near_ref, even_ref, odd_ref):
    me, total = pos_ref[0], pos_ref[1]
    core = me % 2
    chip = (me // 2) % 2 == 0
    near, even, odd = near_ref[...], even_ref[...], odd_ref[...]
    up = jnp.where(chip, even, odd)
    down = jnp.where(chip, odd, even)
    half = near.shape[1] // 2
    side = lax.broadcasted_iota(jnp.int32, near.shape, 1) // half
    across = jnp.where(core == 0, down, up)
    one = jnp.where(side == core, across, near)
    two = jnp.where(side == 0, up, down)
    one = jnp.where(jnp.where(side == 0, me - 1, total - 2 - me) >= 0, one, 0.0)
    two = jnp.where(jnp.where(side == 0, total - 3 - me, me - 2) >= 0, two, 0.0)
    return jnp.concatenate([one, two], axis=1)


def ghost_part(pos_ref, near_ref, even_ref, odd_ref, wf_ref, table_ref, y_ref):
    elements = table_ref.shape[-1]
    ghosts = near_ref.shape[-1] // 2
    index = table_ref[NEIGHBOUR : NEIGHBOUR + 4] - elements
    last = jnp.where(index >= 3 * ghosts, index - ghosts, index + ghosts)
    index = jnp.where(index >= 2 * ghosts, last, index)
    source = ghost_source(pos_ref, near_ref, even_ref, odd_ref)
    far_sides(source, index, table_ref[FACE : FACE + 4], wf_ref, y_ref, 0)


def second_kernel(
    pos_ref, v_ref, dof_ref, near_ref, even_ref, odd_ref, wk_ref, wf_ref, table_ref, ms_ref, mn_ref,
    state_ref, b_ref, near_out, far_out,
    x_ref, first_ref, y_ref,
):
    elements = v_ref.shape[-1]
    ghost_part(pos_ref, near_ref, even_ref, odd_ref, wf_ref, table_ref, y_ref)

    def body(lanes):
        acc = star_sum(y_ref, [mn_ref], lanes, [v_ref[p, :, lanes] for p in range(NQ)])
        fine = table_ref[CLUSTER : CLUSTER + 1, lanes] < 0.5
        for p in range(NQ):
            state_ref[p, :, lanes] = acc[p]
            x_ref[p, :, lanes] = jnp.where(fine, acc[p], padded(dof_ref, p, lanes))

    each_half(elements, body)

    def weights_at(lanes):
        fine = table_ref[CLUSTER : CLUSTER + 1, lanes] < 0.5
        return jnp.where(fine, 0.5, 1.5), jnp.where(fine, 1.0 / 6.0, 7.0 / 6.0)

    taylor_buffer(x_ref, first_ref, y_ref, ms_ref, wk_ref[...], weights_at, b_ref)
    send_blocks(b_ref, table_ref[SEND : SEND + 1], near_out, far_out)


def last_kernel(
    pos_ref, v_ref, near_ref, even_ref, odd_ref, wf_ref, table_ref, mn_ref, mask_ref, wp_ref,
    out_ref,
    x_ref, y_ref,
):
    elements = v_ref.shape[-1]
    ghost_part(pos_ref, near_ref, even_ref, odd_ref, wf_ref, table_ref, y_ref)

    def body(lanes):
        acc = star_sum(y_ref, [mn_ref], lanes, [v_ref[p, :, lanes] for p in range(NQ)])
        for p in range(NQ):
            x_ref[p, :, lanes] = acc[p]

    each_half(elements, body)

    points = [dot(wp_ref[0], stack_values(x_ref[q])) for q in range(6)]
    pressure = (points[0] + points[1] + points[2]) / 3.0
    normal = [points[q] - pressure for q in range(3)]
    normal_sum = normal[0] * normal[0] + normal[1] * normal[1] + normal[2] * normal[2]
    shear_sum = points[3] * points[3] + points[4] * points[4] + points[5] * points[5]
    tau = jnp.sqrt(0.5 * normal_sum + shear_sum)
    strength = table_ref[COHESION : COHESION + 1]
    limit = jnp.maximum(strength - FRICTION * pressure, 0.5 * strength)
    rate = jnp.where(mask_ref[...] > 0.5, RELAXATION * (limit / jnp.maximum(tau, limit) - 1.0), 0.0)
    deviation = normal + points[3:]
    for q in range(6):
        change = dot(wp_ref[1], stack_values(rate * deviation[q]))
        out_ref[q] = (x_ref[q] + change)[:NB]
    for q in range(6, NQ):
        out_ref[q] = x_ref[q, :NB, :]


def spec(shape, dtype=F32):
    return jax.ShapeDtypeStruct(shape, dtype)


VMEM = pl.BlockSpec(memory_space=pltpu.VMEM)
SMEM = pl.BlockSpec(memory_space=pltpu.SMEM)
HBM = pl.BlockSpec(memory_space=pltpu.HBM)


def call(kernel, inputs, outputs, scratch, smem=0, cost=0, space=VMEM, grant=40):
    out_space = space if space is HBM else VMEM
    return pl.pallas_call(
        kernel,
        out_shape=outputs,
        in_specs=[SMEM] * smem + [space] * (len(inputs) - smem),
        out_specs=jax.tree.map(lambda _: out_space, outputs),
        scratch_shapes=[pltpu.VMEM(*one) if isinstance(one, tuple) else one for one in scratch],
        compiler_params=pltpu.CompilerParams(vmem_limit_bytes=grant * 1024 * 1024),
        cost_estimate=pl.CostEstimate(flops=cost, bytes_accessed=1 << 20, transcendentals=0),
    )(*inputs)


def core_swap(total):
    return [(i, i ^ 1) for i in range(total)]


def even_chip_swap(total):
    return [(i, i ^ 2) for i in range(total)]


def odd_chip_swap(total):
    route = [(i, i) for i in (0, 1, total - 2, total - 1)]
    for i in range(2, total - 2, 4):
        for k in (i, i + 1):
            route += [(k, k + 2), (k + 2, k)]
    return route


def exchange(near, far, me, total, beside):
    got = lax.ppermute(near, "dom", core_swap(total))
    left = lax.broadcasted_iota(jnp.int32, got.shape, 1) < got.shape[1] // 2
    forward = left == ((me // 2) % 2 == 0)
    to_even, to_odd = jnp.where(forward, got, far), jnp.where(forward, far, got)
    beside, to_even, to_odd = lax.optimization_barrier((beside, to_even, to_odd))
    even = lax.ppermute(to_even, "dom", even_chip_swap(total))
    odd = lax.ppermute(to_odd, "dom", odd_chip_swap(total))
    return got, even, odd, beside


def per_device(
    dof_values,
    star_mats,
    flux_local,
    flux_neigh,
    kstiff,
    flux_minus,
    flux_plus,
    neighbour,
    neigh_face,
    cluster,
    send_list,
    damage_list,
    damage_count,
    yield_mask,
    cohesion,
    to_points,
    from_points,
):
    elements = dof_values.shape[-1]
    total = lax.axis_size("dom")
    me = lax.axis_index("dom")
    position = jnp.stack([me.astype(jnp.int32), jnp.int32(total)])
    ghosts = send_list.shape[-1]

    field = spec((NQ, R, elements))
    block = spec((NQ * R, 2 * ghosts))
    x_s = (field.shape, F32)

    def y_s(blocks):
        return ((blocks, NQ, R, elements), F32)

    def m_o(blocks):
        return spec((NQ * NQ, blocks, elements))

    star = jnp.transpose(star_mats, (1, 2, 0, 3))
    own = jnp.transpose(flux_local, (1, 2, 0, 3))
    other = jnp.transpose(flux_neigh, (1, 2, 0, 3))
    inputs = [
        dof_values, star, kstiff, send_list, neighbour, neigh_face, cluster[None], damage_list, damage_count, cohesion[None], yield_mask
    ]
    held = [(one.shape, one.dtype) for one in inputs]
    held[3] = (send_list.shape[1:], send_list.dtype)
    held[8] = pltpu.SMEM(damage_count.shape, damage_count.dtype)
    outputs = [field, block, block, spec((ROWS, elements)), spec((3 * R, K3), BF16)]
    buffer_one, near, far, table, wk = call(
        predict_kernel,
        inputs,
        outputs,
        held
        + [((3 * R, LANES), F32), x_s, x_s, y_s(3), (m_o(3).shape, F32)]
        + [(one.shape, one.dtype) for one in outputs]
        + [pltpu.SemaphoreType.DMA((len(inputs),)), pltpu.SemaphoreType.DMA((len(outputs),))],
        space=HBM,
        grant=60,
    )
    wv = stack_weights(jnp.concatenate([jnp.swapaxes(kstiff, 1, 2), -flux_minus])).reshape(7 * R, K3)
    wf = stack_weights(-flux_plus).reshape(4, 4 * R, K3)
    wp = stack_weights(jnp.stack([to_points, from_points]))

    near, even, odd, buffer_one = exchange(near, far, me, total, buffer_one)
    started, ms, ml, mn, mask = call(
        local_kernel,
        [dof_values, buffer_one, star, own, other, wv, wf, table],
        (field, m_o(3), m_o(4), m_o(4), spec((R, elements))),
        [y_s(11)],
        cost=1_000_000_000,
    )
    updated, buffer_two, near, far = call(
        second_kernel,
        [position, started, dof_values, near, even, odd, wk, wf, table, ms, mn],
        (field, field, block, block),
        [x_s, x_s, y_s(4)],
        smem=1,
    )
    near, even, odd, buffer_two = exchange(near, far, me, total, buffer_two)
    started = call(
        again_kernel,
        [updated, buffer_two, wv, wf, table, ms, ml, mn],
        field,
        [y_s(11)],
        cost=1_000_000_000,
    )
    return call(
        last_kernel,
        [position, started, near, even, odd, wf, table, mn, mask, wp],
        spec(dof_values.shape),
        [x_s, y_s(4)],
        smem=1,
    )


def solution(mesh):
    return jax.shard_map(
        per_device,
        mesh=mesh,
        in_specs=(
            P(None, None, "dom"),
            P(None, None, None, "dom"),
            P(None, None, None, "dom"),
            P(None, None, None, "dom"),
            P(),
            P(),
            P(),
            P(None, "dom"),
            P(None, "dom"),
            P("dom"),
            P("dom", None, None),
            P("dom", None),
            P("dom"),
            P(None, "dom"),
            P("dom"),
            P(),
            P(),
        ),
        out_specs=P(None, None, "dom"),
        check_vma=False,
    )
```

```python
import jax
import jax.numpy as jnp
from jax import lax
from jax.experimental import pallas as pl
from jax.experimental.pallas import tpu as pltpu
from jax.sharding import PartitionSpec as P

NQ = 9
NB = 20
R = 24
K3 = 3 * R
LANES = 128
FRICTION = 0.6
RELAXATION = 0.5
F32 = jnp.float32
BF16 = jnp.bfloat16


def stack_values(x):
    high = x.astype(BF16).astype(F32)
    return jnp.concatenate([high, x - high, high], axis=0).astype(BF16)


def dot(a, b):
    return jnp.dot(a, b, preferred_element_type=F32)


def widen(src_ref, dst_ref):
    for q in range(NQ):
        for p in range(NQ):
            dst_ref[q * NQ + p] = src_ref[q, p].astype(F32)


def basis_products(weights, x_ref, y_ref, blocks, base=0):
    for q in range(NQ):
        out = dot(weights, stack_values(x_ref[q]))
        for k in range(blocks):
            y_ref[base + k, q] = out[k * R : (k + 1) * R]


def star_sum(y_ref, m_refs, lanes, start):
    acc = list(start)
    for q in range(NQ):
        k = 0
        for m_ref in m_refs:
            for row in range(m_ref.shape[1]):
                y = y_ref[k, q, :, lanes]
                for p in range(NQ):
                    acc[p] = acc[p] + y * m_ref[q * NQ + p, row : row + 1, lanes]
                k += 1
    return acc


def each_half(elements, body):
    for start in range(0, elements, LANES):
        body(pl.ds(start, LANES))


def taylor_buffer(x_ref, first_ref, y_ref, m_ref, wk, weights_at, out_ref):
    elements = x_ref.shape[-1]
    basis_products(wk, x_ref, y_ref, 3)

    def first(lanes):
        acc = star_sum(y_ref, [m_ref], lanes, [jnp.zeros((R, LANES), F32)] * NQ)
        for p in range(NQ):
            first_ref[p, :, lanes] = acc[p]

    each_half(elements, first)
    basis_products(wk, first_ref, y_ref, 3)

    def second(lanes):
        acc = star_sum(y_ref, [m_ref], lanes, [jnp.zeros((R, LANES), F32)] * NQ)
        w1, w2 = weights_at(lanes)
        for p in range(NQ):
            out_ref[p, :, lanes] = x_ref[p, :, lanes] + (w1 * first_ref[p, :, lanes] + w2 * acc[p])

    each_half(elements, second)


def send_blocks(b_ref, send, near_ref, far_ref):
    elements = b_ref.shape[-1]
    columns = send.shape[-1]
    b = b_ref[...].reshape(NQ * R, elements)
    high = b.astype(BF16)
    low = (b - high.astype(F32)).astype(BF16)
    rows = lax.broadcasted_iota(jnp.int32, (elements, columns), 0).astype(F32)
    hot = jnp.where(rows == send, 1.0, 0.0).astype(BF16)
    out = dot(high, hot) + dot(low, hot)
    for q in range(NQ):
        near_ref[q * NB : (q + 1) * NB] = out[q * R : q * R + NB, : columns // 2]
        far_ref[q * NB : (q + 1) * NB] = out[q * R : q * R + NB, columns // 2 :]


def far_sides(source, index, face, w_ref, y_ref, base):
    high = source.astype(BF16)
    low = (source - high.astype(F32)).astype(BF16)
    both = jnp.concatenate([high, low], axis=0)
    elements = index.shape[-1]
    rows = lax.broadcasted_iota(jnp.int32, (source.shape[-1], elements), 0).astype(F32)
    size = NQ * R
    gathered = []
    for f in range(4):
        hot = jnp.where(rows == index[f : f + 1], 1.0, 0.0).astype(BF16)
        gathered.append(dot(both, hot))
    for f, picked in enumerate(gathered):
        kind = jnp.broadcast_to(face[f : f + 1], (R, elements))
        w = w_ref[W_FAR + 4 * f * R : W_FAR + 4 * (f + 1) * R]
        for q in range(NQ):
            high_rows = picked[q * R : (q + 1) * R]
            low_rows = picked[size + q * R : size + (q + 1) * R]
            out = dot(w, jnp.concatenate([high_rows, low_rows, high_rows], axis=0).astype(BF16))
            y_ref[base + f, q] = jnp.where(
                kind < 2,
                jnp.where(kind == 0, out[:R], out[R : 2 * R]),
                jnp.where(kind == 2, out[2 * R : 3 * R], out[3 * R :]),
            )


def place_kernel(twice_ref, once_ref):
    row = lax.broadcasted_iota(jnp.int32, twice_ref.shape, 0)
    column = lax.broadcasted_iota(jnp.int32, twice_ref.shape, 1)
    twice_ref[...] = jnp.where((column == row) | (column == row + R), 1.0, 0.0).astype(BF16)
    once_ref[...] = jnp.where(column == row + 2 * R, 1.0, 0.0).astype(BF16)


def place_weights(w, twice_ref, once_ref):
    high = w.astype(BF16)
    low = (w - high.astype(F32)).astype(BF16)
    return (dot(high, twice_ref[...]) + dot(low, once_ref[...])).astype(BF16)


W_OWN, W_FAR, W_POINTS, W_ROWS = 0, 7 * R, 23 * R, 25 * R


def fill_stiffness(w_ref, kstiff_ref):
    w_ref[...] = jnp.zeros(w_ref.shape, F32)
    for d in range(3):
        w_ref[d * R : d * R + NB, :NB] = kstiff_ref[d]


def fill_weights(w_ref, kstiff_ref, minus_ref, plus_ref, to_ref, from_ref):
    fill_stiffness(w_ref, kstiff_ref)
    row = lax.broadcasted_iota(jnp.int32, (R, LANES), 0)
    column = lax.broadcasted_iota(jnp.int32, (R, LANES), 1)
    same = jnp.where(row == column, 1.0, 0.0).astype(BF16)
    stiff = w_ref[: 3 * R]
    high = stiff.astype(BF16)
    low = (stiff - high.astype(F32)).astype(BF16)
    turned = [
        lax.dot_general(same, part, (((1,), (1,)), ((), ())), preferred_element_type=F32) for part in (high, low)
    ]
    turned = turned[0] + turned[1]
    for d in range(3):
        w_ref[W_OWN + d * R : W_OWN + (d + 1) * R, :R] = turned[:, d * R : (d + 1) * R]
    for f in range(4):
        start = W_OWN + (3 + f) * R
        w_ref[start : start + NB, :NB] = -minus_ref[:, f, :]
        for h in range(4):
            start = W_FAR + (4 * f + h) * R
            w_ref[start : start + NB, :NB] = -plus_ref[f, :, h, :]
    w_ref[W_POINTS : W_POINTS + NB, :NB] = to_ref[...]
    w_ref[W_POINTS + R : W_POINTS + R + NB, :NB] = from_ref[...]


def send_columns(send_ref):
    slots, ghosts = send_ref.shape
    width = slots * ghosts
    row = lax.broadcasted_iota(jnp.int32, (ghosts, width), 0)
    column = lax.broadcasted_iota(jnp.int32, (ghosts, width), 1)
    repeat = jnp.where(column % ghosts == row, 1.0, 0.0).astype(BF16)
    wide = dot(send_ref[...].astype(F32).astype(BF16), repeat)
    slot = lax.broadcasted_iota(jnp.int32, (1, width), 1) // ghosts
    first = jnp.where(slot == 0, wide[0:1], wide[1:2])
    second = jnp.where(slot == 2, wide[3:4], wide[2:3])
    return jnp.where(slot < 2, first, second)


NEIGHBOUR, FACE, CLUSTER, DAMAGE, COUNT, COHESION, SEND, YIELD = 0, 4, 8, 9, 10, 11, 12, 16
ROWS = 40


def predict_kernel(
    dof_ref, star_ref, kstiff_ref, send_ref, twice_ref, once_ref,
    b_ref, near_ref, far_ref, m_ref, wk_ref, send_out,
    w_ref, x_ref, first_ref, y_ref,
):
    fill_stiffness(w_ref, kstiff_ref)
    wk_ref[...] = place_weights(w_ref[...], twice_ref, once_ref)
    x_ref[:, NB:, :] = jnp.zeros((NQ, R - NB, x_ref.shape[-1]), F32)
    x_ref[:, :NB, :] = dof_ref[...]
    widen(star_ref, m_ref)
    taylor_buffer(x_ref, first_ref, y_ref, m_ref, wk_ref[...], lambda lanes: (0.5, 1.0 / 6.0), b_ref)
    send = send_columns(send_ref.at[0])
    send_out[...] = send
    send_blocks(b_ref, send, near_ref, far_ref)


NEIGHBOUR, FACE, CLUSTER, DAMAGE, COHESION, YIELD = 0, 4, 8, 9, 10, 16
ROWS = 40


def fill_table(table_ref, index_ref, face_ref, cluster_ref, damage_ref, count_ref, cohesion_ref, yield_ref):
    elements = table_ref.shape[-1]
    table_ref[...] = jnp.zeros(table_ref.shape, F32)
    table_ref[NEIGHBOUR : NEIGHBOUR + 4, :] = index_ref[...].astype(F32)
    table_ref[FACE : FACE + 4, :] = face_ref[...].astype(F32)
    table_ref[CLUSTER : CLUSTER + 1, :] = cluster_ref[...].astype(F32)
    slot = lax.broadcasted_iota(jnp.int32, (1, elements), 1)
    count = jnp.broadcast_to(count_ref[...], (1, elements))
    table_ref[DAMAGE : DAMAGE + 1, :] = jnp.where(slot < count, damage_ref[...], -1).astype(F32)
    table_ref[COHESION : COHESION + 1, :] = cohesion_ref[...]
    table_ref[YIELD : YIELD + NB, :] = yield_ref[...].astype(F32)


def local_part(b_ref, w_ref, table_ref, ms_ref, ml_ref, mn_ref, out_ref, y_ref, start):
    elements = b_ref.shape[-1]
    basis_products(w_ref[W_OWN:W_FAR], b_ref, y_ref, 7)
    source = b_ref[...].reshape(NQ * R, elements)
    far_sides(source, table_ref[NEIGHBOUR : NEIGHBOUR + 4], table_ref[FACE : FACE + 4], w_ref, y_ref, 7)

    def body(lanes):
        acc = star_sum(y_ref, [ms_ref, ml_ref, mn_ref], lanes, [start(p, lanes) for p in range(NQ)])
        for p in range(NQ):
            out_ref[p, :, lanes] = acc[p]

    each_half(elements, body)


def padded(ref, p, lanes):
    return jnp.concatenate([ref[p, :, lanes], jnp.zeros((R - NB, LANES), F32)], axis=0)


def local_kernel(
    dof_ref, b_ref, ms_ref, local_ref, neigh_ref,
    kstiff_ref, minus_ref, plus_ref, to_ref, from_ref, twice_ref, once_ref,
    index_ref, face_ref, cluster_ref, damage_ref, count_ref, cohesion_ref, yield_ref,
    out_ref, ml_ref, mn_ref, mask_ref, table_ref, weights_ref,
    w_ref, y_ref,
):
    fill_weights(w_ref, kstiff_ref, minus_ref, plus_ref, to_ref, from_ref)
    weights_ref[...] = place_weights(w_ref[...], twice_ref, once_ref)
    fill_table(table_ref, index_ref, face_ref, cluster_ref, damage_ref, count_ref, cohesion_ref, yield_ref)
    widen(local_ref, ml_ref)
    widen(neigh_ref, mn_ref)
    local_part(
        b_ref, weights_ref, table_ref, ms_ref, ml_ref, mn_ref, out_ref, y_ref, lambda p, lanes: padded(dof_ref, p, lanes)
    )
    elements = out_ref.shape[-1]
    rows = lax.broadcasted_iota(jnp.int32, (elements, elements), 0).astype(F32)
    listed = lax.dot_general(
        jnp.ones((8, elements), BF16),
        jnp.where(rows == table_ref[DAMAGE : DAMAGE + 1], 1.0, 0.0).astype(BF16),
        (((1,), (1,)), ((), ())),
        preferred_element_type=F32,
    )[0:1]
    mask_ref[...] = jnp.where(listed > 0.5, table_ref[YIELD : YIELD + R], 0.0)


def again_kernel(base_ref, b_ref, w_ref, table_ref, ms_ref, ml_ref, mn_ref, out_ref, y_ref):
    local_part(b_ref, w_ref, table_ref, ms_ref, ml_ref, mn_ref, out_ref, y_ref, lambda p, lanes: base_ref[p, :, lanes])


def ghost_source(near_ref, even_ref, odd_ref):
    me, total = lax.axis_index("dom"), lax.axis_size("dom")
    core = me % 2
    chip = (me // 2) % 2 == 0
    near, even, odd = near_ref[...], even_ref[...], odd_ref[...]
    up = jnp.where(chip, even, odd)
    down = jnp.where(chip, odd, even)
    half = near.shape[1] // 2
    side = lax.broadcasted_iota(jnp.int32, near.shape, 1) // half
    across = jnp.where(core == 0, down, up)
    one = jnp.where(side == core, across, near)
    two = jnp.where(side == 0, up, down)
    one = jnp.where(jnp.where(side == 0, me - 1, total - 2 - me) >= 0, one, 0.0)
    two = jnp.where(jnp.where(side == 0, total - 3 - me, me - 2) >= 0, two, 0.0)
    pad = jnp.zeros((R - NB, 2 * near.shape[1]), F32)
    both = jnp.concatenate([one, two], axis=1)
    return jnp.concatenate([piece for q in range(NQ) for piece in (both[q * NB : (q + 1) * NB], pad)], axis=0)


def ghost_part(near_ref, even_ref, odd_ref, w_ref, table_ref, y_ref):
    elements = table_ref.shape[-1]
    ghosts = near_ref.shape[-1] // 2
    index = table_ref[NEIGHBOUR : NEIGHBOUR + 4] - elements
    last = jnp.where(index >= 3 * ghosts, index - ghosts, index + ghosts)
    index = jnp.where(index >= 2 * ghosts, last, index)
    source = ghost_source(near_ref, even_ref, odd_ref)
    far_sides(source, index, table_ref[FACE : FACE + 4], w_ref, y_ref, 0)


def second_kernel(
    v_ref, dof_ref, near_ref, even_ref, odd_ref, wk_ref, send_ref, w_ref, table_ref, ms_ref, mn_ref,
    state_ref, b_ref, near_out, far_out,
    x_ref, first_ref, y_ref,
):
    elements = v_ref.shape[-1]
    ghost_part(near_ref, even_ref, odd_ref, w_ref, table_ref, y_ref)

    def body(lanes):
        acc = star_sum(y_ref, [mn_ref], lanes, [v_ref[p, :, lanes] for p in range(NQ)])
        fine = table_ref[CLUSTER : CLUSTER + 1, lanes] < 0.5
        for p in range(NQ):
            state_ref[p, :, lanes] = acc[p]
            x_ref[p, :, lanes] = jnp.where(fine, acc[p], padded(dof_ref, p, lanes))

    each_half(elements, body)

    def weights_at(lanes):
        fine = table_ref[CLUSTER : CLUSTER + 1, lanes] < 0.5
        return jnp.where(fine, 0.5, 1.5), jnp.where(fine, 1.0 / 6.0, 7.0 / 6.0)

    taylor_buffer(x_ref, first_ref, y_ref, ms_ref, wk_ref[...], weights_at, b_ref)
    send_blocks(b_ref, send_ref[...], near_out, far_out)


def last_kernel(
    v_ref, near_ref, even_ref, odd_ref, w_ref, table_ref, mn_ref, mask_ref,
    result_ref,
    x_ref, y_ref, out_ref, sems,
):
    writes = [pltpu.make_async_copy(out_ref.at[q], result_ref.at[q], sems.at[q]) for q in range(NQ)]
    elements = v_ref.shape[-1]
    ghost_part(near_ref, even_ref, odd_ref, w_ref, table_ref, y_ref)

    def body(lanes):
        acc = star_sum(y_ref, [mn_ref], lanes, [v_ref[p, :, lanes] for p in range(NQ)])
        for p in range(NQ):
            x_ref[p, :, lanes] = acc[p]

    each_half(elements, body)

    for q in range(6, NQ):
        out_ref[q] = x_ref[q, :NB, :]
        writes[q].start()
    points = [dot(w_ref[W_POINTS : W_POINTS + R], stack_values(x_ref[q])) for q in range(6)]
    pressure = (points[0] + points[1] + points[2]) / 3.0
    normal = [points[q] - pressure for q in range(3)]
    normal_sum = normal[0] * normal[0] + normal[1] * normal[1] + normal[2] * normal[2]
    shear_sum = points[3] * points[3] + points[4] * points[4] + points[5] * points[5]
    tau = jnp.sqrt(0.5 * normal_sum + shear_sum)
    strength = table_ref[COHESION : COHESION + 1]
    limit = jnp.maximum(strength - FRICTION * pressure, 0.5 * strength)
    rate = jnp.where(mask_ref[...] > 0.5, RELAXATION * (limit / jnp.maximum(tau, limit) - 1.0), 0.0)
    deviation = normal + points[3:]
    for q in range(6):
        change = dot(w_ref[W_POINTS + R : W_ROWS], stack_values(rate * deviation[q]))
        out_ref[q] = (x_ref[q] + change)[:NB]
        writes[q].start()
    for write in writes:
        write.wait()


def spec(shape, dtype=F32):
    return jax.ShapeDtypeStruct(shape, dtype)


VMEM = pl.BlockSpec(memory_space=pltpu.VMEM)
HBM = pl.BlockSpec(memory_space=pltpu.HBM)


def call(kernel, inputs, outputs, scratch, cost=0, out_space=VMEM):
    return pl.pallas_call(
        kernel,
        out_shape=outputs,
        in_specs=[VMEM] * len(inputs),
        out_specs=jax.tree.map(lambda _: out_space, outputs),
        scratch_shapes=[pltpu.VMEM(*one) if isinstance(one, tuple) else one for one in scratch],
        compiler_params=pltpu.CompilerParams(vmem_limit_bytes=40 * 1024 * 1024),
        cost_estimate=pl.CostEstimate(flops=cost, bytes_accessed=1 << 20, transcendentals=0),
    )(*inputs)


def core_swap(total):
    return [(i, i ^ 1) for i in range(total)]


def even_chip_swap(total):
    return [(i, i ^ 2) for i in range(total)]


def odd_chip_swap(total):
    route = [(i, i) for i in (0, 1, total - 2, total - 1)]
    for i in range(2, total - 2, 4):
        for k in (i, i + 1):
            route += [(k, k + 2), (k + 2, k)]
    return route


def exchange(near, far, me, total, beside):
    got = lax.ppermute(near, "dom", core_swap(total))
    left = lax.broadcasted_iota(jnp.int32, got.shape, 1) < got.shape[1] // 2
    forward = left == ((me // 2) % 2 == 0)
    to_even, to_odd = jnp.where(forward, got, far), jnp.where(forward, far, got)
    beside, to_even, to_odd = lax.optimization_barrier((beside, to_even, to_odd))
    even = lax.ppermute(to_even, "dom", even_chip_swap(total))
    odd = lax.ppermute(to_odd, "dom", odd_chip_swap(total))
    return got, even, odd, beside


def per_device(
    dof_values,
    star_mats,
    flux_local,
    flux_neigh,
    kstiff,
    flux_minus,
    flux_plus,
    neighbour,
    neigh_face,
    cluster,
    send_list,
    damage_list,
    damage_count,
    yield_mask,
    cohesion,
    to_points,
    from_points,
):
    elements = dof_values.shape[-1]
    total = lax.axis_size("dom")
    me = lax.axis_index("dom")
    ghosts = send_list.shape[-1]

    field = spec((NQ, R, elements))
    block = spec((NQ * NB, 2 * ghosts))
    x_s = (field.shape, F32)

    def y_s(blocks):
        return ((blocks, NQ, R, elements), F32)

    def m_o(blocks):
        return spec((NQ * NQ, blocks, elements))

    star = jnp.transpose(star_mats, (1, 2, 0, 3))
    own = jnp.transpose(flux_local, (1, 2, 0, 3))
    other = jnp.transpose(flux_neigh, (1, 2, 0, 3))
    minus = jnp.transpose(flux_minus, (1, 0, 2))
    plus = jnp.transpose(flux_plus, (0, 2, 1, 3))

    place = spec((LANES, K3), BF16)
    twice, once = call(place_kernel, [], (place, place), [], cost=4_000_000_000)
    buffer_one, near, far, ms, wk, send = call(
        predict_kernel,
        [dof_values, star, kstiff, send_list, twice, once],
        (field, block, block, m_o(3), spec((3 * R, K3), BF16), spec((1, 4 * ghosts))),
        [((3 * R, LANES), F32), x_s, x_s, y_s(3)],
    )
    near, even, odd, buffer_one = exchange(near, far, me, total, buffer_one)
    started, ml, mn, mask, table, weights = call(
        local_kernel,
        [
            dof_values, buffer_one, ms, own, other,
            kstiff, minus, plus, to_points, from_points, twice, once,
            neighbour, neigh_face, cluster[None], damage_list, damage_count[None], cohesion[None], yield_mask,
        ],
        (field, m_o(4), m_o(4), spec((R, elements)), spec((ROWS, elements)), spec((W_ROWS, K3), BF16)),
        [((W_ROWS, LANES), F32), y_s(11)],
        cost=1_000_000_000,
    )
    updated, buffer_two, near, far = call(
        second_kernel,
        [started, dof_values, near, even, odd, wk, send, weights, table, ms, mn],
        (field, field, block, block),
        [x_s, x_s, y_s(4)],
    )
    near, even, odd, buffer_two = exchange(near, far, me, total, buffer_two)
    started = call(
        again_kernel,
        [updated, buffer_two, weights, table, ms, ml, mn],
        field,
        [y_s(11)],
        cost=1_000_000_000,
    )
    return call(
        last_kernel,
        [started, near, even, odd, weights, table, mn, mask],
        spec(dof_values.shape),
        [x_s, y_s(4), (dof_values.shape, F32), pltpu.SemaphoreType.DMA((NQ,))],
        out_space=HBM,
    )


def solution(mesh):
    return jax.shard_map(
        per_device,
        mesh=mesh,
        in_specs=(
            P(None, None, "dom"),
            P(None, None, None, "dom"),
            P(None, None, None, "dom"),
            P(None, None, None, "dom"),
            P(),
            P(),
            P(),
            P(None, "dom"),
            P(None, "dom"),
            P("dom"),
            P("dom", None, None),
            P("dom", None),
            P("dom"),
            P(None, "dom"),
            P("dom"),
            P(),
            P(),
        ),
        out_specs=P(None, None, "dom"),
        check_vma=False,
    )
```

```python
import jax
import jax.numpy as jnp
from jax import lax
from jax.experimental import pallas as pl
from jax.experimental.pallas import tpu as pltpu
from jax.sharding import PartitionSpec as P

NQ = 9
NB = 20
R = 24
K3 = 3 * R
LANES = 128
FRICTION = 0.6
RELAXATION = 0.5
F32 = jnp.float32
BF16 = jnp.bfloat16


def stack_values(x):
    high = x.astype(BF16).astype(F32)
    return jnp.concatenate([high, x - high, high], axis=0).astype(BF16)


def dot(a, b):
    return jnp.dot(a, b, preferred_element_type=F32)


def widen(src_ref, dst_ref):
    for q in range(NQ):
        for p in range(NQ):
            dst_ref[q * NQ + p] = src_ref[q, p].astype(F32)


def basis_products(weights, x_ref, y_ref, blocks, base=0):
    for q in range(NQ):
        out = dot(weights, stack_values(x_ref[q]))
        for k in range(blocks):
            y_ref[base + k, q] = out[k * R : (k + 1) * R]


def star_sum(y_ref, m_refs, lanes, start):
    acc = list(start)
    for q in range(NQ):
        k = 0
        for m_ref in m_refs:
            for row in range(m_ref.shape[1]):
                y = y_ref[k, q, :, lanes]
                for p in range(NQ):
                    acc[p] = acc[p] + y * m_ref[q * NQ + p, row : row + 1, lanes]
                k += 1
    return acc


def each_half(elements, body):
    for start in range(0, elements, LANES):
        body(pl.ds(start, LANES))


def in_turns(one, two, stages):
    for now, before in zip(stages + [0], [0] + stages):
        done = 0
        for step in range(now):
            next(one, None)
            while done * now < (step + 1) * before:
                next(two, None)
                done += 1
        while done < before:
            next(two, None)
            done += 1
    next(one, None)
    next(two, None)


def star_steps(acc, ys, m_ref, lanes):
    for q in range(NQ):
        for k in range(m_ref.shape[1]):
            y = ys.pop((k, q))
            for p in range(NQ):
                acc[p] = acc[p] + y * m_ref[q * NQ + p, k : k + 1, lanes]
            yield


def far_steps(ys, both, index, face, w_ref):
    size = NQ * R
    gathered = both
    for f in range(4):
        yield
    for q in range(NQ):
        for f in range(4):
            kind = jnp.broadcast_to(face[f : f + 1], (R, LANES))
            w = w_ref[W_FAR + 4 * f * R : W_FAR + 4 * (f + 1) * R]
            high_rows = gathered[f][q * R : (q + 1) * R]
            low_rows = gathered[f][size + q * R : size + (q + 1) * R]
            out = dot(w, jnp.concatenate([high_rows, low_rows, high_rows], axis=0).astype(BF16))
            ys[f, q] = jnp.where(
                kind < 2,
                jnp.where(kind == 0, out[:R], out[R : 2 * R]),
                jnp.where(kind == 2, out[2 * R : 3 * R], out[3 * R :]),
            )
            yield


def derivative_steps(x, following, wk, m_ref, lanes):
    ys = {}
    for q in range(NQ):
        out = dot(wk, stack_values(x[q]))
        for k in range(3):
            ys[k, q] = out[k * R : (k + 1) * R]
        yield
    yield from star_steps(following, ys, m_ref, lanes)


def taylor_steps(x, wk, m_ref, lanes, w1, w2, out_ref):
    first = [jnp.zeros((R, LANES), F32)] * NQ
    yield from derivative_steps(x, first, wk, m_ref, lanes)
    second = [jnp.zeros((R, LANES), F32)] * NQ
    yield from derivative_steps(first, second, wk, m_ref, lanes)
    for p in range(NQ):
        out_ref[p, :, lanes] = x[p] + (w1 * first[p] + w2 * second[p])


def pick_columns(b_ref, send, out_ref):
    elements = b_ref.shape[-1]
    both = split_rows(b_ref[...].reshape(NQ * R, elements))
    rows = lax.broadcasted_iota(jnp.int32, (elements, send.shape[-1]), 0).astype(F32)
    hot = jnp.where(rows == send, 1.0, 0.0).astype(BF16)
    out = dot(both, hot)
    out = out[: NQ * R] + out[NQ * R :]
    for q in range(NQ):
        out_ref[q * NB : (q + 1) * NB] = out[q * R : q * R + NB]


def far_sides(source, index, face, w_ref, y_ref, base):
    high = source.astype(BF16)
    low = (source - high.astype(F32)).astype(BF16)
    both = jnp.concatenate([high, low], axis=0)
    elements = index.shape[-1]
    rows = lax.broadcasted_iota(jnp.int32, (source.shape[-1], elements), 0).astype(F32)
    size = NQ * R
    gathered = []
    for f in range(4):
        hot = jnp.where(rows == index[f : f + 1], 1.0, 0.0).astype(BF16)
        gathered.append(dot(both, hot))
    for f, picked in enumerate(gathered):
        kind = jnp.broadcast_to(face[f : f + 1], (R, elements))
        w = w_ref[W_FAR + 4 * f * R : W_FAR + 4 * (f + 1) * R]
        for q in range(NQ):
            high_rows = picked[q * R : (q + 1) * R]
            low_rows = picked[size + q * R : size + (q + 1) * R]
            out = dot(w, jnp.concatenate([high_rows, low_rows, high_rows], axis=0).astype(BF16))
            y_ref[base + f, q] = jnp.where(
                kind < 2,
                jnp.where(kind == 0, out[:R], out[R : 2 * R]),
                jnp.where(kind == 2, out[2 * R : 3 * R], out[3 * R :]),
            )


def place_kernel(twice_ref, once_ref):
    row = lax.broadcasted_iota(jnp.int32, twice_ref.shape, 0)
    column = lax.broadcasted_iota(jnp.int32, twice_ref.shape, 1)
    twice_ref[...] = jnp.where((column == row) | (column == row + R), 1.0, 0.0).astype(BF16)
    once_ref[...] = jnp.where(column == row + 2 * R, 1.0, 0.0).astype(BF16)


def place_weights(w, twice_ref, once_ref):
    high = w.astype(BF16)
    low = (w - high.astype(F32)).astype(BF16)
    return (dot(high, twice_ref[...]) + dot(low, once_ref[...])).astype(BF16)


W_OWN, W_FAR, W_POINTS, W_ROWS = 0, 7 * R, 23 * R, 25 * R


def fill_stiffness(w_ref, kstiff_ref):
    w_ref[...] = jnp.zeros(w_ref.shape, F32)
    for d in range(3):
        w_ref[d * R : d * R + NB, :NB] = kstiff_ref[d]


def fill_weights(w_ref, kstiff_ref, minus_ref, plus_ref, to_ref, from_ref):
    fill_stiffness(w_ref, kstiff_ref)
    row = lax.broadcasted_iota(jnp.int32, (R, LANES), 0)
    column = lax.broadcasted_iota(jnp.int32, (R, LANES), 1)
    same = jnp.where(row == column, 1.0, 0.0).astype(BF16)
    stiff = w_ref[: 3 * R]
    high = stiff.astype(BF16)
    low = (stiff - high.astype(F32)).astype(BF16)
    turned = [
        lax.dot_general(same, part, (((1,), (1,)), ((), ())), preferred_element_type=F32) for part in (high, low)
    ]
    turned = turned[0] + turned[1]
    for d in range(3):
        w_ref[W_OWN + d * R : W_OWN + (d + 1) * R, :R] = turned[:, d * R : (d + 1) * R]
    for f in range(4):
        start = W_OWN + (3 + f) * R
        w_ref[start : start + NB, :NB] = -minus_ref[:, f, :]
        for h in range(4):
            start = W_FAR + (4 * f + h) * R
            w_ref[start : start + NB, :NB] = -plus_ref[f, :, h, :]
    w_ref[W_POINTS : W_POINTS + NB, :NB] = to_ref[...]
    w_ref[W_POINTS + R : W_POINTS + R + NB, :NB] = from_ref[...]


def send_columns(send_ref):
    slots, ghosts = send_ref.shape
    width = slots * ghosts
    row = lax.broadcasted_iota(jnp.int32, (ghosts, width), 0)
    column = lax.broadcasted_iota(jnp.int32, (ghosts, width), 1)
    repeat = jnp.where(column % ghosts == row, 1.0, 0.0).astype(BF16)
    wide = dot(send_ref[...].astype(F32).astype(BF16), repeat)
    slot = lax.broadcasted_iota(jnp.int32, (1, width), 1) // ghosts
    first = jnp.where(slot == 0, wide[0:1], wide[1:2])
    second = jnp.where(slot == 2, wide[3:4], wide[2:3])
    return jnp.where(slot < 2, first, second)


NEIGHBOUR, FACE, CLUSTER, DAMAGE, COUNT, COHESION, SEND, YIELD = 0, 4, 8, 9, 10, 11, 12, 16
ROWS = 40


def setup_kernel(kstiff_ref, send_ref, twice_ref, once_ref, wk_ref, send_out, w_ref):
    fill_stiffness(w_ref, kstiff_ref)
    wk_ref[...] = place_weights(w_ref[...], twice_ref, once_ref)
    send_out[...] = send_columns(send_ref.at[0])


def far_kernel(b_ref, send_ref, out_ref):
    pick_columns(b_ref, send_ref[:, send_ref.shape[-1] // 2 :], out_ref)


def predict_kernel(dof_ref, star_ref, wk_ref, send_ref, b_ref, near_ref, m_ref):
    widen(star_ref, m_ref)
    wk = wk_ref[...]

    def half(lanes):
        x = [padded(dof_ref, p, lanes) for p in range(NQ)]
        yield from taylor_steps(x, wk, m_ref, lanes, 0.5, 1.0 / 6.0, b_ref)

    in_turns(half(pl.ds(0, LANES)), half(pl.ds(LANES, LANES)), [NQ, 3 * NQ] * 2)
    pick_columns(b_ref, send_ref[:, : send_ref.shape[-1] // 2], near_ref)


NEIGHBOUR, FACE, CLUSTER, DAMAGE, COHESION, YIELD = 0, 4, 8, 9, 10, 16
ROWS = 40


def fill_table(table_ref, index_ref, face_ref, cluster_ref, damage_ref, count_ref, cohesion_ref, yield_ref):
    elements = table_ref.shape[-1]
    table_ref[...] = jnp.zeros(table_ref.shape, F32)
    table_ref[NEIGHBOUR : NEIGHBOUR + 4, :] = index_ref[...].astype(F32)
    table_ref[FACE : FACE + 4, :] = face_ref[...].astype(F32)
    table_ref[CLUSTER : CLUSTER + 1, :] = cluster_ref[...].astype(F32)
    slot = lax.broadcasted_iota(jnp.int32, (1, elements), 1)
    count = jnp.broadcast_to(count_ref[...], (1, elements))
    table_ref[DAMAGE : DAMAGE + 1, :] = jnp.where(slot < count, damage_ref[...], -1).astype(F32)
    table_ref[COHESION : COHESION + 1, :] = cohesion_ref[...]
    table_ref[YIELD : YIELD + NB, :] = yield_ref[...].astype(F32)


def local_part(b_ref, w_ref, table_ref, ms_ref, ml_ref, mn_ref, out_ref, y_ref, start):
    elements = b_ref.shape[-1]
    basis_products(w_ref[W_OWN:W_FAR], b_ref, y_ref, 7)
    source = b_ref[...].reshape(NQ * R, elements)
    far_sides(source, table_ref[NEIGHBOUR : NEIGHBOUR + 4], table_ref[FACE : FACE + 4], w_ref, y_ref, 7)

    def body(lanes):
        acc = star_sum(y_ref, [ms_ref, ml_ref, mn_ref], lanes, [start(p, lanes) for p in range(NQ)])
        for p in range(NQ):
            out_ref[p, :, lanes] = acc[p]

    each_half(elements, body)


def padded(ref, p, lanes):
    return jnp.concatenate([ref[p, :, lanes], jnp.zeros((R - NB, LANES), F32)], axis=0)


def local_kernel(
    dof_ref, b_ref, ms_ref, local_ref, neigh_ref,
    kstiff_ref, minus_ref, plus_ref, to_ref, from_ref, twice_ref, once_ref,
    index_ref, face_ref, cluster_ref, damage_ref, count_ref, cohesion_ref, yield_ref,
    out_ref, ml_ref, mn_ref, mask_ref, table_ref, weights_ref,
    w_ref, y_ref,
):
    fill_weights(w_ref, kstiff_ref, minus_ref, plus_ref, to_ref, from_ref)
    weights_ref[...] = place_weights(w_ref[...], twice_ref, once_ref)
    fill_table(table_ref, index_ref, face_ref, cluster_ref, damage_ref, count_ref, cohesion_ref, yield_ref)
    widen(local_ref, ml_ref)
    widen(neigh_ref, mn_ref)
    local_part(
        b_ref, weights_ref, table_ref, ms_ref, ml_ref, mn_ref, out_ref, y_ref, lambda p, lanes: padded(dof_ref, p, lanes)
    )
    elements = out_ref.shape[-1]
    rows = lax.broadcasted_iota(jnp.int32, (elements, elements), 0).astype(F32)
    listed = lax.dot_general(
        jnp.ones((8, elements), BF16),
        jnp.where(rows == table_ref[DAMAGE : DAMAGE + 1], 1.0, 0.0).astype(BF16),
        (((1,), (1,)), ((), ())),
        preferred_element_type=F32,
    )[0:1]
    mask_ref[...] = jnp.where(listed > 0.5, table_ref[YIELD : YIELD + R], 0.0)


def again_kernel(base_ref, b_ref, w_ref, table_ref, ms_ref, ml_ref, mn_ref, out_ref, y_ref):
    local_part(b_ref, w_ref, table_ref, ms_ref, ml_ref, mn_ref, out_ref, y_ref, lambda p, lanes: base_ref[p, :, lanes])


def ghost_source(near_ref, even_ref, odd_ref):
    me, total = lax.axis_index("dom"), lax.axis_size("dom")
    core = me % 2
    chip = (me // 2) % 2 == 0
    near, even, odd = near_ref[...], even_ref[...], odd_ref[...]
    up = jnp.where(chip, even, odd)
    down = jnp.where(chip, odd, even)
    half = near.shape[1] // 2
    side = lax.broadcasted_iota(jnp.int32, near.shape, 1) // half
    across = jnp.where(core == 0, down, up)
    one = jnp.where(side == core, across, near)
    two = jnp.where(side == 0, up, down)
    one = jnp.where(jnp.where(side == 0, me - 1, total - 2 - me) >= 0, one, 0.0)
    two = jnp.where(jnp.where(side == 0, total - 3 - me, me - 2) >= 0, two, 0.0)
    pad = jnp.zeros((R - NB, 2 * near.shape[1]), F32)
    both = jnp.concatenate([one, two], axis=1)
    return jnp.concatenate([piece for q in range(NQ) for piece in (both[q * NB : (q + 1) * NB], pad)], axis=0)


def gather_all(both, index):
    rows = lax.broadcasted_iota(jnp.int32, (both.shape[1], index.shape[1]), 0).astype(F32)
    gathered = []
    for f in range(4):
        hot = jnp.where(rows == index[f : f + 1], 1.0, 0.0).astype(BF16)
        gathered.append(dot(both, hot))
    return gathered


def ghost_index(table_ref, ghosts):
    index = table_ref[NEIGHBOUR : NEIGHBOUR + 4] - table_ref.shape[-1]
    last = jnp.where(index >= 3 * ghosts, index - ghosts, index + ghosts)
    return jnp.where(index >= 2 * ghosts, last, index)


def split_rows(source):
    high = source.astype(BF16)
    return jnp.concatenate([high, (source - high.astype(F32)).astype(BF16)], axis=0)


def second_kernel(
    v_ref, dof_ref, near_ref, even_ref, odd_ref, wk_ref, send_ref, w_ref, table_ref, ms_ref, mn_ref,
    state_ref, b_ref, near_out,
):
    both = split_rows(ghost_source(near_ref, even_ref, odd_ref))
    index = ghost_index(table_ref, near_ref.shape[-1] // 2)
    both = gather_all(both, index)
    wk = wk_ref[...]

    def half(at):
        lanes = pl.ds(at, LANES)
        ys = {}
        yield from far_steps(ys, [one[:, at : at + LANES] for one in both], index[:, at : at + LANES], table_ref[FACE : FACE + 4, lanes], w_ref)
        acc = [v_ref[p, :, lanes] for p in range(NQ)]
        yield from star_steps(acc, ys, mn_ref, lanes)
        fine = table_ref[CLUSTER : CLUSTER + 1, lanes] < 0.5
        x = []
        for p in range(NQ):
            state_ref[p, :, lanes] = acc[p]
            x.append(jnp.where(fine, acc[p], padded(dof_ref, p, lanes)))
        w1, w2 = jnp.where(fine, 0.5, 1.5), jnp.where(fine, 1.0 / 6.0, 7.0 / 6.0)
        yield from taylor_steps(x, wk, ms_ref, lanes, w1, w2, b_ref)

    in_turns(half(0), half(LANES), [4 + 4 * NQ, 4 * NQ] + [NQ, 3 * NQ] * 2)
    pick_columns(b_ref, send_ref[:, : send_ref.shape[-1] // 2], near_out)


def last_kernel(
    v_ref, near_ref, even_ref, odd_ref, w_ref, table_ref, mn_ref, mask_ref,
    result_ref,
    out_ref, sems,
):
    both = split_rows(ghost_source(near_ref, even_ref, odd_ref))
    index = ghost_index(table_ref, near_ref.shape[-1] // 2)
    both = gather_all(both, index)
    writes = []

    def send_out(quantities, lanes):
        write = pltpu.make_async_copy(
            out_ref.at[quantities, :, lanes], result_ref.at[quantities, :, lanes], sems.at[len(writes)]
        )
        write.start()
        writes.append(write)

    def half(at):
        lanes = pl.ds(at, LANES)
        ys = {}
        yield from far_steps(ys, [one[:, at : at + LANES] for one in both], index[:, at : at + LANES], table_ref[FACE : FACE + 4, lanes], w_ref)
        state = [v_ref[p, :, lanes] for p in range(NQ)]
        yield from star_steps(state, ys, mn_ref, lanes)
        for q in range(6, NQ):
            out_ref[q, :, lanes] = state[q][:NB]
        send_out(pl.ds(6, 3), lanes)
        points = []
        for q in range(6):
            points.append(dot(w_ref[W_POINTS : W_POINTS + R], stack_values(state[q])))
            yield
        pressure = (points[0] + points[1] + points[2]) / 3.0
        normal = [points[q] - pressure for q in range(3)]
        normal_sum = normal[0] * normal[0] + normal[1] * normal[1] + normal[2] * normal[2]
        shear_sum = points[3] * points[3] + points[4] * points[4] + points[5] * points[5]
        tau = jnp.sqrt(0.5 * normal_sum + shear_sum)
        strength = table_ref[COHESION : COHESION + 1, lanes]
        limit = jnp.maximum(strength - FRICTION * pressure, 0.5 * strength)
        yield
        rate = RELAXATION * (limit / jnp.maximum(tau, limit) - 1.0)
        rate = jnp.where(mask_ref[:, lanes] > 0.5, rate, 0.0)
        yield
        deviation = normal + points[3:]
        for q in range(6):
            change = dot(w_ref[W_POINTS + R : W_ROWS], stack_values(rate * deviation[q]))
            out_ref[q, :, lanes] = (state[q] + change)[:NB]
            yield
        send_out(pl.ds(0, 6), lanes)

    in_turns(half(0), half(LANES), [4 + 4 * NQ, 4 * NQ, 14])
    for write in writes:
        write.wait()


def spec(shape, dtype=F32):
    return jax.ShapeDtypeStruct(shape, dtype)


VMEM = pl.BlockSpec(memory_space=pltpu.VMEM)
HBM = pl.BlockSpec(memory_space=pltpu.HBM)


def call(kernel, inputs, outputs, scratch, cost=0, out_space=VMEM):
    return pl.pallas_call(
        kernel,
        out_shape=outputs,
        in_specs=[VMEM] * len(inputs),
        out_specs=jax.tree.map(lambda _: out_space, outputs),
        scratch_shapes=[pltpu.VMEM(*one) if isinstance(one, tuple) else one for one in scratch],
        compiler_params=pltpu.CompilerParams(vmem_limit_bytes=40 * 1024 * 1024),
        cost_estimate=pl.CostEstimate(flops=cost, bytes_accessed=1 << 20, transcendentals=0),
    )(*inputs)


def core_swap(total):
    return [(i, i ^ 1) for i in range(total)]


def even_chip_swap(total):
    return [(i, i ^ 2) for i in range(total)]


def odd_chip_swap(total):
    route = [(i, i) for i in (0, 1, total - 2, total - 1)]
    for i in range(2, total - 2, 4):
        for k in (i, i + 1):
            route += [(k, k + 2), (k + 2, k)]
    return route


def exchange(near, buffer, send, me, total):
    got = lax.ppermute(near, "dom", core_swap(total))
    far = call(far_kernel, [buffer, send], spec(near.shape), [], cost=500_000_000)
    left = lax.broadcasted_iota(jnp.int32, got.shape, 1) < got.shape[1] // 2
    forward = left == ((me // 2) % 2 == 0)
    to_even, to_odd = jnp.where(forward, got, far), jnp.where(forward, far, got)
    buffer, to_even, to_odd = lax.optimization_barrier((buffer, to_even, to_odd))
    even = lax.ppermute(to_even, "dom", even_chip_swap(total))
    odd = lax.ppermute(to_odd, "dom", odd_chip_swap(total))
    return got, even, odd, buffer


def per_device(
    dof_values,
    star_mats,
    flux_local,
    flux_neigh,
    kstiff,
    flux_minus,
    flux_plus,
    neighbour,
    neigh_face,
    cluster,
    send_list,
    damage_list,
    damage_count,
    yield_mask,
    cohesion,
    to_points,
    from_points,
):
    elements = dof_values.shape[-1]
    total = lax.axis_size("dom")
    me = lax.axis_index("dom")
    ghosts = send_list.shape[-1]

    field = spec((NQ, R, elements))
    block = spec((NQ * NB, 2 * ghosts))

    def y_s(blocks):
        return ((blocks, NQ, R, elements), F32)

    def m_o(blocks):
        return spec((NQ * NQ, blocks, elements))

    star = jnp.transpose(star_mats, (1, 2, 0, 3))
    own = jnp.transpose(flux_local, (1, 2, 0, 3))
    other = jnp.transpose(flux_neigh, (1, 2, 0, 3))
    minus = jnp.transpose(flux_minus, (1, 0, 2))
    plus = jnp.transpose(flux_plus, (0, 2, 1, 3))

    place = spec((LANES, K3), BF16)
    twice, once = call(place_kernel, [], (place, place), [], cost=4_000_000_000)
    wk, send = call(
        setup_kernel,
        [kstiff, send_list, twice, once],
        (spec((3 * R, K3), BF16), spec((1, 4 * ghosts))),
        [((3 * R, LANES), F32)],
    )
    buffer_one, near, ms = call(predict_kernel, [dof_values, star, wk, send], (field, block, m_o(3)), [])
    near, even, odd, buffer_one = exchange(near, buffer_one, send, me, total)
    started, ml, mn, mask, table, weights = call(
        local_kernel,
        [
            dof_values, buffer_one, ms, own, other,
            kstiff, minus, plus, to_points, from_points, twice, once,
            neighbour, neigh_face, cluster[None], damage_list, damage_count[None], cohesion[None], yield_mask,
        ],
        (field, m_o(4), m_o(4), spec((R, elements)), spec((ROWS, elements)), spec((W_ROWS, K3), BF16)),
        [((W_ROWS, LANES), F32), y_s(11)],
        cost=1_000_000_000,
    )
    updated, buffer_two, near = call(
        second_kernel,
        [started, dof_values, near, even, odd, wk, send, weights, table, ms, mn],
        (field, field, block),
        [],
    )
    near, even, odd, buffer_two = exchange(near, buffer_two, send, me, total)
    started = call(
        again_kernel,
        [updated, buffer_two, weights, table, ms, ml, mn],
        field,
        [y_s(11)],
        cost=1_000_000_000,
    )
    return call(
        last_kernel,
        [started, near, even, odd, weights, table, mn, mask],
        spec(dof_values.shape),
        [(dof_values.shape, F32), pltpu.SemaphoreType.DMA((4,))],
        out_space=HBM,
    )


def solution(mesh):
    return jax.shard_map(
        per_device,
        mesh=mesh,
        in_specs=(
            P(None, None, "dom"),
            P(None, None, None, "dom"),
            P(None, None, None, "dom"),
            P(None, None, None, "dom"),
            P(),
            P(),
            P(),
            P(None, "dom"),
            P(None, "dom"),
            P("dom"),
            P("dom", None, None),
            P("dom", None),
            P("dom"),
            P(None, "dom"),
            P("dom"),
            P(),
            P(),
        ),
        out_specs=P(None, None, "dom"),
        check_vma=False,
    )
```

```python
import jax
import jax.numpy as jnp
from jax import lax
from jax.experimental import pallas as pl
from jax.experimental.pallas import tpu as pltpu
from jax.sharding import PartitionSpec as P

NQ = 9
NB = 20
R = 24
K3 = 3 * R
LANES = 128
FRICTION = 0.6
RELAXATION = 0.5
F32 = jnp.float32
BF16 = jnp.bfloat16


def stack_values(x):
    high = x.astype(BF16).astype(F32)
    return jnp.concatenate([high, x - high, high], axis=0).astype(BF16)


def dot(a, b):
    return jnp.dot(a, b, preferred_element_type=F32)


def widen(src_ref, dst_ref):
    for q in range(NQ):
        for p in range(NQ):
            dst_ref[q * NQ + p] = src_ref[q, p].astype(F32)


def basis_products(weights, x_ref, y_ref, blocks, base=0):
    for q in range(NQ):
        out = dot(weights, stack_values(x_ref[q]))
        for k in range(blocks):
            y_ref[base + k, q] = out[k * R : (k + 1) * R]


def star_sum(y_ref, m_refs, lanes, start):
    acc = list(start)
    for q in range(NQ):
        k = 0
        for m_ref in m_refs:
            for row in range(m_ref.shape[1]):
                y = y_ref[k, q, :, lanes]
                for p in range(NQ):
                    acc[p] = acc[p] + y * m_ref[q * NQ + p, row : row + 1, lanes]
                k += 1
    return acc


def each_half(elements, body):
    for start in range(0, elements, LANES):
        body(pl.ds(start, LANES))


def in_turns(one, two, stages):
    for now, before in zip(stages + [[]], [[]] + stages):
        order = []
        for steps, weights in ((one, now), (two, before)):
            done = 0
            for weight in weights:
                order.append((done / sum(weights), steps))
                done += weight
        for _, steps in sorted(order, key=lambda entry: entry[0]):
            next(steps, None)
    next(one, None)
    next(two, None)


FAR = [0.01] * 4 + [1] * 4 * NQ


def star_steps(acc, ys, m_ref, lanes):
    for q in range(NQ):
        for k in range(m_ref.shape[1]):
            y = ys.pop((k, q))
            for p in range(NQ):
                acc[p] = acc[p] + y * m_ref[q * NQ + p, k : k + 1, lanes]
            yield


def far_steps(ys, both, index, face, w_ref):
    size = NQ * R
    gathered = both
    for f in range(4):
        yield
    for q in range(NQ):
        for f in range(4):
            kind = jnp.broadcast_to(face[f : f + 1], (R, LANES))
            w = w_ref[W_FAR + 4 * f * R : W_FAR + 4 * (f + 1) * R]
            high_rows = gathered[f][q * R : (q + 1) * R]
            low_rows = gathered[f][size + q * R : size + (q + 1) * R]
            out = dot(w, jnp.concatenate([high_rows, low_rows, high_rows], axis=0).astype(BF16))
            ys[f, q] = jnp.where(
                kind < 2,
                jnp.where(kind == 0, out[:R], out[R : 2 * R]),
                jnp.where(kind == 2, out[2 * R : 3 * R], out[3 * R :]),
            )
            yield


def derivative_steps(x, following, wk, m_ref, lanes):
    ys = {}
    for q in range(NQ):
        out = dot(wk, stack_values(x[q]))
        for k in range(3):
            ys[k, q] = out[k * R : (k + 1) * R]
        yield
    yield from star_steps(following, ys, m_ref, lanes)


def taylor_steps(x, wk, m_ref, lanes, w1, w2, out_ref):
    first = [jnp.zeros((R, LANES), F32)] * NQ
    yield from derivative_steps(x, first, wk, m_ref, lanes)
    second = [jnp.zeros((R, LANES), F32)] * NQ
    yield from derivative_steps(first, second, wk, m_ref, lanes)
    for p in range(NQ):
        out_ref[p, :, lanes] = x[p] + (w1 * first[p] + w2 * second[p])


def pick_columns(b_ref, send, out_ref):
    elements = b_ref.shape[-1]
    both = split_rows(b_ref[...].reshape(NQ * R, elements))
    rows = lax.broadcasted_iota(jnp.int32, (elements, send.shape[-1]), 0).astype(F32)
    hot = jnp.where(rows == send, 1.0, 0.0).astype(BF16)
    out = dot(both, hot)
    out = out[: NQ * R] + out[NQ * R :]
    for q in range(NQ):
        out_ref[q * NB : (q + 1) * NB] = out[q * R : q * R + NB]


def far_sides(source, index, face, w_ref, y_ref, base):
    high = source.astype(BF16)
    low = (source - high.astype(F32)).astype(BF16)
    both = jnp.concatenate([high, low], axis=0)
    elements = index.shape[-1]
    rows = lax.broadcasted_iota(jnp.int32, (source.shape[-1], elements), 0).astype(F32)
    size = NQ * R
    gathered = []
    for f in range(4):
        hot = jnp.where(rows == index[f : f + 1], 1.0, 0.0).astype(BF16)
        gathered.append(dot(both, hot))
    for f, picked in enumerate(gathered):
        kind = jnp.broadcast_to(face[f : f + 1], (R, elements))
        w = w_ref[W_FAR + 4 * f * R : W_FAR + 4 * (f + 1) * R]
        for q in range(NQ):
            high_rows = picked[q * R : (q + 1) * R]
            low_rows = picked[size + q * R : size + (q + 1) * R]
            out = dot(w, jnp.concatenate([high_rows, low_rows, high_rows], axis=0).astype(BF16))
            y_ref[base + f, q] = jnp.where(
                kind < 2,
                jnp.where(kind == 0, out[:R], out[R : 2 * R]),
                jnp.where(kind == 2, out[2 * R : 3 * R], out[3 * R :]),
            )


def place_kernel(twice_ref, once_ref):
    row = lax.broadcasted_iota(jnp.int32, twice_ref.shape, 0)
    column = lax.broadcasted_iota(jnp.int32, twice_ref.shape, 1)
    twice_ref[...] = jnp.where((column == row) | (column == row + R), 1.0, 0.0).astype(BF16)
    once_ref[...] = jnp.where(column == row + 2 * R, 1.0, 0.0).astype(BF16)


def place_weights(w, twice_ref, once_ref):
    high = w.astype(BF16)
    low = (w - high.astype(F32)).astype(BF16)
    return (dot(high, twice_ref[...]) + dot(low, once_ref[...])).astype(BF16)


W_OWN, W_FAR, W_POINTS, W_ROWS = 0, 7 * R, 23 * R, 25 * R


def fill_stiffness(w_ref, kstiff_ref):
    w_ref[...] = jnp.zeros(w_ref.shape, F32)
    for d in range(3):
        w_ref[d * R : d * R + NB, :NB] = kstiff_ref[d]


def fill_weights(w_ref, kstiff_ref, minus_ref, plus_ref, to_ref, from_ref):
    fill_stiffness(w_ref, kstiff_ref)
    row = lax.broadcasted_iota(jnp.int32, (R, LANES), 0)
    column = lax.broadcasted_iota(jnp.int32, (R, LANES), 1)
    same = jnp.where(row == column, 1.0, 0.0).astype(BF16)
    stiff = w_ref[: 3 * R]
    high = stiff.astype(BF16)
    low = (stiff - high.astype(F32)).astype(BF16)
    turned = [
        lax.dot_general(same, part, (((1,), (1,)), ((), ())), preferred_element_type=F32) for part in (high, low)
    ]
    turned = turned[0] + turned[1]
    for d in range(3):
        w_ref[W_OWN + d * R : W_OWN + (d + 1) * R, :R] = turned[:, d * R : (d + 1) * R]
    for f in range(4):
        start = W_OWN + (3 + f) * R
        w_ref[start : start + NB, :NB] = -minus_ref[:, f, :]
        for h in range(4):
            start = W_FAR + (4 * f + h) * R
            w_ref[start : start + NB, :NB] = -plus_ref[f, :, h, :]
    w_ref[W_POINTS : W_POINTS + NB, :NB] = to_ref[...]
    w_ref[W_POINTS + R : W_POINTS + R + NB, :NB] = from_ref[...]


def send_columns(send_ref):
    slots, ghosts = send_ref.shape
    width = slots * ghosts
    row = lax.broadcasted_iota(jnp.int32, (ghosts, width), 0)
    column = lax.broadcasted_iota(jnp.int32, (ghosts, width), 1)
    repeat = jnp.where(column % ghosts == row, 1.0, 0.0).astype(BF16)
    wide = dot(send_ref[...].astype(F32).astype(BF16), repeat)
    slot = lax.broadcasted_iota(jnp.int32, (1, width), 1) // ghosts
    first = jnp.where(slot == 0, wide[0:1], wide[1:2])
    second = jnp.where(slot == 2, wide[3:4], wide[2:3])
    return jnp.where(slot < 2, first, second)


def setup_kernel(kstiff_ref, send_ref, twice_ref, once_ref, wk_ref, send_out, w_ref):
    fill_stiffness(w_ref, kstiff_ref)
    wk_ref[...] = place_weights(w_ref[...], twice_ref, once_ref)
    send_out[...] = send_columns(send_ref.at[0])


def far_kernel(b_ref, send_ref, near_ref, far_ref, even_ref, flag_ref):
    pick_columns(b_ref, send_ref[:, send_ref.shape[-1] // 2 :], far_ref)
    chip = (lax.axis_index("dom") // 2) % 2
    half = near_ref.shape[1] // 2
    side = lax.broadcasted_iota(jnp.int32, near_ref.shape, 1) // half
    even_ref[...] = jnp.where(side == chip, near_ref[...], far_ref[...])
    lane = lax.broadcasted_iota(jnp.int32, flag_ref.shape, 1) // half
    flag_ref[...] = jnp.where(lane == chip, 1.0, 0.0)


def predict_kernel(dof_ref, star_ref, wk_ref, send_ref, b_ref, near_ref, m_ref):
    widen(star_ref, m_ref)
    wk = wk_ref[...]

    def half(lanes):
        x = [padded(dof_ref, p, lanes) for p in range(NQ)]
        yield from taylor_steps(x, wk, m_ref, lanes, 0.5, 1.0 / 6.0, b_ref)

    in_turns(half(pl.ds(0, LANES)), half(pl.ds(LANES, LANES)), [[1] * NQ, [1] * 3 * NQ] * 2)
    pick_columns(b_ref, send_ref[:, : send_ref.shape[-1] // 2], near_ref)


NEIGHBOUR, FACE, CLUSTER, DAMAGE, COHESION, YIELD = 0, 4, 8, 9, 10, 16
ROWS = 40


def fill_table(table_ref, index_ref, face_ref, cluster_ref, damage_ref, count_ref, cohesion_ref, yield_ref):
    elements = table_ref.shape[-1]
    table_ref[...] = jnp.zeros(table_ref.shape, F32)
    table_ref[NEIGHBOUR : NEIGHBOUR + 4, :] = index_ref[...].astype(F32)
    table_ref[FACE : FACE + 4, :] = face_ref[...].astype(F32)
    table_ref[CLUSTER : CLUSTER + 1, :] = cluster_ref[...].astype(F32)
    slot = lax.broadcasted_iota(jnp.int32, (1, elements), 1)
    count = jnp.broadcast_to(count_ref[...], (1, elements))
    table_ref[DAMAGE : DAMAGE + 1, :] = jnp.where(slot < count, damage_ref[...], -1).astype(F32)
    table_ref[COHESION : COHESION + 1, :] = cohesion_ref[...]
    table_ref[YIELD : YIELD + NB, :] = yield_ref[...].astype(F32)


def local_part(b_ref, w_ref, table_ref, ms_ref, ml_ref, mn_ref, out_ref, y_ref, start):
    elements = b_ref.shape[-1]
    basis_products(w_ref[W_OWN:W_FAR], b_ref, y_ref, 7)
    source = b_ref[...].reshape(NQ * R, elements)
    far_sides(source, table_ref[NEIGHBOUR : NEIGHBOUR + 4], table_ref[FACE : FACE + 4], w_ref, y_ref, 7)

    def body(lanes):
        acc = star_sum(y_ref, [ms_ref, ml_ref, mn_ref], lanes, [start(p, lanes) for p in range(NQ)])
        for p in range(NQ):
            out_ref[p, :, lanes] = acc[p]

    each_half(elements, body)


def padded(ref, p, lanes):
    return jnp.concatenate([ref[p, :, lanes], jnp.zeros((R - NB, LANES), F32)], axis=0)


def local_kernel(
    dof_ref, b_ref, ms_ref, local_ref, neigh_ref,
    kstiff_ref, minus_ref, plus_ref, to_ref, from_ref, twice_ref, once_ref,
    index_ref, face_ref, cluster_ref, damage_ref, count_ref, cohesion_ref, yield_ref,
    out_ref, ml_ref, mn_ref, mask_ref, table_ref, weights_ref,
    w_ref, y_ref,
):
    fill_weights(w_ref, kstiff_ref, minus_ref, plus_ref, to_ref, from_ref)
    weights_ref[...] = place_weights(w_ref[...], twice_ref, once_ref)
    fill_table(table_ref, index_ref, face_ref, cluster_ref, damage_ref, count_ref, cohesion_ref, yield_ref)
    widen(local_ref, ml_ref)
    widen(neigh_ref, mn_ref)
    local_part(
        b_ref, weights_ref, table_ref, ms_ref, ml_ref, mn_ref, out_ref, y_ref, lambda p, lanes: padded(dof_ref, p, lanes)
    )
    elements = out_ref.shape[-1]
    rows = lax.broadcasted_iota(jnp.int32, (elements, elements), 0).astype(F32)
    listed = lax.dot_general(
        jnp.ones((8, elements), BF16),
        jnp.where(rows == table_ref[DAMAGE : DAMAGE + 1], 1.0, 0.0).astype(BF16),
        (((1,), (1,)), ((), ())),
        preferred_element_type=F32,
    )[0:1]
    mask_ref[...] = jnp.where(listed > 0.5, table_ref[YIELD : YIELD + R], 0.0)


def again_kernel(base_ref, b_ref, w_ref, table_ref, ms_ref, ml_ref, mn_ref, out_ref, y_ref):
    local_part(b_ref, w_ref, table_ref, ms_ref, ml_ref, mn_ref, out_ref, y_ref, lambda p, lanes: base_ref[p, :, lanes])


def ghost_source(near_ref, even_ref, odd_ref, cross_ref):
    me, total = lax.axis_index("dom"), lax.axis_size("dom")
    core = me % 2
    chip = (me // 2) % 2 == 0
    near, even, odd = near_ref[...], even_ref[...], odd_ref[...]
    up = jnp.where(chip, even, odd)
    down = jnp.where(chip, odd, even)
    half = near.shape[1] // 2
    side = lax.broadcasted_iota(jnp.int32, near.shape, 1) // half
    across = jnp.where((me // 2) % 2 == core, odd, cross_ref[...])
    one = jnp.where(side == core, across, near)
    two = jnp.where(side == 0, up, down)
    one = jnp.where(jnp.where(side == 0, me - 1, total - 2 - me) >= 0, one, 0.0)
    two = jnp.where(jnp.where(side == 0, total - 3 - me, me - 2) >= 0, two, 0.0)
    pad = jnp.zeros((R - NB, 2 * near.shape[1]), F32)
    both = jnp.concatenate([one, two], axis=1)
    return jnp.concatenate([piece for q in range(NQ) for piece in (both[q * NB : (q + 1) * NB], pad)], axis=0)


def gather_all(both, index):
    rows = lax.broadcasted_iota(jnp.int32, (both.shape[1], index.shape[1]), 0).astype(F32)
    gathered = []
    for f in range(4):
        hot = jnp.where(rows == index[f : f + 1], 1.0, 0.0).astype(BF16)
        gathered.append(dot(both, hot))
    return gathered


def ghost_index(table_ref, ghosts):
    index = table_ref[NEIGHBOUR : NEIGHBOUR + 4] - table_ref.shape[-1]
    last = jnp.where(index >= 3 * ghosts, index - ghosts, index + ghosts)
    return jnp.where(index >= 2 * ghosts, last, index)


def split_rows(source):
    high = source.astype(BF16)
    return jnp.concatenate([high, (source - high.astype(F32)).astype(BF16)], axis=0)


def second_kernel(
    v_ref, dof_ref, near_ref, even_ref, odd_ref, cross_ref, wk_ref, send_ref, w_ref, table_ref, ms_ref, mn_ref,
    state_ref, b_ref, near_out,
):
    both = split_rows(ghost_source(near_ref, even_ref, odd_ref, cross_ref))
    index = ghost_index(table_ref, near_ref.shape[-1] // 2)
    both = gather_all(both, index)
    wk = wk_ref[...]

    def half(at):
        lanes = pl.ds(at, LANES)
        ys = {}
        yield from far_steps(ys, [one[:, at : at + LANES] for one in both], index[:, at : at + LANES], table_ref[FACE : FACE + 4, lanes], w_ref)
        acc = [v_ref[p, :, lanes] for p in range(NQ)]
        yield from star_steps(acc, ys, mn_ref, lanes)
        fine = table_ref[CLUSTER : CLUSTER + 1, lanes] < 0.5
        x = []
        for p in range(NQ):
            state_ref[p, :, lanes] = acc[p]
            x.append(jnp.where(fine, acc[p], padded(dof_ref, p, lanes)))
        w1, w2 = jnp.where(fine, 0.5, 1.5), jnp.where(fine, 1.0 / 6.0, 7.0 / 6.0)
        yield from taylor_steps(x, wk, ms_ref, lanes, w1, w2, b_ref)

    in_turns(half(0), half(LANES), [FAR, [1] * 4 * NQ] + [[1] * NQ, [1] * 3 * NQ] * 2)
    pick_columns(b_ref, send_ref[:, : send_ref.shape[-1] // 2], near_out)


def last_kernel(
    v_ref, near_ref, even_ref, odd_ref, cross_ref, w_ref, table_ref, mn_ref, mask_ref,
    result_ref,
    out_ref, sems,
):
    both = split_rows(ghost_source(near_ref, even_ref, odd_ref, cross_ref))
    index = ghost_index(table_ref, near_ref.shape[-1] // 2)
    both = gather_all(both, index)
    writes = []

    def send_out(quantities, lanes):
        write = pltpu.make_async_copy(
            out_ref.at[quantities, :, lanes], result_ref.at[quantities, :, lanes], sems.at[len(writes)]
        )
        write.start()
        writes.append(write)

    def half(at):
        lanes = pl.ds(at, LANES)
        ys = {}
        yield from far_steps(ys, [one[:, at : at + LANES] for one in both], index[:, at : at + LANES], table_ref[FACE : FACE + 4, lanes], w_ref)
        state = [v_ref[p, :, lanes] for p in range(NQ)]
        yield from star_steps(state, ys, mn_ref, lanes)
        for q in range(6, NQ):
            out_ref[q, :, lanes] = state[q][:NB]
        send_out(pl.ds(6, 3), lanes)
        points = []
        for q in range(6):
            points.append(dot(w_ref[W_POINTS : W_POINTS + R], stack_values(state[q])))
            yield
        pressure = (points[0] + points[1] + points[2]) / 3.0
        normal = [points[q] - pressure for q in range(3)]
        normal_sum = normal[0] * normal[0] + normal[1] * normal[1] + normal[2] * normal[2]
        shear_sum = points[3] * points[3] + points[4] * points[4] + points[5] * points[5]
        tau = jnp.sqrt(0.5 * normal_sum + shear_sum)
        strength = table_ref[COHESION : COHESION + 1, lanes]
        limit = jnp.maximum(strength - FRICTION * pressure, 0.5 * strength)
        yield
        rate = RELAXATION * (limit / jnp.maximum(tau, limit) - 1.0)
        rate = jnp.where(mask_ref[:, lanes] > 0.5, rate, 0.0)
        yield
        deviation = normal + points[3:]
        for q in range(6):
            change = dot(w_ref[W_POINTS + R : W_ROWS], stack_values(rate * deviation[q]))
            out_ref[q, :, lanes] = (state[q] + change)[:NB]
            yield
        send_out(pl.ds(0, 6), lanes)

    in_turns(half(0), half(LANES), [FAR, [1] * 4 * NQ, [1] * 14])
    for write in writes:
        write.wait()


def spec(shape, dtype=F32):
    return jax.ShapeDtypeStruct(shape, dtype)


VMEM = pl.BlockSpec(memory_space=pltpu.VMEM)
HBM = pl.BlockSpec(memory_space=pltpu.HBM)


def call(kernel, inputs, outputs, scratch, cost=0, out_space=VMEM):
    return pl.pallas_call(
        kernel,
        out_shape=outputs,
        in_specs=[VMEM] * len(inputs),
        out_specs=jax.tree.map(lambda _: out_space, outputs),
        scratch_shapes=[pltpu.VMEM(*one) if isinstance(one, tuple) else one for one in scratch],
        compiler_params=pltpu.CompilerParams(vmem_limit_bytes=40 * 1024 * 1024),
        cost_estimate=pl.CostEstimate(flops=cost, bytes_accessed=1 << 20, transcendentals=0),
    )(*inputs)


def core_swap(total):
    return [(i, i ^ 1) for i in range(total)]


def even_chip_swap(total):
    return [(i, i ^ 2) for i in range(total)]


def odd_chip_swap(total):
    route = [(i, i) for i in (0, 1, total - 2, total - 1)]
    for i in range(2, total - 2, 4):
        for k in (i, i + 1):
            route += [(k, k + 2), (k + 2, k)]
    return route


def exchange(near, buffer, send, total):
    got = lax.ppermute(near, "dom", core_swap(total))
    far, to_even, flag = call(
        far_kernel, [buffer, send, near], (spec(near.shape), spec(near.shape), spec((8, near.shape[1]))), [], cost=0
    )
    even = lax.ppermute(to_even, "dom", even_chip_swap(total))
    to_odd = jnp.where(flag[:1] > 0.5, far, got)
    odd = lax.ppermute(to_odd, "dom", odd_chip_swap(total))
    buffer, even, to_odd = lax.optimization_barrier((buffer, even, to_odd))
    cross = lax.ppermute(even, "dom", core_swap(total))
    return got, even, odd, cross, buffer


def per_device(
    dof_values,
    star_mats,
    flux_local,
    flux_neigh,
    kstiff,
    flux_minus,
    flux_plus,
    neighbour,
    neigh_face,
    cluster,
    send_list,
    damage_list,
    damage_count,
    yield_mask,
    cohesion,
    to_points,
    from_points,
):
    elements = dof_values.shape[-1]
    total = lax.axis_size("dom")
    ghosts = send_list.shape[-1]

    field = spec((NQ, R, elements))
    block = spec((NQ * NB, 2 * ghosts))

    def y_s(blocks):
        return ((blocks, NQ, R, elements), F32)

    def m_o(blocks):
        return spec((NQ * NQ, blocks, elements))

    star = jnp.transpose(star_mats, (1, 2, 0, 3))
    own = jnp.transpose(flux_local, (1, 2, 0, 3))
    other = jnp.transpose(flux_neigh, (1, 2, 0, 3))
    minus = jnp.transpose(flux_minus, (1, 0, 2))
    plus = jnp.transpose(flux_plus, (0, 2, 1, 3))

    place = spec((LANES, K3), BF16)
    twice, once = call(place_kernel, [], (place, place), [], cost=4_000_000_000)
    wk, send = call(
        setup_kernel,
        [kstiff, send_list, twice, once],
        (spec((3 * R, K3), BF16), spec((1, 4 * ghosts))),
        [((3 * R, LANES), F32)],
    )
    buffer_one, near, ms = call(predict_kernel, [dof_values, star, wk, send], (field, block, m_o(3)), [])
    near, even, odd, cross, buffer_one = exchange(near, buffer_one, send, total)
    started, ml, mn, mask, table, weights = call(
        local_kernel,
        [
            dof_values, buffer_one, ms, own, other,
            kstiff, minus, plus, to_points, from_points, twice, once,
            neighbour, neigh_face, cluster[None], damage_list, damage_count[None], cohesion[None], yield_mask,
        ],
        (field, m_o(4), m_o(4), spec((R, elements)), spec((ROWS, elements)), spec((W_ROWS, K3), BF16)),
        [((W_ROWS, LANES), F32), y_s(11)],
        cost=1_000_000_000,
    )
    updated, buffer_two, near = call(
        second_kernel,
        [started, dof_values, near, even, odd, cross, wk, send, weights, table, ms, mn],
        (field, field, block),
        [],
    )
    near, even, odd, cross, buffer_two = exchange(near, buffer_two, send, total)
    started = call(
        again_kernel,
        [updated, buffer_two, weights, table, ms, ml, mn],
        field,
        [y_s(11)],
        cost=1_000_000_000,
    )
    return call(
        last_kernel,
        [started, near, even, odd, cross, weights, table, mn, mask],
        spec(dof_values.shape),
        [(dof_values.shape, F32), pltpu.SemaphoreType.DMA((4,))],
        out_space=HBM,
    )


def solution(mesh):
    return jax.shard_map(
        per_device,
        mesh=mesh,
        in_specs=(
            P(None, None, "dom"),
            P(None, None, None, "dom"),
            P(None, None, None, "dom"),
            P(None, None, None, "dom"),
            P(),
            P(),
            P(),
            P(None, "dom"),
            P(None, "dom"),
            P("dom"),
            P("dom", None, None),
            P("dom", None),
            P("dom"),
            P(None, "dom"),
            P("dom"),
            P(),
            P(),
        ),
        out_specs=P(None, None, "dom"),
        check_vma=False,
    )
```

```python
import jax
import jax.numpy as jnp
from jax import lax
from jax.experimental import pallas as pl
from jax.experimental.pallas import tpu as pltpu
from jax.sharding import PartitionSpec as P

NQ = 9
NB = 20
R = 24
K3 = 3 * R
LANES = 128
FRICTION = 0.6
RELAXATION = 0.5
F32 = jnp.float32
BF16 = jnp.bfloat16


def stack_values(x):
    high = x.astype(BF16).astype(F32)
    return jnp.concatenate([high, x - high, high], axis=0).astype(BF16)


def dot(a, b):
    return jnp.dot(a, b, preferred_element_type=F32)


def widen(src_ref, dst_ref):
    for q in range(NQ):
        for p in range(NQ):
            dst_ref[q * NQ + p] = src_ref[q, p].astype(F32)


def basis_products(weights, x_ref, y_ref, blocks, base=0):
    for q in range(NQ):
        out = dot(weights, stack_values(x_ref[q]))
        for k in range(blocks):
            y_ref[base + k, q] = out[k * R : (k + 1) * R]


def star_sum(y_ref, m_refs, lanes, start):
    acc = list(start)
    for q in range(NQ):
        k = 0
        for m_ref in m_refs:
            for row in range(m_ref.shape[1]):
                y = y_ref[k, q, :, lanes]
                for p in range(NQ):
                    acc[p] = acc[p] + y * m_ref[q * NQ + p, row : row + 1, lanes]
                k += 1
    return acc


def each_half(elements, body):
    for start in range(0, elements, LANES):
        body(pl.ds(start, LANES))


def in_turns(one, two, stages):
    for now, before in zip(stages + [[]], [[]] + stages):
        order = []
        for steps, weights in ((one, now), (two, before)):
            done = 0
            for weight in weights:
                order.append((done / sum(weights), steps))
                done += weight
        for _, steps in sorted(order, key=lambda entry: entry[0]):
            next(steps, None)
    next(one, None)
    next(two, None)


FAR = [0.01] * 4 + [1] * 4 * NQ


def star_steps(acc, ys, m_ref, lanes):
    for q in range(NQ):
        for k in range(m_ref.shape[1]):
            y = ys.pop((k, q))
            for p in range(NQ):
                acc[p] = acc[p] + y * m_ref[q * NQ + p, k : k + 1, lanes]
            yield


def far_steps(ys, both, index, face, w_ref):
    size = NQ * R
    gathered = both
    for f in range(4):
        yield
    for q in range(NQ):
        for f in range(4):
            kind = jnp.broadcast_to(face[f : f + 1], (R, LANES))
            w = w_ref[W_FAR + 4 * f * R : W_FAR + 4 * (f + 1) * R]
            high_rows = gathered[f][q * R : (q + 1) * R]
            low_rows = gathered[f][size + q * R : size + (q + 1) * R]
            out = dot(w, jnp.concatenate([high_rows, low_rows, high_rows], axis=0).astype(BF16))
            ys[f, q] = jnp.where(
                kind < 2,
                jnp.where(kind == 0, out[:R], out[R : 2 * R]),
                jnp.where(kind == 2, out[2 * R : 3 * R], out[3 * R :]),
            )
            yield


def derivative_steps(x, following, wk, m_ref, lanes):
    ys = {}
    for q in range(NQ):
        out = dot(wk, stack_values(x[q]))
        for k in range(3):
            ys[k, q] = out[k * R : (k + 1) * R]
        yield
    yield from star_steps(following, ys, m_ref, lanes)


def taylor_steps(x, wk, m_ref, lanes, w1, w2, out_ref):
    first = [jnp.zeros((R, LANES), F32)] * NQ
    yield from derivative_steps(x, first, wk, m_ref, lanes)
    second = [jnp.zeros((R, LANES), F32)] * NQ
    yield from derivative_steps(first, second, wk, m_ref, lanes)
    for p in range(NQ):
        out_ref[p, :, lanes] = x[p] + (w1 * first[p] + w2 * second[p])


def pick_columns(b_ref, send, out_ref):
    elements = b_ref.shape[-1]
    both = split_rows(b_ref[...].reshape(NQ * R, elements))
    rows = lax.broadcasted_iota(jnp.int32, (elements, send.shape[-1]), 0).astype(F32)
    hot = jnp.where(rows == send, 1.0, 0.0).astype(BF16)
    out = dot(both, hot)
    out = out[: NQ * R] + out[NQ * R :]
    for q in range(NQ):
        out_ref[q * NB : (q + 1) * NB] = out[q * R : q * R + NB]


def far_sides(source, index, face, w_ref, y_ref, base):
    high = source.astype(BF16)
    low = (source - high.astype(F32)).astype(BF16)
    both = jnp.concatenate([high, low], axis=0)
    elements = index.shape[-1]
    rows = lax.broadcasted_iota(jnp.int32, (source.shape[-1], elements), 0).astype(F32)
    size = NQ * R
    gathered = []
    for f in range(4):
        hot = jnp.where(rows == index[f : f + 1], 1.0, 0.0).astype(BF16)
        gathered.append(dot(both, hot))
    for f, picked in enumerate(gathered):
        kind = jnp.broadcast_to(face[f : f + 1], (R, elements))
        w = w_ref[W_FAR + 4 * f * R : W_FAR + 4 * (f + 1) * R]
        for q in range(NQ):
            high_rows = picked[q * R : (q + 1) * R]
            low_rows = picked[size + q * R : size + (q + 1) * R]
            out = dot(w, jnp.concatenate([high_rows, low_rows, high_rows], axis=0).astype(BF16))
            y_ref[base + f, q] = jnp.where(
                kind < 2,
                jnp.where(kind == 0, out[:R], out[R : 2 * R]),
                jnp.where(kind == 2, out[2 * R : 3 * R], out[3 * R :]),
            )


def place_kernel(twice_ref, once_ref):
    row = lax.broadcasted_iota(jnp.int32, twice_ref.shape, 0)
    column = lax.broadcasted_iota(jnp.int32, twice_ref.shape, 1)
    twice_ref[...] = jnp.where((column == row) | (column == row + R), 1.0, 0.0).astype(BF16)
    once_ref[...] = jnp.where(column == row + 2 * R, 1.0, 0.0).astype(BF16)


def place_weights(w, twice_ref, once_ref):
    high = w.astype(BF16)
    low = (w - high.astype(F32)).astype(BF16)
    return (dot(high, twice_ref[...]) + dot(low, once_ref[...])).astype(BF16)


W_OWN, W_FAR, W_POINTS, W_ROWS = 0, 7 * R, 23 * R, 25 * R


def fill_stiffness(w_ref, kstiff_ref):
    w_ref[...] = jnp.zeros(w_ref.shape, F32)
    for d in range(3):
        w_ref[d * R : d * R + NB, :NB] = kstiff_ref[d]


def fill_weights(w_ref, kstiff_ref, minus_ref, plus_ref, to_ref, from_ref):
    fill_stiffness(w_ref, kstiff_ref)
    row = lax.broadcasted_iota(jnp.int32, (R, LANES), 0)
    column = lax.broadcasted_iota(jnp.int32, (R, LANES), 1)
    same = jnp.where(row == column, 1.0, 0.0).astype(BF16)
    stiff = w_ref[: 3 * R]
    high = stiff.astype(BF16)
    low = (stiff - high.astype(F32)).astype(BF16)
    turned = [
        lax.dot_general(same, part, (((1,), (1,)), ((), ())), preferred_element_type=F32) for part in (high, low)
    ]
    turned = turned[0] + turned[1]
    for d in range(3):
        w_ref[W_OWN + d * R : W_OWN + (d + 1) * R, :R] = turned[:, d * R : (d + 1) * R]
    for f in range(4):
        start = W_OWN + (3 + f) * R
        w_ref[start : start + NB, :NB] = -minus_ref[:, f, :]
        for h in range(4):
            start = W_FAR + (4 * f + h) * R
            w_ref[start : start + NB, :NB] = -plus_ref[f, :, h, :]
    w_ref[W_POINTS : W_POINTS + NB, :NB] = to_ref[...]
    w_ref[W_POINTS + R : W_POINTS + R + NB, :NB] = from_ref[...]


def send_columns(send_ref):
    slots, ghosts = send_ref.shape
    width = slots * ghosts
    row = lax.broadcasted_iota(jnp.int32, (ghosts, width), 0)
    column = lax.broadcasted_iota(jnp.int32, (ghosts, width), 1)
    repeat = jnp.where(column % ghosts == row, 1.0, 0.0).astype(BF16)
    wide = dot(send_ref[...].astype(F32).astype(BF16), repeat)
    slot = lax.broadcasted_iota(jnp.int32, (1, width), 1) // ghosts
    first = jnp.where(slot == 0, wide[0:1], wide[1:2])
    second = jnp.where(slot == 2, wide[3:4], wide[2:3])
    return jnp.where(slot < 2, first, second)


NEIGHBOUR, FACE, CLUSTER, COHESION, LIVE, YIELD = 0, 4, 8, 9, 10, 16
ROWS = 40


def setup_kernel(kstiff_ref, count_ref, twice_ref, once_ref, wk_ref, count_out, w_ref):
    fill_stiffness(w_ref, kstiff_ref)
    wk_ref[...] = place_weights(w_ref[...], twice_ref, once_ref)
    count_out[...] = jnp.broadcast_to(count_ref[...], count_out.shape).astype(F32)


def near_kernel(b_ref, lists_ref, near_ref, send_ref):
    send = send_columns(lists_ref.at[0])
    send_ref[...] = send
    pick_columns(b_ref, send[:, : send.shape[-1] // 2], near_ref)


def far_kernel(b_ref, send_ref, near_ref, far_ref, even_ref, flag_ref):
    pick_columns(b_ref, send_ref[:, send_ref.shape[-1] // 2 :], far_ref)
    chip = (lax.axis_index("dom") // 2) % 2
    half = near_ref.shape[1] // 2
    side = lax.broadcasted_iota(jnp.int32, near_ref.shape, 1) // half
    even_ref[...] = jnp.where(side == chip, near_ref[...], far_ref[...])
    lane = lax.broadcasted_iota(jnp.int32, flag_ref.shape, 1) // half
    flag_ref[...] = jnp.where(lane == chip, 1.0, 0.0)


def predict_kernel(dof_ref, star_ref, wk_ref, b_ref, m_ref):
    widen(star_ref, m_ref)
    wk = wk_ref[...]

    def half(lanes):
        x = [padded(dof_ref, p, lanes) for p in range(NQ)]
        yield from taylor_steps(x, wk, m_ref, lanes, 0.5, 1.0 / 6.0, b_ref)

    in_turns(half(pl.ds(0, LANES)), half(pl.ds(LANES, LANES)), [[1] * NQ, [1] * 3 * NQ] * 2)


def fill_table(table_ref, index_ref, face_ref, cluster_ref, cohesion_ref, damage_ref, count_ref, yield_ref):
    table_ref[...] = jnp.zeros(table_ref.shape, F32)
    table_ref[NEIGHBOUR : NEIGHBOUR + 4, :] = index_ref[...].astype(F32)
    table_ref[FACE : FACE + 4, :] = face_ref[...].astype(F32)
    table_ref[CLUSTER : CLUSTER + 1, :] = cluster_ref[...].astype(F32)
    table_ref[COHESION : COHESION + 1, :] = cohesion_ref[...]
    slot = lax.broadcasted_iota(jnp.int32, damage_ref.shape, 1).astype(F32)
    table_ref[LIVE : LIVE + 1, :] = jnp.where(slot < count_ref[...], damage_ref[...].astype(F32), -1.0)
    table_ref[YIELD : YIELD + NB, :] = yield_ref[...].astype(F32)


def local_part(b_ref, w_ref, table_ref, ms_ref, ml_ref, mn_ref, out_ref, y_ref, start):
    elements = b_ref.shape[-1]
    basis_products(w_ref[W_OWN:W_FAR], b_ref, y_ref, 7)
    source = b_ref[...].reshape(NQ * R, elements)
    far_sides(source, table_ref[NEIGHBOUR : NEIGHBOUR + 4], table_ref[FACE : FACE + 4], w_ref, y_ref, 7)

    def body(lanes):
        acc = star_sum(y_ref, [ms_ref, ml_ref, mn_ref], lanes, [start(p, lanes) for p in range(NQ)])
        for p in range(NQ):
            out_ref[p, :, lanes] = acc[p]

    each_half(elements, body)


def padded(ref, p, lanes):
    return jnp.concatenate([ref[p, :, lanes], jnp.zeros((R - NB, LANES), F32)], axis=0)


def local_kernel(
    dof_ref, b_ref, ms_ref, local_ref, neigh_ref,
    kstiff_ref, minus_ref, plus_ref, to_ref, from_ref, twice_ref, once_ref,
    index_ref, face_ref, cluster_ref, cohesion_ref, damage_ref, count_ref, yield_ref,
    out_ref, ml_ref, mn_ref, table_ref, weights_ref,
    w_ref, y_ref,
):
    fill_weights(w_ref, kstiff_ref, minus_ref, plus_ref, to_ref, from_ref)
    weights_ref[...] = place_weights(w_ref[...], twice_ref, once_ref)
    fill_table(table_ref, index_ref, face_ref, cluster_ref, cohesion_ref, damage_ref, count_ref, yield_ref)
    widen(local_ref, ml_ref)
    widen(neigh_ref, mn_ref)
    local_part(
        b_ref, weights_ref, table_ref, ms_ref, ml_ref, mn_ref, out_ref, y_ref, lambda p, lanes: padded(dof_ref, p, lanes)
    )


def again_kernel(
    base_ref, b_ref, w_ref, table_ref, ms_ref, ml_ref, mn_ref, out_ref, mask_ref, y_ref
):
    local_part(b_ref, w_ref, table_ref, ms_ref, ml_ref, mn_ref, out_ref, y_ref, lambda p, lanes: base_ref[p, :, lanes])
    elements = out_ref.shape[-1]
    rows = lax.broadcasted_iota(jnp.int32, (elements, elements), 0).astype(F32)
    listed = lax.dot_general(
        jnp.ones((8, elements), BF16),
        jnp.where(rows == table_ref[LIVE : LIVE + 1], 1.0, 0.0).astype(BF16),
        (((1,), (1,)), ((), ())),
        preferred_element_type=F32,
    )[0:1]
    mask_ref[...] = jnp.where(listed > 0.5, table_ref[YIELD : YIELD + R], 0.0)


def ghost_source(near_ref, even_ref, odd_ref, cross_ref):
    me, total = lax.axis_index("dom"), lax.axis_size("dom")
    core = me % 2
    chip = (me // 2) % 2 == 0
    near, even, odd = near_ref[...], even_ref[...], odd_ref[...]
    up = jnp.where(chip, even, odd)
    down = jnp.where(chip, odd, even)
    half = near.shape[1] // 2
    side = lax.broadcasted_iota(jnp.int32, near.shape, 1) // half
    across = jnp.where((me // 2) % 2 == core, odd, cross_ref[...])
    one = jnp.where(side == core, across, near)
    two = jnp.where(side == 0, up, down)
    one = jnp.where(jnp.where(side == 0, me - 1, total - 2 - me) >= 0, one, 0.0)
    two = jnp.where(jnp.where(side == 0, total - 3 - me, me - 2) >= 0, two, 0.0)
    pad = jnp.zeros((R - NB, 2 * near.shape[1]), F32)
    both = jnp.concatenate([one, two], axis=1)
    return jnp.concatenate([piece for q in range(NQ) for piece in (both[q * NB : (q + 1) * NB], pad)], axis=0)


def gather_all(both, index):
    rows = lax.broadcasted_iota(jnp.int32, (both.shape[1], index.shape[1]), 0).astype(F32)
    gathered = []
    for f in range(4):
        hot = jnp.where(rows == index[f : f + 1], 1.0, 0.0).astype(BF16)
        gathered.append(dot(both, hot))
    return gathered


def ghost_index(table_ref, ghosts):
    index = table_ref[NEIGHBOUR : NEIGHBOUR + 4] - table_ref.shape[-1]
    last = jnp.where(index >= 3 * ghosts, index - ghosts, index + ghosts)
    return jnp.where(index >= 2 * ghosts, last, index)


def split_rows(source):
    high = source.astype(BF16)
    return jnp.concatenate([high, (source - high.astype(F32)).astype(BF16)], axis=0)


def second_kernel(
    v_ref, dof_ref, near_ref, even_ref, odd_ref, cross_ref, wk_ref, send_ref, w_ref, table_ref, ms_ref, mn_ref,
    state_ref, b_ref, near_out,
):
    both = split_rows(ghost_source(near_ref, even_ref, odd_ref, cross_ref))
    index = ghost_index(table_ref, near_ref.shape[-1] // 2)
    both = gather_all(both, index)
    wk = wk_ref[...]

    def half(at):
        lanes = pl.ds(at, LANES)
        ys = {}
        yield from far_steps(ys, [one[:, at : at + LANES] for one in both], index[:, at : at + LANES], table_ref[FACE : FACE + 4, lanes], w_ref)
        acc = [v_ref[p, :, lanes] for p in range(NQ)]
        yield from star_steps(acc, ys, mn_ref, lanes)
        fine = table_ref[CLUSTER : CLUSTER + 1, lanes] < 0.5
        x = []
        for p in range(NQ):
            state_ref[p, :, lanes] = acc[p]
            x.append(jnp.where(fine, acc[p], padded(dof_ref, p, lanes)))
        w1, w2 = jnp.where(fine, 0.5, 1.5), jnp.where(fine, 1.0 / 6.0, 7.0 / 6.0)
        yield from taylor_steps(x, wk, ms_ref, lanes, w1, w2, b_ref)

    in_turns(half(0), half(LANES), [FAR, [1] * 4 * NQ] + [[1] * NQ, [1] * 3 * NQ] * 2)
    pick_columns(b_ref, send_ref[:, : send_ref.shape[-1] // 2], near_out)


def last_kernel(
    v_ref, near_ref, even_ref, odd_ref, cross_ref, w_ref, table_ref, mn_ref, mask_ref,
    result_ref,
    out_ref, sems,
):
    both = split_rows(ghost_source(near_ref, even_ref, odd_ref, cross_ref))
    index = ghost_index(table_ref, near_ref.shape[-1] // 2)
    both = gather_all(both, index)
    writes = []

    def send_out(quantities, lanes):
        write = pltpu.make_async_copy(
            out_ref.at[quantities, :, lanes], result_ref.at[quantities, :, lanes], sems.at[len(writes)]
        )
        write.start()
        writes.append(write)

    def half(at):
        lanes = pl.ds(at, LANES)
        ys = {}
        yield from far_steps(ys, [one[:, at : at + LANES] for one in both], index[:, at : at + LANES], table_ref[FACE : FACE + 4, lanes], w_ref)
        state = [v_ref[p, :, lanes] for p in range(NQ)]
        yield from star_steps(state, ys, mn_ref, lanes)
        for q in range(6, NQ):
            out_ref[q, :, lanes] = state[q][:NB]
        send_out(pl.ds(6, 3), lanes)
        points = []
        for q in range(6):
            points.append(dot(w_ref[W_POINTS : W_POINTS + R], stack_values(state[q])))
            yield
        pressure = (points[0] + points[1] + points[2]) / 3.0
        normal = [points[q] - pressure for q in range(3)]
        normal_sum = normal[0] * normal[0] + normal[1] * normal[1] + normal[2] * normal[2]
        shear_sum = points[3] * points[3] + points[4] * points[4] + points[5] * points[5]
        tau = jnp.sqrt(0.5 * normal_sum + shear_sum)
        strength = table_ref[COHESION : COHESION + 1, lanes]
        limit = jnp.maximum(strength - FRICTION * pressure, 0.5 * strength)
        yield
        rate = RELAXATION * (limit / jnp.maximum(tau, limit) - 1.0)
        rate = jnp.where(mask_ref[:, lanes] > 0.5, rate, 0.0)
        yield
        deviation = normal + points[3:]
        for q in range(6):
            change = dot(w_ref[W_POINTS + R : W_ROWS], stack_values(rate * deviation[q]))
            out_ref[q, :, lanes] = (state[q] + change)[:NB]
            yield
        send_out(pl.ds(0, 6), lanes)

    in_turns(half(0), half(LANES), [FAR, [1] * 4 * NQ, [1] * 14])
    for write in writes:
        write.wait()


def spec(shape, dtype=F32):
    return jax.ShapeDtypeStruct(shape, dtype)


VMEM = pl.BlockSpec(memory_space=pltpu.VMEM)
HBM = pl.BlockSpec(memory_space=pltpu.HBM)


def call(kernel, inputs, outputs, scratch, cost=0, out_space=VMEM):
    return pl.pallas_call(
        kernel,
        out_shape=outputs,
        in_specs=[VMEM] * len(inputs),
        out_specs=jax.tree.map(lambda _: out_space, outputs),
        scratch_shapes=[pltpu.VMEM(*one) if isinstance(one, tuple) else one for one in scratch],
        compiler_params=pltpu.CompilerParams(vmem_limit_bytes=40 * 1024 * 1024),
        cost_estimate=pl.CostEstimate(flops=cost, bytes_accessed=1 << 20, transcendentals=0),
    )(*inputs)


def core_swap(total):
    return [(i, i ^ 1) for i in range(total)]


def even_chip_swap(total):
    return [(i, i ^ 2) for i in range(total)]


def odd_chip_swap(total):
    route = [(i, i) for i in (0, 1, total - 2, total - 1)]
    for i in range(2, total - 2, 4):
        for k in (i, i + 1):
            route += [(k, k + 2), (k + 2, k)]
    return route


def exchange(near, buffer, send, total):
    got = lax.ppermute(near, "dom", core_swap(total))
    far, to_even, flag = call(
        far_kernel, [buffer, send, near], (spec(near.shape), spec(near.shape), spec((8, near.shape[1]))), [], cost=0
    )
    even = lax.ppermute(to_even, "dom", even_chip_swap(total))
    to_odd = jnp.where(flag[:1] > 0.5, far, got)
    odd = lax.ppermute(to_odd, "dom", odd_chip_swap(total))
    buffer, even, to_odd = lax.optimization_barrier((buffer, even, to_odd))
    cross = lax.ppermute(even, "dom", core_swap(total))
    return got, even, odd, cross, buffer


def per_device(
    dof_values,
    star_mats,
    flux_local,
    flux_neigh,
    kstiff,
    flux_minus,
    flux_plus,
    neighbour,
    neigh_face,
    cluster,
    send_list,
    damage_list,
    damage_count,
    yield_mask,
    cohesion,
    to_points,
    from_points,
):
    elements = dof_values.shape[-1]
    total = lax.axis_size("dom")
    ghosts = send_list.shape[-1]

    field = spec((NQ, R, elements))
    block = spec((NQ * NB, 2 * ghosts))

    def y_s(blocks):
        return ((blocks, NQ, R, elements), F32)

    def m_o(blocks):
        return spec((NQ * NQ, blocks, elements))

    star = jnp.transpose(star_mats, (1, 2, 0, 3))
    own = jnp.transpose(flux_local, (1, 2, 0, 3))
    other = jnp.transpose(flux_neigh, (1, 2, 0, 3))
    minus = jnp.transpose(flux_minus, (1, 0, 2))
    plus = jnp.transpose(flux_plus, (0, 2, 1, 3))

    place = spec((LANES, K3), BF16)
    twice, once = call(place_kernel, [], (place, place), [], cost=4_000_000_000)
    wk, count = call(
        setup_kernel,
        [kstiff, damage_count[None], twice, once],
        (spec((3 * R, K3), BF16), spec((1, elements))),
        [((3 * R, LANES), F32)],
    )
    buffer_one, ms = call(predict_kernel, [dof_values, star, wk], (field, m_o(3)), [])
    near, send = call(near_kernel, [buffer_one, send_list], (block, spec((1, 4 * ghosts))), [])
    near, even, odd, cross, buffer_one = exchange(near, buffer_one, send, total)
    started, ml, mn, table, weights = call(
        local_kernel,
        [
            dof_values, buffer_one, ms, own, other,
            kstiff, minus, plus, to_points, from_points, twice, once,
            neighbour, neigh_face, cluster[None], cohesion[None], damage_list, count, yield_mask,
        ],
        (field, m_o(4), m_o(4), spec((ROWS, elements)), spec((W_ROWS, K3), BF16)),
        [((W_ROWS, LANES), F32), y_s(11)],
        cost=1_000_000_000,
    )
    updated, buffer_two, near = call(
        second_kernel,
        [started, dof_values, near, even, odd, cross, wk, send, weights, table, ms, mn],
        (field, field, block),
        [],
    )
    near, even, odd, cross, buffer_two = exchange(near, buffer_two, send, total)
    started, mask = call(
        again_kernel,
        [updated, buffer_two, weights, table, ms, ml, mn],
        (field, spec((R, elements))),
        [y_s(11)],
        cost=1_000_000_000,
    )
    return call(
        last_kernel,
        [started, near, even, odd, cross, weights, table, mn, mask],
        spec(dof_values.shape),
        [(dof_values.shape, F32), pltpu.SemaphoreType.DMA((4,))],
        out_space=HBM,
    )


def solution(mesh):
    return jax.shard_map(
        per_device,
        mesh=mesh,
        in_specs=(
            P(None, None, "dom"),
            P(None, None, None, "dom"),
            P(None, None, None, "dom"),
            P(None, None, None, "dom"),
            P(),
            P(),
            P(),
            P(None, "dom"),
            P(None, "dom"),
            P("dom"),
            P("dom", None, None),
            P("dom", None),
            P("dom"),
            P(None, "dom"),
            P("dom"),
            P(),
            P(),
        ),
        out_specs=P(None, None, "dom"),
        check_vma=False,
    )
```

```python
import jax
import jax.numpy as jnp
from jax import lax
from jax.experimental import pallas as pl
from jax.experimental.pallas import tpu as pltpu
from jax.sharding import PartitionSpec as P

NQ = 9
NB = 20
R = 24
K3 = 3 * R
LANES = 128
FRICTION = 0.6
RELAXATION = 0.5
F32 = jnp.float32
BF16 = jnp.bfloat16


def stack_values(x):
    high = x.astype(BF16).astype(F32)
    return jnp.concatenate([high, x - high, high], axis=0).astype(BF16)


def dot(a, b):
    return jnp.dot(a, b, preferred_element_type=F32)


def widen(src_ref, dst_ref):
    for q in range(NQ):
        for p in range(NQ):
            dst_ref[q * NQ + p] = src_ref[q, p].astype(F32)


def basis_products(weights, x_ref, y_ref, blocks, base=0):
    for q in range(NQ):
        out = dot(weights, stack_values(x_ref[q]))
        for k in range(blocks):
            y_ref[base + k, q] = out[k * R : (k + 1) * R]


def star_sum(y_ref, m_refs, lanes, start):
    acc = list(start)
    for q in range(NQ):
        k = 0
        for m_ref in m_refs:
            for row in range(m_ref.shape[1]):
                y = y_ref[k, q, :, lanes]
                for p in range(NQ):
                    acc[p] = acc[p] + y * m_ref[q * NQ + p, row : row + 1, lanes]
                k += 1
    return acc


def each_half(elements, body):
    for start in range(0, elements, LANES):
        body(pl.ds(start, LANES))


def in_turns(one, two, stages):
    for now, before in zip(stages + [[]], [[]] + stages):
        order = []
        for steps, weights in ((one, now), (two, before)):
            done = 0
            for weight in weights:
                order.append((done / sum(weights), steps))
                done += weight
        for _, steps in sorted(order, key=lambda entry: entry[0]):
            next(steps, None)
    next(one, None)
    next(two, None)


FAR = [0.01] * 4 + [1] * 4 * NQ


def star_steps(acc, ys, m_ref, lanes):
    for q in range(NQ):
        for k in range(m_ref.shape[1]):
            y = ys.pop((k, q))
            for p in range(NQ):
                acc[p] = acc[p] + y * m_ref[q * NQ + p, k : k + 1, lanes]
            yield


def far_steps(ys, both, index, face, w_ref):
    size = NQ * R
    gathered = both
    for f in range(4):
        yield
    for q in range(NQ):
        for f in range(4):
            kind = jnp.broadcast_to(face[f : f + 1], (R, LANES))
            w = w_ref[W_FAR + 4 * f * R : W_FAR + 4 * (f + 1) * R]
            high_rows = gathered[f][q * R : (q + 1) * R]
            low_rows = gathered[f][size + q * R : size + (q + 1) * R]
            out = dot(w, jnp.concatenate([high_rows, low_rows, high_rows], axis=0).astype(BF16))
            ys[f, q] = jnp.where(
                kind < 2,
                jnp.where(kind == 0, out[:R], out[R : 2 * R]),
                jnp.where(kind == 2, out[2 * R : 3 * R], out[3 * R :]),
            )
            yield


def derivative_steps(x, following, wk, m_ref, lanes):
    ys = {}
    for q in range(NQ):
        out = dot(wk, stack_values(x[q]))
        for k in range(3):
            ys[k, q] = out[k * R : (k + 1) * R]
        yield
    yield from star_steps(following, ys, m_ref, lanes)


def taylor_steps(x, wk, m_ref, lanes, w1, w2, out_ref):
    first = [jnp.zeros((R, LANES), F32)] * NQ
    yield from derivative_steps(x, first, wk, m_ref, lanes)
    second = [jnp.zeros((R, LANES), F32)] * NQ
    yield from derivative_steps(first, second, wk, m_ref, lanes)
    for p in range(NQ):
        out_ref[p, :, lanes] = x[p] + (w1 * first[p] + w2 * second[p])


def pick_columns(b_ref, send, near_ref, far_ref):
    elements = b_ref.shape[-1]
    both = split_rows(b_ref[...].reshape(NQ * R, elements))
    rows = lax.broadcasted_iota(jnp.int32, (elements, send.shape[-1]), 0).astype(F32)
    hot = jnp.where(rows == send, 1.0, 0.0).astype(BF16)
    out = dot(both, hot)
    out = out[: NQ * R] + out[NQ * R :]
    half = send.shape[-1] // 2
    for q in range(NQ):
        near_ref[q * NB : (q + 1) * NB] = out[q * R : q * R + NB, :half]
        far_ref[q * NB : (q + 1) * NB] = out[q * R : q * R + NB, half:]


def far_sides(source, index, face, w_ref, y_ref, base):
    high = source.astype(BF16)
    low = (source - high.astype(F32)).astype(BF16)
    both = jnp.concatenate([high, low], axis=0)
    elements = index.shape[-1]
    rows = lax.broadcasted_iota(jnp.int32, (source.shape[-1], elements), 0).astype(F32)
    size = NQ * R
    gathered = []
    for f in range(4):
        hot = jnp.where(rows == index[f : f + 1], 1.0, 0.0).astype(BF16)
        gathered.append(dot(both, hot))
    for f, picked in enumerate(gathered):
        kind = jnp.broadcast_to(face[f : f + 1], (R, elements))
        w = w_ref[W_FAR + 4 * f * R : W_FAR + 4 * (f + 1) * R]
        for q in range(NQ):
            high_rows = picked[q * R : (q + 1) * R]
            low_rows = picked[size + q * R : size + (q + 1) * R]
            out = dot(w, jnp.concatenate([high_rows, low_rows, high_rows], axis=0).astype(BF16))
            y_ref[base + f, q] = jnp.where(
                kind < 2,
                jnp.where(kind == 0, out[:R], out[R : 2 * R]),
                jnp.where(kind == 2, out[2 * R : 3 * R], out[3 * R :]),
            )


def place_kernel(twice_ref, once_ref):
    row = lax.broadcasted_iota(jnp.int32, twice_ref.shape, 0)
    column = lax.broadcasted_iota(jnp.int32, twice_ref.shape, 1)
    twice_ref[...] = jnp.where((column == row) | (column == row + R), 1.0, 0.0).astype(BF16)
    once_ref[...] = jnp.where(column == row + 2 * R, 1.0, 0.0).astype(BF16)


def place_weights(w, twice_ref, once_ref):
    high = w.astype(BF16)
    low = (w - high.astype(F32)).astype(BF16)
    return (dot(high, twice_ref[...]) + dot(low, once_ref[...])).astype(BF16)


W_OWN, W_FAR, W_POINTS, W_ROWS = 0, 7 * R, 23 * R, 25 * R


def fill_stiffness(w_ref, kstiff_ref):
    w_ref[...] = jnp.zeros(w_ref.shape, F32)
    for d in range(3):
        w_ref[d * R : d * R + NB, :NB] = kstiff_ref[d]


def fill_weights(w_ref, kstiff_ref, minus_ref, plus_ref, to_ref, from_ref):
    fill_stiffness(w_ref, kstiff_ref)
    row = lax.broadcasted_iota(jnp.int32, (R, LANES), 0)
    column = lax.broadcasted_iota(jnp.int32, (R, LANES), 1)
    same = jnp.where(row == column, 1.0, 0.0).astype(BF16)
    stiff = w_ref[: 3 * R]
    high = stiff.astype(BF16)
    low = (stiff - high.astype(F32)).astype(BF16)
    turned = [
        lax.dot_general(same, part, (((1,), (1,)), ((), ())), preferred_element_type=F32) for part in (high, low)
    ]
    turned = turned[0] + turned[1]
    for d in range(3):
        w_ref[W_OWN + d * R : W_OWN + (d + 1) * R, :R] = turned[:, d * R : (d + 1) * R]
    for f in range(4):
        start = W_OWN + (3 + f) * R
        w_ref[start : start + NB, :NB] = -minus_ref[:, f, :]
        for h in range(4):
            start = W_FAR + (4 * f + h) * R
            w_ref[start : start + NB, :NB] = -plus_ref[f, :, h, :]
    w_ref[W_POINTS : W_POINTS + NB, :NB] = to_ref[...]
    w_ref[W_POINTS + R : W_POINTS + R + NB, :NB] = from_ref[...]


def send_columns(send_ref):
    slots, ghosts = send_ref.shape
    width = slots * ghosts
    row = lax.broadcasted_iota(jnp.int32, (ghosts, width), 0)
    column = lax.broadcasted_iota(jnp.int32, (ghosts, width), 1)
    repeat = jnp.where(column % ghosts == row, 1.0, 0.0).astype(BF16)
    wide = dot(send_ref[...].astype(F32).astype(BF16), repeat)
    slot = lax.broadcasted_iota(jnp.int32, (1, width), 1) // ghosts
    first = jnp.where(slot == 0, wide[0:1], wide[1:2])
    second = jnp.where(slot == 2, wide[3:4], wide[2:3])
    return jnp.where(slot < 2, first, second)


NEIGHBOUR, FACE, CLUSTER, COHESION, LIVE, YIELD = 0, 4, 8, 9, 10, 16
ROWS = 40


def setup_kernel(kstiff_ref, count_ref, twice_ref, once_ref, wk_ref, count_out, w_ref):
    fill_stiffness(w_ref, kstiff_ref)
    wk_ref[...] = place_weights(w_ref[...], twice_ref, once_ref)
    count_out[...] = jnp.broadcast_to(count_ref[...], count_out.shape).astype(F32)


def pick_kernel(b_ref, lists_ref, near_ref, far_ref, send_ref):
    send = send_columns(lists_ref.at[0])
    send_ref[...] = send
    pick_columns(b_ref, send, near_ref, far_ref)


def route_kernel(near_ref, far_ref, even_ref, flag_ref):
    chip = (lax.axis_index("dom") // 2) % 2
    half = near_ref.shape[1] // 2
    side = lax.broadcasted_iota(jnp.int32, near_ref.shape, 1) // half
    even_ref[...] = jnp.where(side == chip, near_ref[...], far_ref[...])
    lane = lax.broadcasted_iota(jnp.int32, flag_ref.shape, 1) // half
    flag_ref[...] = jnp.where(lane == chip, 1.0, 0.0)


def predict_kernel(dof_ref, star_ref, wk_ref, b_ref, m_ref):
    widen(star_ref, m_ref)
    wk = wk_ref[...]

    def half(lanes):
        x = [padded(dof_ref, p, lanes) for p in range(NQ)]
        yield from taylor_steps(x, wk, m_ref, lanes, 0.5, 1.0 / 6.0, b_ref)

    in_turns(half(pl.ds(0, LANES)), half(pl.ds(LANES, LANES)), [[1] * NQ, [1] * 3 * NQ] * 2)


def fill_table(table_ref, index_ref, face_ref, cluster_ref, cohesion_ref, damage_ref, count_ref, yield_ref):
    table_ref[...] = jnp.zeros(table_ref.shape, F32)
    table_ref[NEIGHBOUR : NEIGHBOUR + 4, :] = index_ref[...].astype(F32)
    table_ref[FACE : FACE + 4, :] = face_ref[...].astype(F32)
    table_ref[CLUSTER : CLUSTER + 1, :] = cluster_ref[...].astype(F32)
    table_ref[COHESION : COHESION + 1, :] = cohesion_ref[...]
    slot = lax.broadcasted_iota(jnp.int32, damage_ref.shape, 1).astype(F32)
    table_ref[LIVE : LIVE + 1, :] = jnp.where(slot < count_ref[...], damage_ref[...].astype(F32), -1.0)
    table_ref[YIELD : YIELD + NB, :] = yield_ref[...].astype(F32)


def local_part(b_ref, w_ref, table_ref, ms_ref, ml_ref, mn_ref, out_ref, y_ref, start):
    elements = b_ref.shape[-1]
    basis_products(w_ref[W_OWN:W_FAR], b_ref, y_ref, 7)
    source = b_ref[...].reshape(NQ * R, elements)
    far_sides(source, table_ref[NEIGHBOUR : NEIGHBOUR + 4], table_ref[FACE : FACE + 4], w_ref, y_ref, 7)

    def body(lanes):
        acc = star_sum(y_ref, [ms_ref, ml_ref, mn_ref], lanes, [start(p, lanes) for p in range(NQ)])
        for p in range(NQ):
            out_ref[p, :, lanes] = acc[p]

    each_half(elements, body)


def padded(ref, p, lanes):
    return jnp.concatenate([ref[p, :, lanes], jnp.zeros((R - NB, LANES), F32)], axis=0)


def local_kernel(
    dof_ref, b_ref, ms_ref, local_ref, neigh_ref,
    kstiff_ref, minus_ref, plus_ref, to_ref, from_ref, twice_ref, once_ref,
    index_ref, face_ref, cluster_ref, cohesion_ref, damage_ref, count_ref, yield_ref,
    out_ref, ml_ref, mn_ref, table_ref, weights_ref,
    w_ref, y_ref,
):
    fill_weights(w_ref, kstiff_ref, minus_ref, plus_ref, to_ref, from_ref)
    weights_ref[...] = place_weights(w_ref[...], twice_ref, once_ref)
    fill_table(table_ref, index_ref, face_ref, cluster_ref, cohesion_ref, damage_ref, count_ref, yield_ref)
    widen(local_ref, ml_ref)
    widen(neigh_ref, mn_ref)
    local_part(
        b_ref, weights_ref, table_ref, ms_ref, ml_ref, mn_ref, out_ref, y_ref, lambda p, lanes: padded(dof_ref, p, lanes)
    )


def again_kernel(
    base_ref, b_ref, w_ref, table_ref, ms_ref, ml_ref, mn_ref, out_ref, mask_ref, y_ref
):
    local_part(b_ref, w_ref, table_ref, ms_ref, ml_ref, mn_ref, out_ref, y_ref, lambda p, lanes: base_ref[p, :, lanes])
    elements = out_ref.shape[-1]
    rows = lax.broadcasted_iota(jnp.int32, (elements, elements), 0).astype(F32)
    listed = lax.dot_general(
        jnp.ones((8, elements), BF16),
        jnp.where(rows == table_ref[LIVE : LIVE + 1], 1.0, 0.0).astype(BF16),
        (((1,), (1,)), ((), ())),
        preferred_element_type=F32,
    )[0:1]
    mask_ref[...] = jnp.where(listed > 0.5, table_ref[YIELD : YIELD + R], 0.0)


def ghost_source(near_ref, even_ref, odd_ref, cross_ref):
    me, total = lax.axis_index("dom"), lax.axis_size("dom")
    core = me % 2
    chip = (me // 2) % 2 == 0
    near, even, odd = near_ref[...], even_ref[...], odd_ref[...]
    up = jnp.where(chip, even, odd)
    down = jnp.where(chip, odd, even)
    half = near.shape[1] // 2
    side = lax.broadcasted_iota(jnp.int32, near.shape, 1) // half
    across = jnp.where((me // 2) % 2 == core, odd, cross_ref[...])
    one = jnp.where(side == core, across, near)
    two = jnp.where(side == 0, up, down)
    one = jnp.where(jnp.where(side == 0, me - 1, total - 2 - me) >= 0, one, 0.0)
    two = jnp.where(jnp.where(side == 0, total - 3 - me, me - 2) >= 0, two, 0.0)
    pad = jnp.zeros((R - NB, 2 * near.shape[1]), F32)
    both = jnp.concatenate([one, two], axis=1)
    return jnp.concatenate([piece for q in range(NQ) for piece in (both[q * NB : (q + 1) * NB], pad)], axis=0)


def gather_all(both, index):
    rows = lax.broadcasted_iota(jnp.int32, (both.shape[1], index.shape[1]), 0).astype(F32)
    gathered = []
    for f in range(4):
        hot = jnp.where(rows == index[f : f + 1], 1.0, 0.0).astype(BF16)
        gathered.append(dot(both, hot))
    return gathered


def ghost_index(table_ref, ghosts):
    index = table_ref[NEIGHBOUR : NEIGHBOUR + 4] - table_ref.shape[-1]
    last = jnp.where(index >= 3 * ghosts, index - ghosts, index + ghosts)
    return jnp.where(index >= 2 * ghosts, last, index)


def split_rows(source):
    high = source.astype(BF16)
    return jnp.concatenate([high, (source - high.astype(F32)).astype(BF16)], axis=0)


def second_kernel(
    v_ref, dof_ref, near_ref, even_ref, odd_ref, cross_ref, wk_ref, send_ref, w_ref, table_ref, ms_ref, mn_ref,
    state_ref, b_ref, near_out, far_out,
):
    both = split_rows(ghost_source(near_ref, even_ref, odd_ref, cross_ref))
    index = ghost_index(table_ref, near_ref.shape[-1] // 2)
    both = gather_all(both, index)
    wk = wk_ref[...]

    def half(at):
        lanes = pl.ds(at, LANES)
        ys = {}
        yield from far_steps(ys, [one[:, at : at + LANES] for one in both], index[:, at : at + LANES], table_ref[FACE : FACE + 4, lanes], w_ref)
        acc = [v_ref[p, :, lanes] for p in range(NQ)]
        yield from star_steps(acc, ys, mn_ref, lanes)
        fine = table_ref[CLUSTER : CLUSTER + 1, lanes] < 0.5
        x = []
        for p in range(NQ):
            state_ref[p, :, lanes] = acc[p]
            x.append(jnp.where(fine, acc[p], padded(dof_ref, p, lanes)))
        w1, w2 = jnp.where(fine, 0.5, 1.5), jnp.where(fine, 1.0 / 6.0, 7.0 / 6.0)
        yield from taylor_steps(x, wk, ms_ref, lanes, w1, w2, b_ref)

    in_turns(half(0), half(LANES), [FAR, [1] * 4 * NQ] + [[1] * NQ, [1] * 3 * NQ] * 2)
    pick_columns(b_ref, send_ref[...], near_out, far_out)


def last_kernel(
    v_ref, near_ref, even_ref, odd_ref, cross_ref, w_ref, table_ref, mn_ref, mask_ref,
    result_ref,
    out_ref, sems,
):
    both = split_rows(ghost_source(near_ref, even_ref, odd_ref, cross_ref))
    index = ghost_index(table_ref, near_ref.shape[-1] // 2)
    both = gather_all(both, index)
    writes = []

    def send_out(quantities, lanes):
        write = pltpu.make_async_copy(
            out_ref.at[quantities, :, lanes], result_ref.at[quantities, :, lanes], sems.at[len(writes)]
        )
        write.start()
        writes.append(write)

    def half(at):
        lanes = pl.ds(at, LANES)
        ys = {}
        yield from far_steps(ys, [one[:, at : at + LANES] for one in both], index[:, at : at + LANES], table_ref[FACE : FACE + 4, lanes], w_ref)
        state = [v_ref[p, :, lanes] for p in range(NQ)]
        yield from star_steps(state, ys, mn_ref, lanes)
        for q in range(6, NQ):
            out_ref[q, :, lanes] = state[q][:NB]
        send_out(pl.ds(6, 3), lanes)
        points = []
        for q in range(6):
            points.append(dot(w_ref[W_POINTS : W_POINTS + R], stack_values(state[q])))
            yield
        pressure = (points[0] + points[1] + points[2]) / 3.0
        normal = [points[q] - pressure for q in range(3)]
        normal_sum = normal[0] * normal[0] + normal[1] * normal[1] + normal[2] * normal[2]
        shear_sum = points[3] * points[3] + points[4] * points[4] + points[5] * points[5]
        tau = jnp.sqrt(0.5 * normal_sum + shear_sum)
        strength = table_ref[COHESION : COHESION + 1, lanes]
        limit = jnp.maximum(strength - FRICTION * pressure, 0.5 * strength)
        yield
        rate = RELAXATION * (limit / jnp.maximum(tau, limit) - 1.0)
        rate = jnp.where(mask_ref[:, lanes] > 0.5, rate, 0.0)
        yield
        deviation = normal + points[3:]
        for q in range(6):
            change = dot(w_ref[W_POINTS + R : W_ROWS], stack_values(rate * deviation[q]))
            out_ref[q, :, lanes] = (state[q] + change)[:NB]
            yield
        send_out(pl.ds(0, 6), lanes)

    in_turns(half(0), half(LANES), [FAR, [1] * 4 * NQ, [1] * 14])
    for write in writes:
        write.wait()


def spec(shape, dtype=F32):
    return jax.ShapeDtypeStruct(shape, dtype)


VMEM = pl.BlockSpec(memory_space=pltpu.VMEM)
HBM = pl.BlockSpec(memory_space=pltpu.HBM)


def call(kernel, inputs, outputs, scratch, cost=0, out_space=VMEM):
    return pl.pallas_call(
        kernel,
        out_shape=outputs,
        in_specs=[VMEM] * len(inputs),
        out_specs=jax.tree.map(lambda _: out_space, outputs),
        scratch_shapes=[pltpu.VMEM(*one) if isinstance(one, tuple) else one for one in scratch],
        compiler_params=pltpu.CompilerParams(vmem_limit_bytes=40 * 1024 * 1024),
        cost_estimate=pl.CostEstimate(flops=cost, bytes_accessed=1 << 20, transcendentals=0),
    )(*inputs)


def core_swap(total):
    return [(i, i ^ 1) for i in range(total)]


def even_chip_swap(total):
    return [(i, i ^ 2) for i in range(total)]


def odd_chip_swap(total):
    route = [(i, i) for i in (0, 1, total - 2, total - 1)]
    for i in range(2, total - 2, 4):
        for k in (i, i + 1):
            route += [(k, k + 2), (k + 2, k)]
    return route


def exchange(near, far, buffer, total):
    got = lax.ppermute(near, "dom", core_swap(total))
    to_even, flag = call(route_kernel, [near, far], (spec(near.shape), spec((8, near.shape[1]))), [])
    even = lax.ppermute(to_even, "dom", even_chip_swap(total))
    to_odd = jnp.where(flag[:1] > 0.5, far, got)
    odd = lax.ppermute(to_odd, "dom", odd_chip_swap(total))
    buffer, even, to_odd = lax.optimization_barrier((buffer, even, to_odd))
    cross = lax.ppermute(even, "dom", core_swap(total))
    return got, even, odd, cross, buffer


def per_device(
    dof_values,
    star_mats,
    flux_local,
    flux_neigh,
    kstiff,
    flux_minus,
    flux_plus,
    neighbour,
    neigh_face,
    cluster,
    send_list,
    damage_list,
    damage_count,
    yield_mask,
    cohesion,
    to_points,
    from_points,
):
    elements = dof_values.shape[-1]
    total = lax.axis_size("dom")
    ghosts = send_list.shape[-1]

    field = spec((NQ, R, elements))
    block = spec((NQ * NB, 2 * ghosts))

    def y_s(blocks):
        return ((blocks, NQ, R, elements), F32)

    def m_o(blocks):
        return spec((NQ * NQ, blocks, elements))

    star = jnp.transpose(star_mats, (1, 2, 0, 3))
    own = jnp.transpose(flux_local, (1, 2, 0, 3))
    other = jnp.transpose(flux_neigh, (1, 2, 0, 3))
    minus = jnp.transpose(flux_minus, (1, 0, 2))
    plus = jnp.transpose(flux_plus, (0, 2, 1, 3))

    place = spec((LANES, K3), BF16)
    twice, once = call(place_kernel, [], (place, place), [], cost=4_000_000_000)
    wk, count = call(
        setup_kernel,
        [kstiff, damage_count[None], twice, once],
        (spec((3 * R, K3), BF16), spec((1, elements))),
        [((3 * R, LANES), F32)],
    )
    buffer_one, ms = call(predict_kernel, [dof_values, star, wk], (field, m_o(3)), [])
    near, far, send = call(pick_kernel, [buffer_one, send_list], (block, block, spec((1, 4 * ghosts))), [])
    near, even, odd, cross, buffer_one = exchange(near, far, buffer_one, total)
    started, ml, mn, table, weights = call(
        local_kernel,
        [
            dof_values, buffer_one, ms, own, other,
            kstiff, minus, plus, to_points, from_points, twice, once,
            neighbour, neigh_face, cluster[None], cohesion[None], damage_list, count, yield_mask,
        ],
        (field, m_o(4), m_o(4), spec((ROWS, elements)), spec((W_ROWS, K3), BF16)),
        [((W_ROWS, LANES), F32), y_s(11)],
        cost=1_000_000_000,
    )
    updated, buffer_two, near, far = call(
        second_kernel,
        [started, dof_values, near, even, odd, cross, wk, send, weights, table, ms, mn],
        (field, field, block, block),
        [],
    )
    near, even, odd, cross, buffer_two = exchange(near, far, buffer_two, total)
    started, mask = call(
        again_kernel,
        [updated, buffer_two, weights, table, ms, ml, mn],
        (field, spec((R, elements))),
        [y_s(11)],
        cost=1_000_000_000,
    )
    return call(
        last_kernel,
        [started, near, even, odd, cross, weights, table, mn, mask],
        spec(dof_values.shape),
        [(dof_values.shape, F32), pltpu.SemaphoreType.DMA((4,))],
        out_space=HBM,
    )


def solution(mesh):
    return jax.shard_map(
        per_device,
        mesh=mesh,
        in_specs=(
            P(None, None, "dom"),
            P(None, None, None, "dom"),
            P(None, None, None, "dom"),
            P(None, None, None, "dom"),
            P(),
            P(),
            P(),
            P(None, "dom"),
            P(None, "dom"),
            P("dom"),
            P("dom", None, None),
            P("dom", None),
            P("dom"),
            P(None, "dom"),
            P("dom"),
            P(),
            P(),
        ),
        out_specs=P(None, None, "dom"),
        check_vma=False,
    )
```

```python
import jax
import jax.numpy as jnp
from jax import lax
from jax.experimental import pallas as pl
from jax.experimental.pallas import tpu as pltpu
from jax.sharding import PartitionSpec as P

NQ = 9
NB = 20
R = 24
K3 = 3 * R
LANES = 128
FRICTION = 0.6
RELAXATION = 0.5
F32 = jnp.float32
BF16 = jnp.bfloat16


def stack_values(x):
    high = x.astype(BF16).astype(F32)
    return jnp.concatenate([high, x - high, high], axis=0).astype(BF16)


def dot(a, b):
    return jnp.dot(a, b, preferred_element_type=F32)


def widen(src_ref, dst_ref):
    for q in range(NQ):
        for p in range(NQ):
            dst_ref[q * NQ + p] = src_ref[q, p].astype(F32)


def basis_products(weights, x_ref, y_ref, blocks, base=0):
    for q in range(NQ):
        out = dot(weights, stack_values(x_ref[q]))
        for k in range(blocks):
            y_ref[base + k, q] = out[k * R : (k + 1) * R]


def star_add(acc, y_ref, k, m_ref, row, lanes):
    acc = list(acc)
    for q in range(NQ):
        y = y_ref[k, q, :, lanes]
        for p in range(NQ):
            acc[p] = acc[p] + y * m_ref[q * NQ + p, row : row + 1, lanes]
    return acc


def in_turns(one, two, stages):
    for now, before in zip(stages + [[]], [[]] + stages):
        order = []
        for steps, weights in ((one, now), (two, before)):
            done = 0
            for weight in weights:
                order.append((done / sum(weights), steps))
                done += weight
        for _, steps in sorted(order, key=lambda entry: entry[0]):
            next(steps, None)
    next(one, None)
    next(two, None)


FAR = [0.01] * 4 + [1] * 4 * NQ


def star_steps(acc, ys, m_ref, lanes):
    for q in range(NQ):
        for k in range(m_ref.shape[1]):
            y = ys.pop((k, q))
            for p in range(NQ):
                acc[p] = acc[p] + y * m_ref[q * NQ + p, k : k + 1, lanes]
            yield


def far_steps(ys, both, index, face, w_ref):
    size = NQ * R
    gathered = both
    for f in range(4):
        yield
    for q in range(NQ):
        for f in range(4):
            kind = jnp.broadcast_to(face[f : f + 1], (R, LANES))
            w = w_ref[W_FAR + 4 * f * R : W_FAR + 4 * (f + 1) * R]
            high_rows = gathered[f][q * R : (q + 1) * R]
            low_rows = gathered[f][size + q * R : size + (q + 1) * R]
            out = dot(w, jnp.concatenate([high_rows, low_rows, high_rows], axis=0).astype(BF16))
            ys[f, q] = jnp.where(
                kind < 2,
                jnp.where(kind == 0, out[:R], out[R : 2 * R]),
                jnp.where(kind == 2, out[2 * R : 3 * R], out[3 * R :]),
            )
            yield


def derivative_steps(x, following, wk, m_ref, lanes):
    ys = {}
    for q in range(NQ):
        out = dot(wk, stack_values(x[q]))
        for k in range(3):
            ys[k, q] = out[k * R : (k + 1) * R]
        yield
    yield from star_steps(following, ys, m_ref, lanes)


def taylor_steps(x, wk, m_ref, lanes, w1, w2, out_ref):
    first = [jnp.zeros((R, LANES), F32)] * NQ
    yield from derivative_steps(x, first, wk, m_ref, lanes)
    second = [jnp.zeros((R, LANES), F32)] * NQ
    yield from derivative_steps(first, second, wk, m_ref, lanes)
    for p in range(NQ):
        out_ref[p, :, lanes] = x[p] + (w1 * first[p] + w2 * second[p])


def pick_columns(b_ref, send, near_ref, far_ref):
    elements = b_ref.shape[-1]
    both = split_rows(b_ref[...].reshape(NQ * R, elements))
    rows = lax.broadcasted_iota(jnp.int32, (elements, send.shape[-1]), 0).astype(F32)
    hot = jnp.where(rows == send, 1.0, 0.0).astype(BF16)
    out = dot(both, hot)
    out = out[: NQ * R] + out[NQ * R :]
    half = send.shape[-1] // 2
    for q in range(NQ):
        near_ref[q * NB : (q + 1) * NB] = out[q * R : q * R + NB, :half]
        far_ref[q * NB : (q + 1) * NB] = out[q * R : q * R + NB, half:]


def far_sides(source, index, face, w_ref, y_ref, base, between):
    high = source.astype(BF16)
    low = (source - high.astype(F32)).astype(BF16)
    both = jnp.concatenate([high, low], axis=0)
    elements = index.shape[-1]
    rows = lax.broadcasted_iota(jnp.int32, (source.shape[-1], elements), 0).astype(F32)
    size = NQ * R
    gathered = []
    for f in range(4):
        hot = jnp.where(rows == index[f : f + 1], 1.0, 0.0).astype(BF16)
        gathered.append(dot(both, hot))
    for f, picked in enumerate(gathered):
        kind = jnp.broadcast_to(face[f : f + 1], (R, elements))
        w = w_ref[W_FAR + 4 * f * R : W_FAR + 4 * (f + 1) * R]
        for q in range(NQ):
            high_rows = picked[q * R : (q + 1) * R]
            low_rows = picked[size + q * R : size + (q + 1) * R]
            out = dot(w, jnp.concatenate([high_rows, low_rows, high_rows], axis=0).astype(BF16))
            y_ref[base + f, q] = jnp.where(
                kind < 2,
                jnp.where(kind == 0, out[:R], out[R : 2 * R]),
                jnp.where(kind == 2, out[2 * R : 3 * R], out[3 * R :]),
            )
        between(f)


def place_kernel(twice_ref, once_ref):
    row = lax.broadcasted_iota(jnp.int32, twice_ref.shape, 0)
    column = lax.broadcasted_iota(jnp.int32, twice_ref.shape, 1)
    twice_ref[...] = jnp.where((column == row) | (column == row + R), 1.0, 0.0).astype(BF16)
    once_ref[...] = jnp.where(column == row + 2 * R, 1.0, 0.0).astype(BF16)


def place_weights(w, twice_ref, once_ref):
    high = w.astype(BF16)
    low = (w - high.astype(F32)).astype(BF16)
    return (dot(high, twice_ref[...]) + dot(low, once_ref[...])).astype(BF16)


W_OWN, W_FAR, W_POINTS, W_ROWS = 0, 7 * R, 23 * R, 25 * R


def fill_stiffness(w_ref, kstiff_ref):
    w_ref[...] = jnp.zeros(w_ref.shape, F32)
    for d in range(3):
        w_ref[d * R : d * R + NB, :NB] = kstiff_ref[d]


def fill_weights(w_ref, kstiff_ref, minus_ref, plus_ref, to_ref, from_ref):
    fill_stiffness(w_ref, kstiff_ref)
    row = lax.broadcasted_iota(jnp.int32, (R, LANES), 0)
    column = lax.broadcasted_iota(jnp.int32, (R, LANES), 1)
    same = jnp.where(row == column, 1.0, 0.0).astype(BF16)
    stiff = w_ref[: 3 * R]
    high = stiff.astype(BF16)
    low = (stiff - high.astype(F32)).astype(BF16)
    turned = [
        lax.dot_general(same, part, (((1,), (1,)), ((), ())), preferred_element_type=F32) for part in (high, low)
    ]
    turned = turned[0] + turned[1]
    for d in range(3):
        w_ref[W_OWN + d * R : W_OWN + (d + 1) * R, :R] = turned[:, d * R : (d + 1) * R]
    for f in range(4):
        start = W_OWN + (3 + f) * R
        w_ref[start : start + NB, :NB] = -minus_ref[:, f, :]
        for h in range(4):
            start = W_FAR + (4 * f + h) * R
            w_ref[start : start + NB, :NB] = -plus_ref[f, :, h, :]
    w_ref[W_POINTS : W_POINTS + NB, :NB] = to_ref[...]
    w_ref[W_POINTS + R : W_POINTS + R + NB, :NB] = from_ref[...]


def send_columns(send_ref):
    slots, ghosts = send_ref.shape
    width = slots * ghosts
    row = lax.broadcasted_iota(jnp.int32, (ghosts, width), 0)
    column = lax.broadcasted_iota(jnp.int32, (ghosts, width), 1)
    repeat = jnp.where(column % ghosts == row, 1.0, 0.0).astype(BF16)
    wide = dot(send_ref[...].astype(F32).astype(BF16), repeat)
    slot = lax.broadcasted_iota(jnp.int32, (1, width), 1) // ghosts
    first = jnp.where(slot == 0, wide[0:1], wide[1:2])
    second = jnp.where(slot == 2, wide[3:4], wide[2:3])
    return jnp.where(slot < 2, first, second)


NEIGHBOUR, FACE, CLUSTER, COHESION, LIVE, YIELD = 0, 4, 8, 9, 10, 16
ROWS = 40


def setup_kernel(kstiff_ref, count_ref, twice_ref, once_ref, wk_ref, count_out, w_ref):
    fill_stiffness(w_ref, kstiff_ref)
    wk_ref[...] = place_weights(w_ref[...], twice_ref, once_ref)
    count_out[...] = jnp.broadcast_to(count_ref[...], count_out.shape).astype(F32)


def pick_kernel(b_ref, lists_ref, near_ref, far_ref, send_ref):
    send = send_columns(lists_ref.at[0])
    send_ref[...] = send
    pick_columns(b_ref, send, near_ref, far_ref)


def route_kernel(near_ref, far_ref, even_ref, flag_ref):
    chip = (lax.axis_index("dom") // 2) % 2
    half = near_ref.shape[1] // 2
    side = lax.broadcasted_iota(jnp.int32, near_ref.shape, 1) // half
    even_ref[...] = jnp.where(side == chip, near_ref[...], far_ref[...])
    lane = lax.broadcasted_iota(jnp.int32, flag_ref.shape, 1) // half
    flag_ref[...] = jnp.where(lane == chip, 1.0, 0.0)


def predict_kernel(dof_ref, star_ref, wk_ref, b_ref, m_ref):
    widen(star_ref, m_ref)
    wk = wk_ref[...]

    def half(lanes):
        x = [padded(dof_ref, p, lanes) for p in range(NQ)]
        yield from taylor_steps(x, wk, m_ref, lanes, 0.5, 1.0 / 6.0, b_ref)

    in_turns(half(pl.ds(0, LANES)), half(pl.ds(LANES, LANES)), [[1] * NQ, [1] * 3 * NQ] * 2)


def fill_table(table_ref, index_ref, face_ref, cluster_ref, cohesion_ref, damage_ref, count_ref, yield_ref):
    table_ref[...] = jnp.zeros(table_ref.shape, F32)
    table_ref[NEIGHBOUR : NEIGHBOUR + 4, :] = index_ref[...].astype(F32)
    table_ref[FACE : FACE + 4, :] = face_ref[...].astype(F32)
    table_ref[CLUSTER : CLUSTER + 1, :] = cluster_ref[...].astype(F32)
    table_ref[COHESION : COHESION + 1, :] = cohesion_ref[...]
    slot = lax.broadcasted_iota(jnp.int32, damage_ref.shape, 1).astype(F32)
    table_ref[LIVE : LIVE + 1, :] = jnp.where(slot < count_ref[...], damage_ref[...].astype(F32), -1.0)
    table_ref[YIELD : YIELD + NB, :] = yield_ref[...].astype(F32)


def local_part(b_ref, w_ref, table_ref, ms_ref, ml_ref, mn_ref, out_ref, y_ref, start):
    elements = b_ref.shape[-1]
    basis_products(w_ref[W_OWN:W_FAR], b_ref, y_ref, 7)
    source = b_ref[...].reshape(NQ * R, elements)
    halves = [pl.ds(at, LANES) for at in range(0, elements, LANES)]
    acc = [[start(p, lanes) for p in range(NQ)] for lanes in halves]

    def add(k, m_ref, row):
        for i, lanes in enumerate(halves):
            acc[i] = star_add(acc[i], y_ref, k, m_ref, row, lanes)

    def between(f):
        for k in ((0, 1), (2, 3), (4, 5), (6,))[f]:
            add(k, ms_ref if k < 3 else ml_ref, k if k < 3 else k - 3)

    far_sides(source, table_ref[NEIGHBOUR : NEIGHBOUR + 4], table_ref[FACE : FACE + 4], w_ref, y_ref, 7, between)
    for f in range(4):
        add(7 + f, mn_ref, f)
    for i, lanes in enumerate(halves):
        for p in range(NQ):
            out_ref[p, :, lanes] = acc[i][p]


def padded(ref, p, lanes):
    return jnp.concatenate([ref[p, :, lanes], jnp.zeros((R - NB, LANES), F32)], axis=0)


def local_kernel(
    dof_ref, b_ref, ms_ref, local_ref, neigh_ref,
    kstiff_ref, minus_ref, plus_ref, to_ref, from_ref, twice_ref, once_ref,
    index_ref, face_ref, cluster_ref, cohesion_ref, damage_ref, count_ref, yield_ref,
    out_ref, ml_ref, mn_ref, table_ref, weights_ref,
    w_ref, y_ref,
):
    fill_weights(w_ref, kstiff_ref, minus_ref, plus_ref, to_ref, from_ref)
    weights_ref[...] = place_weights(w_ref[...], twice_ref, once_ref)
    fill_table(table_ref, index_ref, face_ref, cluster_ref, cohesion_ref, damage_ref, count_ref, yield_ref)
    widen(local_ref, ml_ref)
    widen(neigh_ref, mn_ref)
    local_part(
        b_ref, weights_ref, table_ref, ms_ref, ml_ref, mn_ref, out_ref, y_ref, lambda p, lanes: padded(dof_ref, p, lanes)
    )


def again_kernel(
    base_ref, b_ref, w_ref, table_ref, ms_ref, ml_ref, mn_ref, out_ref, mask_ref, y_ref
):
    local_part(b_ref, w_ref, table_ref, ms_ref, ml_ref, mn_ref, out_ref, y_ref, lambda p, lanes: base_ref[p, :, lanes])
    elements = out_ref.shape[-1]
    rows = lax.broadcasted_iota(jnp.int32, (elements, elements), 0).astype(F32)
    listed = lax.dot_general(
        jnp.ones((8, elements), BF16),
        jnp.where(rows == table_ref[LIVE : LIVE + 1], 1.0, 0.0).astype(BF16),
        (((1,), (1,)), ((), ())),
        preferred_element_type=F32,
    )[0:1]
    mask_ref[...] = jnp.where(listed > 0.5, table_ref[YIELD : YIELD + R], 0.0)


def ghost_source(near_ref, even_ref, odd_ref, cross_ref):
    me, total = lax.axis_index("dom"), lax.axis_size("dom")
    core = me % 2
    chip = (me // 2) % 2 == 0
    near, even, odd = near_ref[...], even_ref[...], odd_ref[...]
    up = jnp.where(chip, even, odd)
    down = jnp.where(chip, odd, even)
    half = near.shape[1] // 2
    side = lax.broadcasted_iota(jnp.int32, near.shape, 1) // half
    across = jnp.where((me // 2) % 2 == core, odd, cross_ref[...])
    one = jnp.where(side == core, across, near)
    two = jnp.where(side == 0, up, down)
    one = jnp.where(jnp.where(side == 0, me - 1, total - 2 - me) >= 0, one, 0.0)
    two = jnp.where(jnp.where(side == 0, total - 3 - me, me - 2) >= 0, two, 0.0)
    pad = jnp.zeros((R - NB, 2 * near.shape[1]), F32)
    both = jnp.concatenate([one, two], axis=1)
    return jnp.concatenate([piece for q in range(NQ) for piece in (both[q * NB : (q + 1) * NB], pad)], axis=0)


def gather_all(both, index):
    rows = lax.broadcasted_iota(jnp.int32, (both.shape[1], index.shape[1]), 0).astype(F32)
    gathered = []
    for f in range(4):
        hot = jnp.where(rows == index[f : f + 1], 1.0, 0.0).astype(BF16)
        gathered.append(dot(both, hot))
    return gathered


def ghost_index(table_ref, ghosts):
    index = table_ref[NEIGHBOUR : NEIGHBOUR + 4] - table_ref.shape[-1]
    last = jnp.where(index >= 3 * ghosts, index - ghosts, index + ghosts)
    return jnp.where(index >= 2 * ghosts, last, index)


def split_rows(source):
    high = source.astype(BF16)
    return jnp.concatenate([high, (source - high.astype(F32)).astype(BF16)], axis=0)


def second_kernel(
    v_ref, dof_ref, near_ref, even_ref, odd_ref, cross_ref, wk_ref, send_ref, w_ref, table_ref, ms_ref, mn_ref,
    state_ref, b_ref, near_out, far_out,
):
    both = split_rows(ghost_source(near_ref, even_ref, odd_ref, cross_ref))
    index = ghost_index(table_ref, near_ref.shape[-1] // 2)
    both = gather_all(both, index)
    wk = wk_ref[...]

    def half(at):
        lanes = pl.ds(at, LANES)
        ys = {}
        yield from far_steps(ys, [one[:, at : at + LANES] for one in both], index[:, at : at + LANES], table_ref[FACE : FACE + 4, lanes], w_ref)
        acc = [v_ref[p, :, lanes] for p in range(NQ)]
        yield from star_steps(acc, ys, mn_ref, lanes)
        fine = table_ref[CLUSTER : CLUSTER + 1, lanes] < 0.5
        x = []
        for p in range(NQ):
            state_ref[p, :, lanes] = acc[p]
            x.append(jnp.where(fine, acc[p], padded(dof_ref, p, lanes)))
        w1, w2 = jnp.where(fine, 0.5, 1.5), jnp.where(fine, 1.0 / 6.0, 7.0 / 6.0)
        yield from taylor_steps(x, wk, ms_ref, lanes, w1, w2, b_ref)

    in_turns(half(0), half(LANES), [FAR, [1] * 4 * NQ] + [[1] * NQ, [1] * 3 * NQ] * 2)
    pick_columns(b_ref, send_ref[...], near_out, far_out)


def last_kernel(
    v_ref, near_ref, even_ref, odd_ref, cross_ref, w_ref, table_ref, mn_ref, mask_ref,
    result_ref,
    out_ref, sems,
):
    both = split_rows(ghost_source(near_ref, even_ref, odd_ref, cross_ref))
    index = ghost_index(table_ref, near_ref.shape[-1] // 2)
    both = gather_all(both, index)
    writes = []

    def send_out(quantities, lanes):
        write = pltpu.make_async_copy(
            out_ref.at[quantities, :, lanes], result_ref.at[quantities, :, lanes], sems.at[len(writes)]
        )
        write.start()
        writes.append(write)

    def half(at):
        lanes = pl.ds(at, LANES)
        ys = {}
        yield from far_steps(ys, [one[:, at : at + LANES] for one in both], index[:, at : at + LANES], table_ref[FACE : FACE + 4, lanes], w_ref)
        state = [v_ref[p, :, lanes] for p in range(NQ)]
        yield from star_steps(state, ys, mn_ref, lanes)
        for q in range(6, NQ):
            out_ref[q, :, lanes] = state[q][:NB]
        send_out(pl.ds(6, 3), lanes)
        points = []
        for q in range(6):
            points.append(dot(w_ref[W_POINTS : W_POINTS + R], stack_values(state[q])))
            yield
        pressure = (points[0] + points[1] + points[2]) / 3.0
        normal = [points[q] - pressure for q in range(3)]
        normal_sum = normal[0] * normal[0] + normal[1] * normal[1] + normal[2] * normal[2]
        shear_sum = points[3] * points[3] + points[4] * points[4] + points[5] * points[5]
        tau = jnp.sqrt(0.5 * normal_sum + shear_sum)
        strength = table_ref[COHESION : COHESION + 1, lanes]
        limit = jnp.maximum(strength - FRICTION * pressure, 0.5 * strength)
        yield
        rate = RELAXATION * (limit / jnp.maximum(tau, limit) - 1.0)
        rate = jnp.where(mask_ref[:, lanes] > 0.5, rate, 0.0)
        yield
        deviation = normal + points[3:]
        for q in range(6):
            change = dot(w_ref[W_POINTS + R : W_ROWS], stack_values(rate * deviation[q]))
            out_ref[q, :, lanes] = (state[q] + change)[:NB]
            yield
        send_out(pl.ds(0, 6), lanes)

    in_turns(half(0), half(LANES), [FAR, [1] * 4 * NQ, [1] * 14])
    for write in writes:
        write.wait()


def spec(shape, dtype=F32):
    return jax.ShapeDtypeStruct(shape, dtype)


VMEM = pl.BlockSpec(memory_space=pltpu.VMEM)
HBM = pl.BlockSpec(memory_space=pltpu.HBM)


def call(kernel, inputs, outputs, scratch, cost=0, out_space=VMEM):
    return pl.pallas_call(
        kernel,
        out_shape=outputs,
        in_specs=[VMEM] * len(inputs),
        out_specs=jax.tree.map(lambda _: out_space, outputs),
        scratch_shapes=[pltpu.VMEM(*one) if isinstance(one, tuple) else one for one in scratch],
        compiler_params=pltpu.CompilerParams(vmem_limit_bytes=40 * 1024 * 1024),
        cost_estimate=pl.CostEstimate(flops=cost, bytes_accessed=1 << 20, transcendentals=0),
    )(*inputs)


def core_swap(total):
    return [(i, i ^ 1) for i in range(total)]


def even_chip_swap(total):
    return [(i, i ^ 2) for i in range(total)]


def odd_chip_swap(total):
    route = [(i, i) for i in (0, 1, total - 2, total - 1)]
    for i in range(2, total - 2, 4):
        for k in (i, i + 1):
            route += [(k, k + 2), (k + 2, k)]
    return route


def exchange(near, far, buffer, total):
    got = lax.ppermute(near, "dom", core_swap(total))
    to_even, flag = call(route_kernel, [near, far], (spec(near.shape), spec((8, near.shape[1]))), [])
    even = lax.ppermute(to_even, "dom", even_chip_swap(total))
    to_odd = jnp.where(flag[:1] > 0.5, far, got)
    odd = lax.ppermute(to_odd, "dom", odd_chip_swap(total))
    buffer, even, to_odd = lax.optimization_barrier((buffer, even, to_odd))
    cross = lax.ppermute(even, "dom", core_swap(total))
    return got, even, odd, cross, buffer


def per_device(
    dof_values,
    star_mats,
    flux_local,
    flux_neigh,
    kstiff,
    flux_minus,
    flux_plus,
    neighbour,
    neigh_face,
    cluster,
    send_list,
    damage_list,
    damage_count,
    yield_mask,
    cohesion,
    to_points,
    from_points,
):
    elements = dof_values.shape[-1]
    total = lax.axis_size("dom")
    ghosts = send_list.shape[-1]

    field = spec((NQ, R, elements))
    block = spec((NQ * NB, 2 * ghosts))

    def y_s(blocks):
        return ((blocks, NQ, R, elements), F32)

    def m_o(blocks):
        return spec((NQ * NQ, blocks, elements))

    star = jnp.transpose(star_mats, (1, 2, 0, 3))
    own = jnp.transpose(flux_local, (1, 2, 0, 3))
    other = jnp.transpose(flux_neigh, (1, 2, 0, 3))
    minus = jnp.transpose(flux_minus, (1, 0, 2))
    plus = jnp.transpose(flux_plus, (0, 2, 1, 3))

    place = spec((LANES, K3), BF16)
    twice, once = call(place_kernel, [], (place, place), [], cost=4_000_000_000)
    wk, count = call(
        setup_kernel,
        [kstiff, damage_count[None], twice, once],
        (spec((3 * R, K3), BF16), spec((1, elements))),
        [((3 * R, LANES), F32)],
    )
    buffer_one, ms = call(predict_kernel, [dof_values, star, wk], (field, m_o(3)), [])
    near, far, send = call(pick_kernel, [buffer_one, send_list], (block, block, spec((1, 4 * ghosts))), [])
    near, even, odd, cross, buffer_one = exchange(near, far, buffer_one, total)
    started, ml, mn, table, weights = call(
        local_kernel,
        [
            dof_values, buffer_one, ms, own, other,
            kstiff, minus, plus, to_points, from_points, twice, once,
            neighbour, neigh_face, cluster[None], cohesion[None], damage_list, count, yield_mask,
        ],
        (field, m_o(4), m_o(4), spec((ROWS, elements)), spec((W_ROWS, K3), BF16)),
        [((W_ROWS, LANES), F32), y_s(11)],
        cost=1_000_000_000,
    )
    updated, buffer_two, near, far = call(
        second_kernel,
        [started, dof_values, near, even, odd, cross, wk, send, weights, table, ms, mn],
        (field, field, block, block),
        [],
    )
    near, even, odd, cross, buffer_two = exchange(near, far, buffer_two, total)
    started, mask = call(
        again_kernel,
        [updated, buffer_two, weights, table, ms, ml, mn],
        (field, spec((R, elements))),
        [y_s(11)],
        cost=1_000_000_000,
    )
    return call(
        last_kernel,
        [started, near, even, odd, cross, weights, table, mn, mask],
        spec(dof_values.shape),
        [(dof_values.shape, F32), pltpu.SemaphoreType.DMA((4,))],
        out_space=HBM,
    )


def solution(mesh):
    return jax.shard_map(
        per_device,
        mesh=mesh,
        in_specs=(
            P(None, None, "dom"),
            P(None, None, None, "dom"),
            P(None, None, None, "dom"),
            P(None, None, None, "dom"),
            P(),
            P(),
            P(),
            P(None, "dom"),
            P(None, "dom"),
            P("dom"),
            P("dom", None, None),
            P("dom", None),
            P("dom"),
            P(None, "dom"),
            P("dom"),
            P(),
            P(),
        ),
        out_specs=P(None, None, "dom"),
        check_vma=False,
    )
```
